256 devices in a mesh: lat: 16 (over z, y_hi), lon: 16 (over y_lo, x, core).
Axes of the slice: x: 4, y: 4 (y_hi: 2, y_lo: 2; y = y_hi * 2 + y_lo), z: 8, core: 2. Of those that a mesh axis runs over, the one named last changes fastest.
Arguments:
- saved_state: bfloat16 [256, 1024, 512], P('lat', 'lon'), may hold values from -6 to 6
- cotangent: bfloat16 [256, 1024, 512], P('lat', 'lon'), may hold values from -6 to 6
- row_mask: int32 [256], P('lat'), may hold values from 0 to 1, as said below
- shifts: int32 [2], replicated, may hold values from 1 to 7, as said below
- norm_gain: float32 [512], replicated, may hold values from 0.5 to 1.5
- w_qkv: bfloat16 [512, 1536], replicated, may hold values from -0.25 to 0.25
- w_out: bfloat16 [512, 512], replicated, may hold values from -0.25 to 0.25
- bias_table: float32 [16, 225], replicated, may hold values from -4 to 260
Outputs:
- state_grad: bfloat16 [256, 1024, 512], P('lat', 'lon')
- qkv_grad: float32 [512, 1536], replicated
- out_grad: float32 [512, 512], replicated
- gain_grad: float32 [512], replicated
- bias_grad: float32 [16, 225], replicated
The draws below stay inside these ranges and needn't reach their ends.
Inputs may be any that keep to these rules, and one draw needn't show every extreme that they name: row_mask is 1 on all rows below some L and 0 from L on, with 224 <= L <= 249. `shifts`: one of the two offsets is 7.
All inputs are finite; a program needn't handle non-finite values.
Results may differ from the reference program's by a relative error of at most 0.013.
Values may be sent and summed in bfloat16 or wider, within the bound.
No kernel may reach another device: no remote copies, remote signals or barrier semaphores. Data moves between devices by JAX's collectives and lax.ppermute only.
A program may use at most 128 MiB of HBM per device.

```python
import math
import jax
import jax.numpy as jnp
from jax import lax

CH = 512
HEADS = 16
WIN = 8
BIAS = 225
CLAT = 16
NLAT = 256
NLON = 1024


def draw_row_mask(key, part):
    key = jax.random.fold_in(key, 7)
    boundary = jax.random.randint(key, (), NLAT - 2 * CLAT, NLAT - 6)
    return (jnp.arange(NLAT) < boundary).astype(jnp.int32)


def draw_shifts(key, part):
    key = jax.random.fold_in(key, 5)
    key_first, key_second = jax.random.split(key)
    first_shift = jax.random.randint(key_first, (), 1, WIN)
    flip_order = jax.random.randint(key_second, (), 0, 2)
    largest = jnp.full((), WIN - 1, jnp.int32)
    return jnp.where(flip_order == 1, jnp.stack([first_shift, largest]), jnp.stack([largest, first_shift])).astype(jnp.int32)


def draw_bias_table(key, part):
    key = jax.random.fold_in(key, 11)
    key_base = jax.random.fold_in(key, 0)
    return jnp.clip(jax.random.normal(key_base, (HEADS, BIAS), jnp.float32), -4.0, 4.0)


def level_of(key, dims, cuts, smallest, high):
    loudness = 1.0
    for position, parts in cuts:
        draws = jax.random.uniform(jax.random.fold_in(jax.random.fold_in(key, 6), position), (parts,), jnp.float32, smallest / len(cuts), high / len(cuts))
        loudness = loudness * jnp.repeat(jnp.exp(draws), dims[position] // parts).reshape((-1,) + (1,) * (len(dims) - 1 - position))
    return loudness


def centred(key, extent, scale, reach, shards=(), held_as=jnp.bfloat16):
    array = scale * jax.random.normal(key, extent, jnp.float32)
    if shards:
        array = array * level_of(key, extent, shards, -0.22, 0.18)
    return jnp.clip(array, -reach, reach).astype(held_as)


def setup_inputs(seed: int = 0) -> dict:
    key_of = jax.random.split(jax.random.key(seed), 9)
    return {
        "saved_state": centred(key_of[0], (NLAT, NLON, CH), 1.0, 6.0, ((0, 16), (1, 16))),
        "cotangent": centred(key_of[1], (NLAT, NLON, CH), 1.0, 6.0, ((0, 16), (1, 16))),
        "row_mask": draw_row_mask(jax.random.fold_in(key_of[8], 71), 0),
        "shifts": draw_shifts(jax.random.fold_in(key_of[8], 71), 0),
        "norm_gain": jnp.clip(1.0 + 0.1 * jax.random.normal(key_of[4], (CH,), jnp.float32), 0.5, 1.5),
        "w_qkv": centred(key_of[5], (CH, 3 * CH), CH ** -0.5, 0.25),
        "w_out": centred(key_of[6], (CH, CH), CH ** -0.5, 0.25),
        "bias_table": draw_bias_table(jax.random.fold_in(key_of[8], 71), 0),
    }


EPSILON = 1e-05

def offsets_table(window):
    cell_count = window * window
    places = jnp.arange(cell_count)
    row_of = places // window
    col_of = places % window
    row_gap = row_of[:, None] - row_of[None, :] + window - 1
    col_gap = col_of[:, None] - col_of[None, :] + window - 1
    flat_gap = (row_gap * (2 * window - 1) + col_gap).reshape(-1)
    entries = jnp.arange((2 * window - 1) ** 2)
    return (flat_gap[:, None] == entries[None, :]).astype(jnp.float32)

def product(pattern, first_op, second_op):
    return jnp.einsum(pattern, first_op.astype(jnp.float32), second_op.astype(jnp.float32))

def window_backward(tokens, cotangent, live_keys, norm_gain, w_qkv, w_out, bias_table):
    n_win, n_cell, n_chan = tokens.shape
    n_head = bias_table.shape[0]
    head_dim = n_chan // n_head
    window = (math.isqrt(bias_table.shape[1]) + 1) // 2
    onehot = offsets_table(window)
    as_float = tokens.astype(jnp.float32)
    centre_mean = lax.optimization_barrier(jnp.mean(as_float, -1, keepdims=True))
    centered = as_float - centre_mean
    inv_std = lax.rsqrt(lax.optimization_barrier(jnp.mean(centered * centered, -1, keepdims=True)) + EPSILON)
    x_hat = centered * inv_std
    normed = (x_hat * norm_gain).astype(jnp.bfloat16)
    projected = product('bnc,cd->bnd', normed, w_qkv)
    qk_scale = head_dim ** (-0.5)
    query_heads = (projected[..., :n_chan] * qk_scale).astype(jnp.bfloat16).reshape(n_win, n_cell, n_head, head_dim)
    key_heads = projected[..., n_chan:2 * n_chan].astype(jnp.bfloat16).reshape(n_win, n_cell, n_head, head_dim)
    value_heads = projected[..., 2 * n_chan:].astype(jnp.bfloat16).reshape(n_win, n_cell, n_head, head_dim)
    bias_full = jnp.dot(bias_table, onehot.T, precision=lax.Precision.HIGHEST).reshape(n_head, n_cell, n_cell)
    scores = product('bqhd,bkhd->bhqk', query_heads, key_heads) + bias_full[None]
    key_live = live_keys[:, None, None, :] > 0.5
    scores = jnp.where(key_live, scores, -1e+30)
    row_max = lax.optimization_barrier(jnp.max(scores, -1, keepdims=True))
    powers = jnp.exp(scores - row_max)
    attention = powers / lax.optimization_barrier(jnp.sum(powers, -1, keepdims=True))
    attn_half = attention.astype(jnp.bfloat16)
    mixed = product('bhqk,bkhd->bqhd', attn_half, value_heads).reshape(n_win, n_cell, n_chan).astype(jnp.bfloat16)
    grad_out = (cotangent.astype(jnp.float32) * live_keys[..., None]).astype(jnp.bfloat16)
    out_sum = product('bnc,bne->ce', mixed, grad_out)
    grad_mixed = product('bne,ce->bnc', grad_out, w_out).astype(jnp.bfloat16).reshape(n_win, n_cell, n_head, head_dim)
    grad_attn = product('bqhd,bkhd->bhqk', grad_mixed, value_heads)
    grad_value = product('bhqk,bqhd->bkhd', attn_half, grad_mixed)
    grad_scores = attention * (grad_attn - lax.optimization_barrier(jnp.sum(attention * grad_attn, -1, keepdims=True)))
    bias_sum = jnp.dot(lax.optimization_barrier(jnp.sum(grad_scores, 0)).reshape(n_head, n_cell * n_cell), onehot, precision=lax.Precision.HIGHEST)
    scores_half = grad_scores.astype(jnp.bfloat16)
    grad_query = product('bhqk,bkhd->bqhd', scores_half, key_heads) * qk_scale
    grad_key = product('bhqk,bqhd->bkhd', scores_half, query_heads)
    grad_proj = jnp.concatenate([grad_query.reshape(n_win, n_cell, n_chan), grad_key.reshape(n_win, n_cell, n_chan), grad_value.reshape(n_win, n_cell, n_chan)], -1).astype(jnp.bfloat16)
    qkv_sum = product('bnc,bnd->cd', normed, grad_proj)
    grad_normed = product('bnd,cd->bnc', grad_proj, w_qkv)
    gain_sum = lax.optimization_barrier(jnp.sum(grad_normed * x_hat, axis=(0, 1)))
    grad_hat = grad_normed * norm_gain
    grad_cells = inv_std * (grad_hat - lax.optimization_barrier(jnp.mean(grad_hat, -1, keepdims=True)) - x_hat * lax.optimization_barrier(jnp.mean(grad_hat * x_hat, -1, keepdims=True)))
    return (grad_cells, qkv_sum, out_sum, gain_sum, bias_sum)

def reference(saved_state, cotangent, row_mask, shifts, norm_gain, w_qkv, w_out, bias_table):
    lat_cells, lon_cells, n_chan = saved_state.shape
    window = (math.isqrt(bias_table.shape[1]) + 1) // 2
    shift_lat = shifts[0]
    shift_lon = shifts[1]
    zero_index = shift_lat * 0

    def place(field):
        padded = jnp.concatenate([jnp.zeros((window, lon_cells, n_chan), field.dtype), field], 0)
        moved = lax.dynamic_slice_in_dim(padded, shift_lat, lat_cells, 0)
        return jnp.roll(moved, window - shift_lon, axis=1)
    padded_mask = jnp.concatenate([jnp.zeros((window,), jnp.int32), row_mask.astype(jnp.int32)])
    live_rows = lax.dynamic_slice_in_dim(padded_mask, shift_lat, lat_cells).astype(jnp.float32)
    win_rows = lat_cells // window
    win_cols = lon_cells // window

    def to_windows(field):
        shaped = field.reshape(win_rows, window, win_cols, window, n_chan)
        return shaped.transpose(0, 2, 1, 3, 4).reshape(win_rows, win_cols, window * window, n_chan)
    state_blocks = to_windows(place(saved_state))
    cot_blocks = to_windows(place(cotangent))
    live_blocks = jnp.broadcast_to(live_rows.reshape(win_rows, 1, window, 1), (win_rows, win_cols, window, window)).reshape(win_rows, win_cols, window * window)

    def window_row(running, inputs_row):
        tok_row, cot_row, live_row = inputs_row
        grad_cells, qkv_sum, out_sum, gain_sum, bias_sum = window_backward(tok_row, cot_row, live_row, norm_gain, w_qkv, w_out, bias_table)
        return ((running[0] + qkv_sum, running[1] + out_sum, running[2] + gain_sum, running[3] + bias_sum), grad_cells)
    start_sums = (jnp.zeros(w_qkv.shape, jnp.float32), jnp.zeros(w_out.shape, jnp.float32), jnp.zeros(norm_gain.shape, jnp.float32), jnp.zeros(bias_table.shape, jnp.float32))
    totals, grad_blocks = lax.scan(window_row, start_sums, (state_blocks, cot_blocks, live_blocks))
    grad_grid = grad_blocks.reshape(win_rows, win_cols, window, window, n_chan).transpose(0, 2, 1, 3, 4).reshape(lat_cells, lon_cells, n_chan)
    rolled = jnp.roll(grad_grid, shift_lon - window, axis=1)
    holder = jnp.zeros((lat_cells + window, lon_cells, n_chan), jnp.float32)
    holder = lax.dynamic_update_slice(holder, rolled, (shift_lat, zero_index, zero_index))
    grad_input = holder[window:]
    state_grad = (cotangent.astype(jnp.float32) + grad_input).astype(jnp.bfloat16)
    norm_factor = 1.0 / math.sqrt(lat_cells * lon_cells)
    return (state_grad, totals[0] * norm_factor, totals[1] * norm_factor, totals[2] * norm_factor, totals[3] * norm_factor)
```

```python
import functools
import math

import jax
import jax.numpy as jnp
from jax import lax
from jax.experimental import pallas as pl
from jax.experimental.pallas import tpu as pltpu
from jax.sharding import PartitionSpec as P

EPSILON = 1e-05


def shifted(value, axis, steps):
    count = lax.axis_size(axis)
    pairs = [(source, (source + steps) % count) for source in range(count)]
    return lax.ppermute(value, axis, pairs)


def from_behind(array, axis, by):
    count = lax.axis_size(axis)
    pairs = [(i, i + by) for i in range(count) if 0 <= i + by < count]
    return lax.ppermute(array, axis, pairs)


def offsets_table(window):
    cell_count = window * window
    places = jnp.arange(cell_count)
    row_of = places // window
    col_of = places % window
    row_gap = row_of[None, :] - row_of[:, None] + window - 1
    col_gap = col_of[None, :] - col_of[:, None] + window - 1
    flat_gap = (row_gap * (2 * window - 1) + col_gap).reshape(-1)
    entries = jnp.arange((2 * window - 1) ** 2)
    return (flat_gap[:, None] == entries[None, :]).astype(jnp.float32)


NT = (((1,), (1,)), ((), ()))
NN = (((1,), (0,)), ((), ()))


def dot(a, b, dims=NN):
    return lax.dot_general(a, b, dims, preferred_element_type=jnp.float32)


def forward_chunk(n_chan, x_ref, go_ref, gain_ref, wt_ref, w_ref, wo_ref, nrm, proj_t, kv, gm_t, scale, base, size):
    rows = pl.ds(base, size)
    x = x_ref[rows].astype(jnp.float32)
    cen = x - jnp.mean(x, -1, keepdims=True)
    inv = lax.rsqrt(jnp.mean(cen * cen, -1, keepdims=True) + EPSILON)
    normed = (cen * inv * gain_ref[...]).astype(jnp.bfloat16)
    nrm[rows] = normed
    proj_t[:n_chan, rows] = (dot(wt_ref[:n_chan], normed, NT) * scale).astype(jnp.bfloat16)
    proj_t[n_chan:, rows] = dot(wt_ref[n_chan:], normed, NT).astype(jnp.bfloat16)
    kv[rows] = dot(normed, w_ref[:, n_chan:]).astype(jnp.bfloat16)
    gm_t[:, rows] = dot(wo_ref[...], go_ref[rows], NT).astype(jnp.bfloat16)


def block_diag(block, step):
    blank = jnp.zeros((step, block.shape[1]), block.dtype)
    count = block.shape[0] // step
    columns = []
    for h in range(count):
        parts = [blank] * count
        parts[h] = block[h * step : (h + 1) * step]
        columns.append(jnp.concatenate(parts, 0))
    return jnp.concatenate(columns, 1)


def attention_unit(n_chan, dim, bias_ref, mask_ref, proj_t, kv, gm_t, mix_t, gp_t, bsum_ref, scale, pair, group, pairs_per_row):
    lanes = pl.ds(pl.multiple_of(pair * 128, 128), 128)
    c0 = pl.multiple_of(group * 128, 128)
    q_t = proj_t[pl.ds(c0, 128), lanes]
    k_t = proj_t[pl.ds(n_chan + c0, 128), lanes]
    v_t = proj_t[pl.ds(2 * n_chan + c0, 128), lanes]
    g_t = gm_t[pl.ds(c0, 128), lanes]
    k_tok = kv[lanes, pl.ds(c0, 128)]
    v_tok = kv[lanes, pl.ds(n_chan + c0, 128)]
    scores = dot(k_tok, block_diag(q_t, dim))
    grads = dot(v_tok, block_diag(g_t, dim))
    first = lax.broadcasted_iota(jnp.int32, (64, 128), 1) < 64
    mask = mask_ref[pair // pairs_per_row]
    heads = 128 // dim
    mixed, dq, dk, dv = [], [], [], []
    for h in range(heads):
        cut = slice(h * 128, (h + 1) * 128)
        rows = slice(h * dim, (h + 1) * dim)
        head = group * heads + h
        s = jnp.where(first, scores[:64, cut], scores[64:, cut]) + bias_ref[head]
        s = s + mask
        e = jnp.exp(s - jnp.max(s, 0, keepdims=True))
        a = e * (1.0 / jnp.sum(e, 0, keepdims=True))
        d = jnp.where(first, grads[:64, cut], grads[64:, cut])
        ad = a * d
        ds = ad - a * jnp.sum(ad, 0, keepdims=True)
        bsum_ref[head] += ds
        zero = jnp.zeros_like(a)
        a2 = jnp.concatenate([jnp.where(first, a, zero), jnp.where(first, zero, a)], 0).astype(jnp.bfloat16)
        ds2 = jnp.concatenate([jnp.where(first, ds, zero), jnp.where(first, zero, ds)], 0).astype(jnp.bfloat16)
        mixed.append(dot(v_t[rows], a2))
        dv.append(dot(g_t[rows], a2, NT))
        dq.append(dot(k_t[rows], ds2) * scale)
        dk.append(dot(q_t[rows], ds2, NT))
    mix_t[pl.ds(c0, 128), lanes] = jnp.concatenate(mixed, 0).astype(jnp.bfloat16)
    gp_t[pl.ds(c0, 128), lanes] = jnp.concatenate(dq, 0).astype(jnp.bfloat16)
    gp_t[pl.ds(n_chan + c0, 128), lanes] = jnp.concatenate(dk, 0).astype(jnp.bfloat16)
    gp_t[pl.ds(2 * n_chan + c0, 128), lanes] = jnp.concatenate(dv, 0).astype(jnp.bfloat16)


def weights_kernel(n_head, pairs_per_row, x_ref, go_ref, bias_ref, mask_ref, gain_ref, wt_ref, w_ref, wo_ref,
                   sums_ref, bsum_ref, gp_t, nrm, proj_t, kv, gm_t, mix_t):
    n_tok, n_chan = x_ref.shape
    dim = n_chan // n_head
    scale = dim ** (-0.5)
    for base in range(0, n_tok, 256):
        forward_chunk(n_chan, x_ref, go_ref, gain_ref, wt_ref, w_ref, wo_ref, nrm, proj_t, kv, gm_t, scale, base, 256)
    bsum_ref[...] = jnp.zeros_like(bsum_ref)
    groups = n_chan // 128

    @pl.loop(0, n_tok // 128 * groups)
    def _(unit):
        attention_unit(n_chan, dim, bias_ref, mask_ref, proj_t, kv, gm_t, mix_t, gp_t, bsum_ref, scale,
                       unit // groups, unit % groups, pairs_per_row)

    for base in range(0, 3 * n_chan, 256):
        sums_ref[base : base + 256] = dot(gp_t[base : base + 256], nrm[...])
    for base in range(0, n_chan, 256):
        sums_ref[3 * n_chan + base : 3 * n_chan + base + 256] = dot(mix_t[base : base + 256], go_ref[...])


def cells_kernel(x_ref, gp_t, gain_ref, w_ref, cells_ref, gsum_ref):
    n_tok, n_chan = x_ref.shape
    total = jnp.zeros((1, n_chan), jnp.float32)
    for base in range(0, n_tok, 256):
        rows = slice(base, base + 256)
        x = x_ref[rows].astype(jnp.float32)
        cen = x - jnp.mean(x, -1, keepdims=True)
        inv = lax.rsqrt(jnp.mean(cen * cen, -1, keepdims=True) + EPSILON)
        x_hat = cen * inv
        grad = dot(w_ref[...], gp_t[:, rows]).T
        total = total + jnp.sum(grad * x_hat, 0, keepdims=True)
        g = grad * gain_ref[...]
        cells_ref[rows] = inv * (g - jnp.mean(g, -1, keepdims=True) - x_hat * jnp.mean(g * x_hat, -1, keepdims=True))
    gsum_ref[...] = total


def window_backward(tokens, grad_out, key_mask, norm_gain, w_qkv, w_out, bias_table):
    n_tok, n_chan = tokens.shape
    n_head = bias_table.shape[0]
    window = (math.isqrt(bias_table.shape[1]) + 1) // 2
    n_cell = window * window
    onehot = offsets_table(window)
    bias = jnp.dot(bias_table, onehot.T, precision=lax.Precision.HIGHEST).reshape(n_head, n_cell, n_cell)
    bias = jnp.concatenate([bias, bias], -1)
    gain = norm_gain.reshape(1, n_chan)
    pairs_per_row = n_tok // 128 // key_mask.shape[0]
    sums, bias_sum, grad_proj = pl.pallas_call(
        functools.partial(weights_kernel, n_head, pairs_per_row),
        out_shape=(
            jax.ShapeDtypeStruct((4 * n_chan, n_chan), jnp.float32),
            jax.ShapeDtypeStruct((n_head, n_cell, 2 * n_cell), jnp.float32),
            jax.ShapeDtypeStruct((3 * n_chan, n_tok), jnp.bfloat16),
        ),
        scratch_shapes=[
            pltpu.VMEM((n_tok, n_chan), jnp.bfloat16),
            pltpu.VMEM((3 * n_chan, n_tok), jnp.bfloat16),
            pltpu.VMEM((n_tok, 2 * n_chan), jnp.bfloat16),
            pltpu.VMEM((n_chan, n_tok), jnp.bfloat16),
            pltpu.VMEM((n_chan, n_tok), jnp.bfloat16),
        ],
        compiler_params=pltpu.CompilerParams(vmem_limit_bytes=48 * 1024 * 1024),
        cost_estimate=pl.CostEstimate(flops=8 * 10**9, bytes_accessed=16 * 2**20, transcendentals=2**20),
        name="weights",
    )(tokens, grad_out, bias, key_mask, gain, w_qkv.T, w_qkv, w_out)
    grad_cells, gain_sum = pl.pallas_call(
        cells_kernel,
        out_shape=(
            jax.ShapeDtypeStruct((n_tok, n_chan), jnp.float32),
            jax.ShapeDtypeStruct((1, n_chan), jnp.float32),
        ),
        compiler_params=pltpu.CompilerParams(vmem_limit_bytes=32 * 1024 * 1024),
        cost_estimate=pl.CostEstimate(flops=16 * 10**8, bytes_accessed=8 * 2**20, transcendentals=0),
        name="cells",
    )(tokens, grad_proj, gain, w_qkv)
    bias_sum = bias_sum[..., :n_cell] + bias_sum[..., n_cell:]
    bias_sum = jnp.dot(bias_sum.reshape(n_head, n_cell * n_cell), onehot, precision=lax.Precision.HIGHEST)
    return grad_cells, sums, gain_sum.reshape(n_chan), bias_sum


def blocks_of(field, window):
    n_rows, n_cols, n_chan = field.shape
    shaped = field.reshape(n_rows // window, window, n_cols // window, window, n_chan)
    return shaped.transpose(0, 2, 1, 3, 4).reshape(n_rows * n_cols, n_chan)


def grid_of(blocks, n_rows, n_cols, window):
    n_chan = blocks.shape[-1]
    shaped = blocks.reshape(n_rows // window, n_cols // window, window, window, n_chan)
    return shaped.transpose(0, 2, 1, 3, 4).reshape(n_rows, n_cols, n_chan)


def total_over_devices(array, axes):
    count = lax.axis_size(axes)
    parts = lax.all_to_all(array.astype(jnp.bfloat16).reshape(count, -1, array.shape[-1]), axes, 0, 0)
    return parts.astype(jnp.float32).sum(0)


def local(saved_state, cotangent, row_mask, shifts, norm_gain, w_qkv, w_out, bias_table):
    band_rows, cycle_cols, n_chan = saved_state.shape
    window = (math.isqrt(bias_table.shape[1]) + 1) // 2
    shift_lat = shifts[0]
    shift_lon = shifts[1]
    zero_index = shift_lat * 0
    mask_half = row_mask.astype(jnp.bfloat16)
    side_edge = shifted((saved_state[:, -window:], cotangent[:, -window:]), "lon", 1)
    wide_state = jnp.concatenate([side_edge[0], saved_state], 1)
    wide_cot = jnp.concatenate([side_edge[1], cotangent], 1)
    upper_edge = from_behind(
        (wide_state[-window:], wide_cot[-window:], mask_half[-window:]), "lat", 1
    )
    ext_state = jnp.concatenate([upper_edge[0], wide_state], 0)
    ext_cot = jnp.concatenate([upper_edge[1], wide_cot], 0)
    ext_mask = jnp.concatenate([upper_edge[2], mask_half], 0)
    crop_state = lax.dynamic_slice(
        ext_state, (shift_lat, shift_lon, zero_index), (band_rows, cycle_cols, n_chan)
    )
    crop_cot = lax.dynamic_slice(
        ext_cot, (shift_lat, shift_lon, zero_index), (band_rows, cycle_cols, n_chan)
    )
    live_rows = lax.dynamic_slice_in_dim(ext_mask, shift_lat, band_rows)
    grad_out = crop_cot * live_rows[:, None, None]
    key_mask = jnp.where(live_rows.astype(jnp.float32) > 0.5, 0.0, -1e30)
    key_mask = jnp.broadcast_to(
        key_mask.reshape(band_rows // window, window, 1, 1), (band_rows // window, window, window, 2 * window * window)
    ).reshape(band_rows // window, window * window, 2 * window * window)
    grad_cells, sums, gain_sum, bias_sum = window_backward(
        blocks_of(crop_state, window),
        blocks_of(grad_out, window),
        key_mask,
        norm_gain,
        w_qkv,
        w_out,
        bias_table,
    )
    grad_block = grid_of(grad_cells, band_rows, cycle_cols, window)
    ext_grad = jnp.zeros((band_rows + window, cycle_cols + window, n_chan), jnp.float32)
    ext_grad = lax.dynamic_update_slice(ext_grad, grad_block, (shift_lat, shift_lon, zero_index))
    lower_back = from_behind(ext_grad[:window].astype(jnp.bfloat16), "lat", -1).astype(jnp.float32)
    own_rows = ext_grad[window:]
    own_rows = jnp.concatenate([own_rows[:-window], own_rows[-window:] + lower_back], 0)
    side_back = shifted(own_rows[:, :window].astype(jnp.bfloat16), "lon", -1).astype(jnp.float32)
    own_cells = own_rows[:, window:]
    own_cells = jnp.concatenate([own_cells[:, :-window], own_cells[:, -window:] + side_back], 1)
    state_grad = (cotangent.astype(jnp.float32) + own_cells).astype(jnp.bfloat16)
    small = jnp.concatenate([gain_sum, bias_sum.reshape(-1)])
    norm_factor = 1.0 / math.sqrt(
        band_rows * lax.axis_size("lat") * cycle_cols * lax.axis_size("lon")
    )
    rest = -small.size % n_chan
    small = jnp.pad(small, (0, rest)).reshape(-1, n_chan)
    part = total_over_devices(total_over_devices(sums, "lon"), "lat")
    part = (part * norm_factor).astype(jnp.bfloat16)
    part = lax.all_gather(lax.all_gather(part, "lat", tiled=True), "lon", tiled=True).astype(jnp.float32)
    small = lax.psum(small, ("lat", "lon")).reshape(-1) * norm_factor
    return (
        state_grad,
        part[: 3 * n_chan].T,
        part[3 * n_chan :],
        small[:n_chan],
        small[n_chan : n_chan + bias_table.size].reshape(bias_table.shape),
    )


def solution(mesh):
    return jax.shard_map(
        local,
        mesh=mesh,
        in_specs=(P("lat", "lon", None), P("lat", "lon", None), P("lat"), P(), P(), P(), P(), P()),
        out_specs=(P("lat", "lon", None), P(), P(), P(), P()),
        check_vma=False,
    )
```

```python
import functools
import itertools
import math

import jax
import jax.numpy as jnp
from jax import lax
from jax.experimental import pallas as pl
from jax.experimental.pallas import tpu as pltpu
from jax.sharding import PartitionSpec as P

EPSILON = 1e-05


NT = (((1,), (1,)), ((), ()))
NN = (((1,), (0,)), ((), ()))
LANES = 128
WINDOW = 8
CELLS = WINDOW * WINDOW
TOKENS = 256
MIB = 1024 * 1024


def dot(a, b, dims=NN):
    return lax.dot_general(a, b, dims, preferred_element_type=jnp.float32)


def whole(*_):
    return pl.BlockSpec(memory_space=pltpu.VMEM)


def norm_stats(x):
    cen = x - jnp.mean(x, -1, keepdims=True)
    inv = lax.rsqrt(jnp.mean(cen * cen, -1, keepdims=True) + EPSILON)
    return cen * inv, inv


def project_chunk(n_chan, scale, gain, wt_ref, w_ref, wo_ref, xf, go_ref, nrm_t, proj_t, kv, gm_t, base):
    rows = slice(base, base + TOKENS)
    x_hat, _ = norm_stats(xf[rows])
    normed_f = x_hat * gain
    normed = normed_f.astype(jnp.bfloat16)
    nrm_t[:, rows] = normed_f.T.astype(jnp.bfloat16)
    proj_t[:n_chan, rows] = (dot(wt_ref[:n_chan], normed, NT) * scale).astype(jnp.bfloat16)
    proj_t[n_chan:, rows] = dot(wt_ref[n_chan:], normed, NT).astype(jnp.bfloat16)
    kv[rows] = dot(normed, w_ref[:, n_chan:]).astype(jnp.bfloat16)
    gm_t[:, rows] = dot(wo_ref[...], go_ref[rows], NT).astype(jnp.bfloat16)


def block_diag(block, step):
    blank = jnp.zeros((step, block.shape[1]), block.dtype)
    count = block.shape[0] // step
    columns = []
    for h in range(count):
        parts = [blank] * count
        parts[h] = block[h * step : (h + 1) * step]
        columns.append(jnp.concatenate(parts, 0))
    return jnp.concatenate(columns, 1)


def attention_unit(n_chan, dim, scale, bias_ref, mask, proj_t, kv, gm_t, mix_t, gp_t, bsum_ref, pair, group):
    lanes = pl.ds(pl.multiple_of(pair * LANES, LANES), LANES)
    c0 = pl.multiple_of(group * LANES, LANES)
    q_t = proj_t[pl.ds(c0, LANES), lanes]
    k_t = proj_t[pl.ds(n_chan + c0, LANES), lanes]
    v_t = proj_t[pl.ds(2 * n_chan + c0, LANES), lanes]
    g_t = gm_t[pl.ds(c0, LANES), lanes]
    k_tok = kv[lanes, pl.ds(c0, LANES)]
    v_tok = kv[lanes, pl.ds(n_chan + c0, LANES)]
    scores = dot(k_tok, block_diag(q_t, dim))
    grads = dot(v_tok, block_diag(g_t, dim))
    first = lax.broadcasted_iota(jnp.int32, (CELLS, LANES), 1) < CELLS
    heads = LANES // dim
    mixed, dq, dk, dv = [], [], [], []
    for h in range(heads):
        cut = slice(h * LANES, (h + 1) * LANES)
        rows = slice(h * dim, (h + 1) * dim)
        head = group * heads + h
        s = jnp.where(first, scores[:CELLS, cut], scores[CELLS:, cut]) + bias_ref[head] + mask
        e = jnp.exp(s - jnp.max(s, 0, keepdims=True))
        a = e * (1.0 / jnp.sum(e, 0, keepdims=True))
        d = jnp.where(first, grads[:CELLS, cut], grads[CELLS:, cut])
        ad = a * d
        ds = ad - a * jnp.sum(ad, 0, keepdims=True)
        bsum_ref[head] += ds
        zero = jnp.zeros_like(a)
        a2 = jnp.concatenate([jnp.where(first, a, zero), jnp.where(first, zero, a)], 0).astype(jnp.bfloat16)
        ds2 = jnp.concatenate([jnp.where(first, ds, zero), jnp.where(first, zero, ds)], 0).astype(jnp.bfloat16)
        mixed.append(dot(v_t[rows], a2))
        dv.append(dot(g_t[rows], a2, NT))
        dq.append(dot(k_t[rows], ds2) * scale)
        dk.append(dot(q_t[rows], ds2, NT))
    mix_t[pl.ds(c0, LANES), lanes] = jnp.concatenate(mixed, 0).astype(jnp.bfloat16)
    gp_t[pl.ds(c0, LANES), lanes] = jnp.concatenate(dq, 0).astype(jnp.bfloat16)
    gp_t[pl.ds(n_chan + c0, LANES), lanes] = jnp.concatenate(dk, 0).astype(jnp.bfloat16)
    gp_t[pl.ds(2 * n_chan + c0, LANES), lanes] = jnp.concatenate(dv, 0).astype(jnp.bfloat16)


def place_row(side, own, shift, out, r, live=None):
    line = jnp.concatenate([side.astype(jnp.float32), own.astype(jnp.float32)], 0).reshape(-1, WINDOW, own.shape[1])
    if live is not None:
        line = line * live
    line = pltpu.roll(line, WINDOW - shift, 1)
    head = lax.broadcasted_iota(jnp.int32, line.shape[1:], 0) < WINDOW - shift
    for w in range(line.shape[0] - 1):
        start = w * CELLS + r * WINDOW
        out[start : start + WINDOW] = jnp.where(head, line[w], line[w + 1])


def window_row(n_head, xf, cf, live, gain_ref, wt_ref, w_ref, wo_ref, bias_ref,
               x_out, go_ref, nrm_t, mix_t, gp_t, bsum_ref, proj_t, kv, gm_t):
    n_tok, n_chan = xf.shape
    dim = n_chan // n_head
    scale = dim ** (-0.5)
    x_out[...] = xf[...].astype(jnp.bfloat16)
    go_ref[...] = cf[...].astype(jnp.bfloat16)
    for base in range(0, n_tok, TOKENS):
        project_chunk(n_chan, scale, gain_ref[...], wt_ref, w_ref, wo_ref, xf, go_ref, nrm_t, proj_t, kv, gm_t, base)
    mask = jnp.concatenate(
        [jnp.broadcast_to((live[r] - 1.0) * 1e30, (WINDOW, LANES)) for r in range(WINDOW)], 0
    )
    groups = n_chan // LANES

    @pl.loop(0, n_tok // LANES * groups)
    def _(unit):
        attention_unit(n_chan, dim, scale, bias_ref, mask, proj_t, kv, gm_t, mix_t, gp_t, bsum_ref,
                       unit // groups, unit % groups)


def inner_kernel(n_head, meta, x_ref, cot_ref, side_ref, bias_ref, gain_ref, wt_ref, w_ref, wo_ref,
                 x_out, go_ref, nrm_t, mix_t, gp_t, bsum_ref, xf, cf, proj_t, kv, gm_t):
    lat, lon = meta[0], meta[1]
    live = []
    for r in range(WINDOW):
        live.append(meta[5 + WINDOW + lat + r].astype(jnp.float32))
        place_row(side_ref[0, lat + r], x_ref[lat + r], lon, xf, r)
        place_row(side_ref[1, lat + r], cot_ref[lat + r], lon, cf, r, live[r])
    bsum_ref[...] = jnp.zeros_like(bsum_ref)
    window_row(n_head, xf, cf, live, gain_ref, wt_ref, w_ref, wo_ref, bias_ref,
               x_out, go_ref, nrm_t, mix_t, gp_t, bsum_ref, proj_t, kv, gm_t)


def outer_kernel(n_head, counts, meta, x_ref, cot_ref, side_ref, top_ref, corner_ref, bias_ref, gain_ref, wt_ref, w_ref, wo_ref,
                 go_in, nrm_in, mix_in, gp_in, bsum_in,
                 x_out, gp_t, keep_ref, send_ref,
                 go_ref, nrm_t, mix_t, bsum_ref, xf, cf, proj_t, kv, gm_t, sums, spread_a, spread_b):
    n_chan = gain_ref.shape[1]
    lat, lon = meta[0], meta[1]
    live = []
    for r in range(WINDOW):
        e = lat + r
        above = e < WINDOW
        up = jnp.minimum(e, WINDOW - 1)
        own = jnp.maximum(e - WINDOW, 0)
        live.append(meta[5 + e].astype(jnp.float32))
        side = [jnp.where(above, corner_ref[k, up], side_ref[k, own]) for k in range(2)]
        place_row(side[0], jnp.where(above, top_ref[0, up], x_ref[own]), lon, xf, r)
        place_row(side[1], jnp.where(above, top_ref[1, up], cot_ref[own]), lon, cf, r, live[r])
    bsum_ref[...] = bsum_in[...]
    window_row(n_head, xf, cf, live, gain_ref, wt_ref, w_ref, wo_ref, bias_ref,
               x_out, go_ref, nrm_t, mix_t, gp_t, bsum_ref, proj_t, kv, gm_t)

    n_proj = 3 * n_chan
    gain_sum = jnp.zeros((n_chan, 1), jnp.float32)
    for base in range(0, n_proj, TOKENS):
        cols = slice(base, base + TOKENS)
        part = dot(nrm_in[...], gp_in[cols], NT) + dot(nrm_t[...], gp_t[cols], NT)
        sums[:, cols] = part
        gain_sum += jnp.sum(part * w_ref[:, cols].astype(jnp.float32), 1, keepdims=True)
    for base in range(0, n_chan, TOKENS):
        cols = slice(base, base + TOKENS)
        sums[:, n_proj + base : n_proj + base + TOKENS] = dot(mix_in[...], go_in[:, cols]) + dot(mix_t[...], go_ref[:, cols])

    width = 2 * LANES
    cell = lax.broadcasted_iota(jnp.int32, (LANES, width), 0) % CELLS
    lane = lax.broadcasted_iota(jnp.int32, (LANES, width), 1)
    place = (cell // WINDOW) * 16 + cell % WINDOW + 119
    onehot = (lane == place).astype(jnp.float32).astype(jnp.bfloat16)
    flat = bsum_ref[...].reshape(n_head * CELLS, LANES)
    high = flat.astype(jnp.bfloat16)
    low = (flat - high.astype(jnp.float32)).astype(jnp.bfloat16)
    spread = dot(high, onehot) + dot(low, onehot)
    spread_a[...] = spread[:, :LANES]
    spread_b[...] = spread[:, LANES:]
    bias_sum = jnp.zeros((n_head, width), jnp.float32)
    for j in range(CELLS):
        row = jnp.concatenate([ref[pl.ds(j, n_head, stride=CELLS), :] for ref in (spread_a, spread_b)], 1)
        by = (j // WINDOW) * 16 + j % WINDOW
        bias_sum += pltpu.roll(row, width - by, 1) if by else row
    tail = lax.broadcasted_iota(jnp.int32, (n_chan, LANES), 1) == LANES - 1
    bias_rows = jnp.concatenate(
        [bias_sum[:, :LANES], bias_sum[:, LANES:], jnp.zeros((n_chan - 2 * n_head, LANES), jnp.float32)], 0
    )
    sums[:, n_proj + n_chan :] = jnp.where(tail, gain_sum * (1.0 / gain_col(gain_ref)), bias_rows)

    n_c, n_x, n_y = counts
    rows = n_chan // (n_c * n_x * n_y)
    for c in range(n_c):
        for x in range(n_x):
            for y in range(n_y):
                chunk = sums[((c * n_x + x) * n_y + y) * rows : ((c * n_x + x) * n_y + y + 1) * rows]
                at = lax.rem(x - meta[3] + n_x, n_x) * n_y + lax.rem(y - meta[4] + n_y, n_y)

                @pl.when(meta[2] == c)
                def _():
                    keep_ref[at] = chunk

                @pl.when(meta[2] != c)
                def _():
                    send_ref[at] = chunk.astype(jnp.bfloat16)


def gain_col(gain_ref):
    n_chan = gain_ref.shape[1]
    return jnp.broadcast_to(gain_ref[...], (LANES, n_chan)).T[:, :1]


def cells_kernel(meta, xa_ref, xb_ref, gpa_ref, gpb_ref, cot_ref, gain_ref, w_ref, base_ref, top_ref, side_ref, ext):
    n_rows, n_cols, n_chan = cot_ref.shape
    lat, lon = meta[0], meta[1]
    ext[...] = jnp.zeros_like(ext)
    for part, (x_ref, gp_t) in enumerate(((xb_ref, gpb_ref), (xa_ref, gpa_ref))):
        n_tok = x_ref.shape[0]
        cells = []
        for base in range(0, n_tok, TOKENS):
            rows = slice(base, base + TOKENS)
            x_hat, inv = norm_stats(x_ref[rows].astype(jnp.float32))
            g = dot(w_ref[...], gp_t[:, rows]).T * gain_ref[...]
            cells.append(inv * (g - jnp.mean(g, -1, keepdims=True) - x_hat * jnp.mean(g * x_hat, -1, keepdims=True)))
        blank = jnp.zeros((1, WINDOW, n_chan), jnp.float32)
        head = lax.broadcasted_iota(jnp.int32, (WINDOW, n_chan), 0) < lon
        for r in range(WINDOW):
            row = jnp.stack(
                [
                    cells[w * CELLS // TOKENS][w * CELLS % TOKENS + r * WINDOW :][:WINDOW]
                    for w in range(n_tok // CELLS)
                ],
                0,
            )
            row = jnp.concatenate([blank, pltpu.roll(row, lon, 1), blank], 0)
            for t in range(row.shape[0] - 1):
                ext[lat + part * WINDOW + r, t * WINDOW : (t + 1) * WINDOW, :] = jnp.where(head, row[t], row[t + 1])
    for r in range(n_rows):
        base_ref[r] = (cot_ref[r].astype(jnp.float32) + ext[WINDOW + r, WINDOW:]).astype(jnp.bfloat16)
        side_ref[r] = ext[WINDOW + r, :WINDOW].astype(jnp.bfloat16)
    top_ref[...] = ext[:WINDOW].astype(jnp.bfloat16)


def first_add_kernel(keep_ref, got_ref, own_ref, *send_refs):
    size = own_ref.shape[0]
    for k in range(len(send_refs) + 1):
        cut = slice(k * size, (k + 1) * size)
        total = keep_ref[cut] + got_ref[cut].astype(jnp.float32)
        if k:
            send_refs[k - 1][...] = total.astype(jnp.bfloat16)
        else:
            own_ref[...] = total


def next_add_kernel(n_got, own_ref, *refs):
    got, out_ref, send_refs = refs[:n_got], refs[n_got], refs[n_got + 1 :]
    size = out_ref.shape[0]
    for k in range(len(send_refs) + 1):
        cut = slice(k * size, (k + 1) * size)
        total = own_ref[cut]
        for ref in got:
            total = total + ref[cut].astype(jnp.float32)
        if k:
            send_refs[k - 1][...] = total.astype(jnp.bfloat16)
        else:
            out_ref[...] = total.astype(out_ref.dtype)


def unpack_kernel(counts, n_proj, factor, meta, mine_ref, other_ref, qkv_ref, out_ref, small_ref):
    n_c, n_x, n_y = counts
    rows = mine_ref.shape[1]
    n_chan = out_ref.shape[1]
    for c in range(n_c):
        for x in range(n_x):
            for y in range(n_y):
                at = lax.rem(x - meta[3] + n_x, n_x) * n_y + lax.rem(y - meta[4] + n_y, n_y)
                chunk = jnp.where(meta[2] == c, mine_ref[at], other_ref[at]).astype(jnp.float32) * factor
                to = slice(((c * n_x + x) * n_y + y) * rows, ((c * n_x + x) * n_y + y + 1) * rows)
                qkv_ref[to] = chunk[:, :n_proj]
                out_ref[to] = chunk[:, n_proj : n_proj + n_chan]
                small_ref[to] = chunk[:, n_proj + n_chan :]


class Places:
    def __init__(self):
        self.n_lat, self.n_lon = lax.axis_size("lat"), lax.axis_size("lon")
        self.c = 2
        self.x = min(4, self.n_lon // self.c)
        self.y_low = self.n_lon // (self.c * self.x)
        self.y_high = 2
        self.y = self.y_low * self.y_high
        self.z = self.n_lat // self.y_high

    def index(self, z, y, x, c):
        high, low = divmod(y, self.y_low)
        return (z * self.y_high + high) * self.n_lon + (low * self.x + x) * self.c + c

    def mine(self):
        lat, lon = lax.axis_index("lat"), lax.axis_index("lon")
        return (
            lon % self.c,
            lon // self.c % self.x,
            lat % self.y_high * self.y_low + lon // (self.c * self.x),
        )

    def move(self, array, to):
        every = itertools.product(range(self.z), range(self.y), range(self.x), range(self.c))
        pairs = [(self.index(*at), self.index(*to(*at))) for at in every]
        return lax.ppermute(array, ("lat", "lon"), pairs)

    def by_c(self, array):
        return self.move(array, lambda z, y, x, c: (z, y, x, 1 - c))

    def by_x(self, array, k):
        return self.move(array, lambda z, y, x, c: (z, y, (x + k) % self.x, c))

    def by_y(self, array, k):
        return self.move(array, lambda z, y, x, c: (z, (y + k) % self.y, x, c))

    def by_z(self, array, bits):
        return self.move(array, lambda z, y, x, c: (z ^ bits, y, x, c))


def small_call(kernel, outs, name, *args):
    return pl.pallas_call(
        kernel,
        out_shape=outs,
        compiler_params=pltpu.CompilerParams(vmem_limit_bytes=32 * MIB),
        name=name,
    )(*args)


def total_over_devices(places, keep, send):
    shape = keep.shape[1:]
    bf = functools.partial(jax.ShapeDtypeStruct, dtype=jnp.bfloat16)
    got = places.by_c(send)
    own = jax.ShapeDtypeStruct((places.y, *shape), jnp.float32)
    own, *sends = small_call(first_add_kernel, (own,) + (bf((places.y, *shape)),) * (places.x - 1), "add_c", keep, got)
    got = [places.by_x(part, k + 1) for k, part in enumerate(sends)]
    nxt = jax.ShapeDtypeStruct((1, *shape), jnp.float32)
    own, *sends = small_call(
        functools.partial(next_add_kernel, len(got)), (nxt,) + (bf((1, *shape)),) * (places.y - 1), "add_x", own, *got
    )
    got = [places.by_y(part, k + 1) for k, part in enumerate(sends)]
    (mine,) = small_call(functools.partial(next_add_kernel, len(got)), (bf((1, *shape)),), "add_y", own, *got)
    for bits in {1: (), 2: (1,), 4: (1, 3), 8: (1, 2, 6)}[places.z]:
        other = places.by_z(mine, bits)
        mine = (mine.astype(jnp.float32) + other.astype(jnp.float32)).astype(jnp.bfloat16)
    mine = jnp.concatenate([mine] + [places.by_y(mine, -k) for k in range(1, places.y)], 0)
    mine = jnp.concatenate([mine] + [places.by_x(mine, -k) for k in range(1, places.x)], 0)
    return mine, places.by_c(mine)


def ring(array, lat, lon):
    n_lat, n_lon = lax.axis_size("lat"), lax.axis_size("lon")
    pairs = [
        (i * n_lon + j, (i + lat) % n_lat * n_lon + (j + lon) % n_lon) for i in range(n_lat) for j in range(n_lon)
    ]
    return lax.ppermute(array, ("lat", "lon"), pairs)


def bias_of_pairs(bias_table):
    places = jnp.arange(CELLS)
    row_of, col_of = places // WINDOW, places % WINDOW
    row_gap = row_of[None, :] - row_of[:, None] + WINDOW - 1
    col_gap = col_of[None, :] - col_of[:, None] + WINDOW - 1
    gap = (row_gap * (2 * WINDOW - 1) + col_gap).reshape(-1)
    onehot = (jnp.arange(bias_table.shape[1])[:, None] == gap[None, :]).astype(jnp.float32)
    full = jnp.dot(bias_table, onehot, precision=lax.Precision.HIGHEST).reshape(-1, CELLS, CELLS)
    return jnp.concatenate([full, full], -1)


def local(saved_state, cotangent, row_mask, shifts, norm_gain, w_qkv, w_out, bias_table):
    n_rows, n_cols, n_chan = saved_state.shape
    n_head = bias_table.shape[0]
    n_proj = w_qkv.shape[1]
    n_tok = n_rows // 2 * n_cols
    places = Places()
    counts = (places.c, places.x, places.y)
    bf, f32 = jnp.bfloat16, jnp.float32

    side = ring(jnp.stack([saved_state[:, -WINDOW:], cotangent[:, -WINDOW:]]), 0, 1)
    top = ring(jnp.stack([saved_state[-WINDOW:], cotangent[-WINDOW:]]), 1, 0)
    mask_block = jnp.broadcast_to(row_mask[-WINDOW:, None, None].astype(bf), (WINDOW, WINDOW, n_chan))
    corner = ring(
        jnp.stack([saved_state[-WINDOW:, -WINDOW:], cotangent[-WINDOW:, -WINDOW:], mask_block]), 1, 1
    )
    at = jnp.stack(places.mine()).astype(jnp.int32)
    bias = bias_of_pairs(bias_table)
    gain = norm_gain.reshape(1, n_chan)
    w_t = w_qkv.T

    smem = pl.BlockSpec(memory_space=pltpu.SMEM)
    tile = functools.partial(jax.ShapeDtypeStruct, dtype=bf)
    work = [
        pltpu.VMEM((n_tok, n_chan), f32),
        pltpu.VMEM((n_tok, n_chan), f32),
        pltpu.VMEM((n_proj, n_tok), bf),
        pltpu.VMEM((n_tok, 2 * n_chan), bf),
        pltpu.VMEM((n_chan, n_tok), bf),
    ]
    meta_inner = jnp.concatenate([shifts, at, jnp.zeros((WINDOW,), jnp.int32), row_mask])
    x_in, go_in, nrm_in, mix_in, gp_in, bsum_in = pl.pallas_call(
        functools.partial(inner_kernel, n_head),
        out_shape=(
            tile((n_tok, n_chan)),
            tile((n_tok, n_chan)),
            tile((n_chan, n_tok)),
            tile((n_chan, n_tok)),
            tile((n_proj, n_tok)),
            jax.ShapeDtypeStruct((n_head, CELLS, LANES), f32),
        ),
        in_specs=[smem] + [whole()] * 8,
        scratch_shapes=work,
        compiler_params=pltpu.CompilerParams(vmem_limit_bytes=40 * MIB),
        cost_estimate=pl.CostEstimate(flops=8 * 10**9, bytes_accessed=16 * MIB, transcendentals=2**19),
        name="inner",
    )(meta_inner, saved_state, cotangent, side, bias, gain, w_t, w_qkv, w_out)

    above = jnp.where(lax.axis_index("lat") > 0, corner[2, :, 0, 0].astype(jnp.int32), 0)
    meta = jnp.concatenate([shifts, at, above, row_mask])
    width = n_proj + n_chan + LANES
    rows = n_chan // math.prod(counts)
    half = math.prod(counts) // 2
    x_out, gp_out, keep, send = pl.pallas_call(
        functools.partial(outer_kernel, n_head, counts),
        out_shape=(
            tile((n_tok, n_chan)),
            tile((n_proj, n_tok)),
            jax.ShapeDtypeStruct((half, rows, width), f32),
            tile((half, rows, width)),
        ),
        in_specs=[smem] + [whole()] * 15,
        scratch_shapes=[
            pltpu.VMEM((n_tok, n_chan), bf),
            pltpu.VMEM((n_chan, n_tok), bf),
            pltpu.VMEM((n_chan, n_tok), bf),
            pltpu.VMEM((n_head, CELLS, LANES), f32),
            *work,
            pltpu.VMEM((n_chan, width), f32),
            pltpu.VMEM((n_head * CELLS, LANES), f32),
            pltpu.VMEM((n_head * CELLS, LANES), f32),
        ],
        compiler_params=pltpu.CompilerParams(vmem_limit_bytes=56 * MIB),
        cost_estimate=pl.CostEstimate(flops=10**10, bytes_accessed=24 * MIB, transcendentals=2**19),
        name="outer",
    )(meta, saved_state, cotangent, side, top, corner, bias, gain, w_t, w_qkv, w_out, go_in, nrm_in, mix_in, gp_in, bsum_in)

    mine, other = total_over_devices(places, keep, send)

    base, top_grad, side_grad = pl.pallas_call(
        cells_kernel,
        out_shape=(
            tile((n_rows, n_cols, n_chan)),
            tile((WINDOW, n_cols + WINDOW, n_chan)),
            tile((n_rows, WINDOW, n_chan)),
        ),
        in_specs=[smem] + [whole()] * 7,
        scratch_shapes=[pltpu.VMEM((n_rows + WINDOW, n_cols + WINDOW, n_chan), f32)],
        compiler_params=pltpu.CompilerParams(vmem_limit_bytes=40 * MIB),
        cost_estimate=pl.CostEstimate(flops=16 * 10**8, bytes_accessed=12 * MIB, transcendentals=0),
        name="cells",
    )(meta, x_in, x_out, gp_in, gp_out, cotangent, gain, w_qkv)
    top_grad = ring(top_grad, -1, 0)
    side_grad = jnp.concatenate([side_grad[:-WINDOW], side_grad[-WINDOW:] + top_grad[:, :WINDOW]], 0)
    side_grad = ring(side_grad, 0, -1)
    edge = jnp.pad(top_grad[:, WINDOW:], ((n_rows - WINDOW, 0), (0, 0), (0, 0)))
    edge = edge + jnp.pad(side_grad, ((0, 0), (n_cols - WINDOW, 0), (0, 0)))
    state_grad = (base.astype(f32) + edge.astype(f32)).astype(bf)

    factor = 1.0 / math.sqrt(n_rows * places.n_lat * n_cols * places.n_lon)
    qkv_grad, out_grad, small = pl.pallas_call(
        functools.partial(unpack_kernel, counts, n_proj, factor),
        out_shape=(
            jax.ShapeDtypeStruct((n_chan, n_proj), f32),
            jax.ShapeDtypeStruct((n_chan, n_chan), f32),
            jax.ShapeDtypeStruct((n_chan, LANES), f32),
        ),
        in_specs=[smem] + [whole()] * 2,
        compiler_params=pltpu.CompilerParams(vmem_limit_bytes=32 * MIB),
        name="unpack",
    )(meta_inner, mine, other)
    bias_grad = jnp.concatenate([small[:n_head], small[n_head : 2 * n_head]], 1).reshape(n_head, 16, 16)
    span = 2 * WINDOW - 1
    return state_grad, qkv_grad, out_grad, small[:, LANES - 1], bias_grad[:, :span, :span].reshape(n_head, -1)


def solution(mesh):
    return jax.shard_map(
        local,
        mesh=mesh,
        in_specs=(P("lat", "lon", None), P("lat", "lon", None), P("lat"), P(), P(), P(), P(), P()),
        out_specs=(P("lat", "lon", None), P(), P(), P(), P()),
        check_vma=False,
    )
```

```python
import functools
import itertools
import math

import jax
import jax.numpy as jnp
from jax import lax
from jax.experimental import pallas as pl
from jax.experimental.pallas import tpu as pltpu
from jax.sharding import PartitionSpec as P

EPSILON = 1e-05


NT = (((1,), (1,)), ((), ()))
NN = (((1,), (0,)), ((), ()))
LANES = 128
WINDOW = 8
CELLS = WINDOW * WINDOW
TOKENS = 256
MIB = 1024 * 1024


def dot(a, b, dims=NN):
    return lax.dot_general(a, b, dims, preferred_element_type=jnp.float32)


def whole(*_):
    return pl.BlockSpec(memory_space=pltpu.VMEM)


def norm_stats(x):
    cen = x - jnp.mean(x, -1, keepdims=True)
    inv = lax.rsqrt(jnp.mean(cen * cen, -1, keepdims=True) + EPSILON)
    return cen * inv, inv


def project_chunk(n_chan, scale, gain, wt_ref, w_ref, wo_ref, xf, go_ref, nrm_t, proj_t, kv, gm_t, base):
    rows = slice(base, base + TOKENS)
    x_hat, _ = norm_stats(xf[rows])
    normed_f = x_hat * gain
    normed = normed_f.astype(jnp.bfloat16)
    nrm_t[:, rows] = normed_f.T.astype(jnp.bfloat16)
    proj_t[:n_chan, rows] = (dot(wt_ref[:n_chan], normed, NT) * scale).astype(jnp.bfloat16)
    proj_t[n_chan:, rows] = dot(wt_ref[n_chan:], normed, NT).astype(jnp.bfloat16)
    kv[rows] = dot(normed, w_ref[:, n_chan:]).astype(jnp.bfloat16)
    gm_t[:, rows] = dot(wo_ref[...], go_ref[rows], NT).astype(jnp.bfloat16)


def block_diag(block, step):
    blank = jnp.zeros((step, block.shape[1]), block.dtype)
    count = block.shape[0] // step
    columns = []
    for h in range(count):
        parts = [blank] * count
        parts[h] = block[h * step : (h + 1) * step]
        columns.append(jnp.concatenate(parts, 0))
    return jnp.concatenate(columns, 1)


def attention_unit(n_chan, dim, scale, bias_ref, mask, proj_t, kv, gm_t, mix_t, gp_t, bsum_ref, pair, group):
    lanes = pl.ds(pl.multiple_of(pair * LANES, LANES), LANES)
    c0 = pl.multiple_of(group * LANES, LANES)
    q_t = proj_t[pl.ds(c0, LANES), lanes]
    k_t = proj_t[pl.ds(n_chan + c0, LANES), lanes]
    v_t = proj_t[pl.ds(2 * n_chan + c0, LANES), lanes]
    g_t = gm_t[pl.ds(c0, LANES), lanes]
    k_tok = kv[lanes, pl.ds(c0, LANES)]
    v_tok = kv[lanes, pl.ds(n_chan + c0, LANES)]
    scores = dot(k_tok, block_diag(q_t, dim))
    grads = dot(v_tok, block_diag(g_t, dim))
    first = lax.broadcasted_iota(jnp.int32, (CELLS, LANES), 1) < CELLS
    heads = LANES // dim
    mixed, dq, dk, dv = [], [], [], []
    for h in range(heads):
        cut = slice(h * LANES, (h + 1) * LANES)
        rows = slice(h * dim, (h + 1) * dim)
        head = group * heads + h
        s = jnp.where(first, scores[:CELLS, cut], scores[CELLS:, cut]) + bias_ref[head] + mask
        e = jnp.exp(s - jnp.max(s, 0, keepdims=True))
        a = e * (1.0 / jnp.sum(e, 0, keepdims=True))
        d = jnp.where(first, grads[:CELLS, cut], grads[CELLS:, cut])
        ad = a * d
        ds = ad - a * jnp.sum(ad, 0, keepdims=True)
        bsum_ref[head] += ds
        zero = jnp.zeros_like(a)
        a2 = jnp.concatenate([jnp.where(first, a, zero), jnp.where(first, zero, a)], 0).astype(jnp.bfloat16)
        ds2 = jnp.concatenate([jnp.where(first, ds, zero), jnp.where(first, zero, ds)], 0).astype(jnp.bfloat16)
        mixed.append(dot(v_t[rows], a2))
        dv.append(dot(g_t[rows], a2, NT))
        dq.append(dot(k_t[rows], ds2) * scale)
        dk.append(dot(q_t[rows], ds2, NT))
    mix_t[pl.ds(c0, LANES), lanes] = jnp.concatenate(mixed, 0).astype(jnp.bfloat16)
    gp_t[pl.ds(c0, LANES), lanes] = jnp.concatenate(dq, 0).astype(jnp.bfloat16)
    gp_t[pl.ds(n_chan + c0, LANES), lanes] = jnp.concatenate(dk, 0).astype(jnp.bfloat16)
    gp_t[pl.ds(2 * n_chan + c0, LANES), lanes] = jnp.concatenate(dv, 0).astype(jnp.bfloat16)


def place_row(side, own, shift, out, r, live=None):
    line = jnp.concatenate([side.astype(jnp.float32), own.astype(jnp.float32)], 0).reshape(-1, WINDOW, own.shape[1])
    if live is not None:
        line = line * live
    line = pltpu.roll(line, WINDOW - shift, 1)
    head = lax.broadcasted_iota(jnp.int32, line.shape[1:], 0) < WINDOW - shift
    for w in range(line.shape[0] - 1):
        start = w * CELLS + r * WINDOW
        out[start : start + WINDOW] = jnp.where(head, line[w], line[w + 1])


def window_row(n_head, xf, cf, live, gain_ref, wt_ref, w_ref, wo_ref, bias_ref,
               x_out, go_ref, nrm_t, mix_t, gp_t, bsum_ref, proj_t, kv, gm_t):
    n_tok, n_chan = xf.shape
    dim = n_chan // n_head
    scale = dim ** (-0.5)
    x_out[...] = xf[...].astype(jnp.bfloat16)
    go_ref[...] = cf[...].astype(jnp.bfloat16)
    for base in range(0, n_tok, TOKENS):
        project_chunk(n_chan, scale, gain_ref[...], wt_ref, w_ref, wo_ref, xf, go_ref, nrm_t, proj_t, kv, gm_t, base)
    mask = jnp.concatenate(
        [jnp.broadcast_to((live[r] - 1.0) * 1e30, (WINDOW, LANES)) for r in range(WINDOW)], 0
    )
    groups = n_chan // LANES

    @pl.loop(0, n_tok // LANES * groups)
    def _(unit):
        attention_unit(n_chan, dim, scale, bias_ref, mask, proj_t, kv, gm_t, mix_t, gp_t, bsum_ref,
                       unit // groups, unit % groups)


def inner_kernel(n_head, meta, x_ref, cot_ref, side_ref, bias_ref, gain_ref, wt_ref, w_ref, wo_ref,
                 x_out, go_ref, nrm_t, mix_t, gp_t, bsum_ref, xf, cf, proj_t, kv, gm_t):
    lat, lon = meta[0], meta[1]
    live = []
    for r in range(WINDOW):
        live.append(meta[5 + WINDOW + lat + r].astype(jnp.float32))
        place_row(side_ref[0, lat + r], x_ref[lat + r], lon, xf, r)
        place_row(side_ref[1, lat + r], cot_ref[lat + r], lon, cf, r, live[r])
    bsum_ref[...] = jnp.zeros_like(bsum_ref)
    window_row(n_head, xf, cf, live, gain_ref, wt_ref, w_ref, wo_ref, bias_ref,
               x_out, go_ref, nrm_t, mix_t, gp_t, bsum_ref, proj_t, kv, gm_t)


def outer_kernel(n_head, counts, meta, x_ref, cot_ref, side_ref, top_ref, corner_ref, bias_ref, gain_ref, wt_ref, w_ref, wo_ref,
                 go_in, nrm_in, mix_in, gp_in, bsum_in,
                 x_out, gp_t, keep_ref, send_ref,
                 go_ref, nrm_t, mix_t, bsum_ref, xf, cf, proj_t, kv, gm_t, sums, spread_a, spread_b):
    n_chan = gain_ref.shape[1]
    n_top = top_ref.shape[1]
    lat, lon = meta[0], meta[1]
    live = []
    for r in range(WINDOW):
        e = lat + r
        above = e < WINDOW
        up = jnp.clip(e - (WINDOW - n_top), 0, n_top - 1)
        own = jnp.maximum(e - WINDOW, 0)
        live.append(meta[5 + e].astype(jnp.float32))
        side = [jnp.where(above, corner_ref[k, up], side_ref[k, own]) for k in range(2)]
        place_row(side[0], jnp.where(above, top_ref[0, up], x_ref[own]), lon, xf, r)
        place_row(side[1], jnp.where(above, top_ref[1, up], cot_ref[own]), lon, cf, r, live[r])
    bsum_ref[...] = bsum_in[...]
    window_row(n_head, xf, cf, live, gain_ref, wt_ref, w_ref, wo_ref, bias_ref,
               x_out, go_ref, nrm_t, mix_t, gp_t, bsum_ref, proj_t, kv, gm_t)

    n_proj = 3 * n_chan
    gain_sum = jnp.zeros((n_chan, 1), jnp.float32)
    for base in range(0, n_proj, TOKENS):
        cols = slice(base, base + TOKENS)
        part = dot(nrm_in[...], gp_in[cols], NT) + dot(nrm_t[...], gp_t[cols], NT)
        sums[:, cols] = part
        gain_sum += jnp.sum(part * w_ref[:, cols].astype(jnp.float32), 1, keepdims=True)
    for base in range(0, n_chan, TOKENS):
        cols = slice(base, base + TOKENS)
        sums[:, n_proj + base : n_proj + base + TOKENS] = dot(mix_in[...], go_in[:, cols]) + dot(mix_t[...], go_ref[:, cols])

    width = 2 * LANES
    cell = lax.broadcasted_iota(jnp.int32, (LANES, width), 0) % CELLS
    lane = lax.broadcasted_iota(jnp.int32, (LANES, width), 1)
    place = (cell // WINDOW) * 16 + cell % WINDOW + 119
    onehot = (lane == place).astype(jnp.float32).astype(jnp.bfloat16)
    flat = bsum_ref[...].reshape(n_head * CELLS, LANES)
    high = flat.astype(jnp.bfloat16)
    low = (flat - high.astype(jnp.float32)).astype(jnp.bfloat16)
    spread = dot(high, onehot) + dot(low, onehot)
    spread_a[...] = spread[:, :LANES]
    spread_b[...] = spread[:, LANES:]
    bias_sum = jnp.zeros((n_head, width), jnp.float32)
    for j in range(CELLS):
        row = jnp.concatenate([ref[pl.ds(j, n_head, stride=CELLS), :] for ref in (spread_a, spread_b)], 1)
        by = (j // WINDOW) * 16 + j % WINDOW
        bias_sum += pltpu.roll(row, width - by, 1) if by else row
    tail = lax.broadcasted_iota(jnp.int32, (n_chan, LANES), 1) == LANES - 1
    bias_rows = jnp.concatenate(
        [bias_sum[:, :LANES], bias_sum[:, LANES:], jnp.zeros((n_chan - 2 * n_head, LANES), jnp.float32)], 0
    )
    sums[:, n_proj + n_chan :] = jnp.where(tail, gain_sum * (1.0 / gain_col(gain_ref)), bias_rows)

    n_c, n_x, n_y = counts
    rows = n_chan // (n_c * n_x * n_y)
    for c in range(n_c):
        for x in range(n_x):
            for y in range(n_y):
                chunk = sums[((c * n_x + x) * n_y + y) * rows : ((c * n_x + x) * n_y + y + 1) * rows]
                at = lax.rem(x - meta[3] + n_x, n_x) * n_y + lax.rem(y - meta[4] + n_y, n_y)

                @pl.when(meta[2] == c)
                def _():
                    keep_ref[at] = chunk

                @pl.when(meta[2] != c)
                def _():
                    send_ref[at] = chunk.astype(jnp.bfloat16)


def gain_col(gain_ref):
    n_chan = gain_ref.shape[1]
    return jnp.broadcast_to(gain_ref[...], (LANES, n_chan)).T[:, :1]


def cells_kernel(meta, xa_ref, xb_ref, gpa_ref, gpb_ref, cot_ref, gain_ref, w_ref, base_ref, top_ref, side_ref, ext):
    n_rows, n_cols, n_chan = cot_ref.shape
    lat, lon = meta[0], meta[1]
    ext[...] = jnp.zeros_like(ext)
    for part, (x_ref, gp_t) in enumerate(((xb_ref, gpb_ref), (xa_ref, gpa_ref))):
        n_tok = x_ref.shape[0]
        cells = []
        for base in range(0, n_tok, TOKENS):
            rows = slice(base, base + TOKENS)
            x_hat, inv = norm_stats(x_ref[rows].astype(jnp.float32))
            g = dot(w_ref[...], gp_t[:, rows]).T * gain_ref[...]
            cells.append(inv * (g - jnp.mean(g, -1, keepdims=True) - x_hat * jnp.mean(g * x_hat, -1, keepdims=True)))
        blank = jnp.zeros((1, WINDOW, n_chan), jnp.float32)
        head = lax.broadcasted_iota(jnp.int32, (WINDOW, n_chan), 0) < lon
        for r in range(WINDOW):
            row = jnp.stack(
                [
                    cells[w * CELLS // TOKENS][w * CELLS % TOKENS + r * WINDOW :][:WINDOW]
                    for w in range(n_tok // CELLS)
                ],
                0,
            )
            row = jnp.concatenate([blank, pltpu.roll(row, lon, 1), blank], 0)
            for t in range(row.shape[0] - 1):
                ext[lat + part * WINDOW + r, t * WINDOW : (t + 1) * WINDOW, :] = jnp.where(head, row[t], row[t + 1])
    for r in range(n_rows):
        base_ref[r] = (cot_ref[r].astype(jnp.float32) + ext[WINDOW + r, WINDOW:]).astype(jnp.bfloat16)
        side_ref[r] = ext[WINDOW + r, :WINDOW].astype(jnp.bfloat16)
    top_ref[...] = ext[WINDOW - top_ref.shape[0] : WINDOW].astype(jnp.bfloat16)


def prepare_kernel(bias_ref, w_ref, full_ref, wt_ref):
    n_head, n_gap = bias_ref.shape
    span = 2 * WINDOW - 1
    width = 2 * LANES
    lane = lax.broadcasted_iota(jnp.int32, (width, LANES), 0)
    cell = lax.broadcasted_iota(jnp.int32, (width, LANES), 1) % CELLS
    place = cell // WINDOW * span + cell % WINDOW + n_gap // 2
    onehot = (lane == place).astype(jnp.float32).astype(jnp.bfloat16)
    table = jnp.concatenate([bias_ref[...], jnp.zeros((n_head, width - n_gap), jnp.float32)], 1)
    for h in range(n_head):
        line = jnp.broadcast_to(table[h : h + 1], (WINDOW, width))
        rows = [pltpu.roll(line, r * span, 1, stride=1, stride_axis=0) for r in range(WINDOW)]
        rest = jnp.concatenate(rows, 0)
        total = jnp.zeros((CELLS, LANES), jnp.float32)
        for _ in range(3):
            part = rest.astype(jnp.bfloat16)
            total += dot(part, onehot)
            rest = rest - part.astype(jnp.float32)
        full_ref[h] = total
    wt_ref[...] = w_ref[...].T


def pack_kernel(n_top, x_ref, cot_ref, mask, side_ref, top_ref, corner_ref):
    n_rows, n_cols, n_chan = x_ref.shape
    for k, ref in enumerate((x_ref, cot_ref)):
        for r in range(n_rows):
            edge = ref[r, n_cols - 2 * WINDOW :, :][WINDOW:]
            side_ref[k, r] = edge
            if r >= n_rows - n_top:
                top_ref[k, r - n_rows + n_top] = ref[r]
                corner_ref[k, r - n_rows + n_top] = edge
    for r in range(WINDOW):
        live = mask[n_rows - WINDOW + r].astype(jnp.float32)
        corner_ref[2, r] = jnp.broadcast_to(live, (WINDOW, n_chan)).astype(jnp.bfloat16)
    for k in range(2):
        for r in range(n_top, WINDOW):
            corner_ref[k, r] = jnp.zeros((WINDOW, n_chan), jnp.bfloat16)


def first_add_kernel(keep_ref, got_ref, own_ref, *send_refs):
    size = own_ref.shape[0]
    for k in range(len(send_refs) + 1):
        cut = slice(k * size, (k + 1) * size)
        total = keep_ref[cut] + got_ref[cut].astype(jnp.float32)
        if k:
            send_refs[k - 1][...] = total.astype(jnp.bfloat16)
        else:
            own_ref[...] = total


def next_add_kernel(n_got, n_more, own_ref, *refs):
    got, (out_ref, *send_refs) = refs[:n_got], refs[n_got + n_more :]
    size = out_ref.shape[0]
    for k in range(len(send_refs) + 1):
        cut = slice(k * size, (k + 1) * size)
        total = own_ref[cut]
        for ref in got:
            total = total + ref[cut].astype(jnp.float32)
        if k:
            send_refs[k - 1][...] = total.astype(jnp.bfloat16)
        else:
            out_ref[...] = total.astype(out_ref.dtype)


def unpack_kernel(counts, n_proj, factor, meta, mine_ref, other_ref, qkv_ref, out_ref, small_ref):
    n_c, n_x, n_y = counts
    rows = mine_ref.shape[1]
    n_chan = out_ref.shape[1]
    for c in range(n_c):
        for x in range(n_x):
            for y in range(n_y):
                at = lax.rem(x - meta[3] + n_x, n_x) * n_y + lax.rem(y - meta[4] + n_y, n_y)
                chunk = jnp.where(meta[2] == c, mine_ref[at], other_ref[at]).astype(jnp.float32) * factor
                to = slice(((c * n_x + x) * n_y + y) * rows, ((c * n_x + x) * n_y + y + 1) * rows)
                qkv_ref[to] = chunk[:, :n_proj]
                out_ref[to] = chunk[:, n_proj : n_proj + n_chan]
                small_ref[to] = chunk[:, n_proj + n_chan :]


class Places:
    def __init__(self):
        self.n_lat, self.n_lon = lax.axis_size("lat"), lax.axis_size("lon")
        self.c = 2
        self.x = min(4, self.n_lon // self.c)
        self.y_low = self.n_lon // (self.c * self.x)
        self.y_high = 2
        self.y = self.y_low * self.y_high
        self.z = self.n_lat // self.y_high

    def index(self, z, y, x, c):
        high, low = divmod(y, self.y_low)
        return (z * self.y_high + high) * self.n_lon + (low * self.x + x) * self.c + c

    def mine(self):
        lat, lon = lax.axis_index("lat"), lax.axis_index("lon")
        return (
            lon % self.c,
            lon // self.c % self.x,
            lat % self.y_high * self.y_low + lon // (self.c * self.x),
        )

    def move(self, array, to):
        every = itertools.product(range(self.z), range(self.y), range(self.x), range(self.c))
        pairs = [(self.index(*at), self.index(*to(*at))) for at in every]
        return lax.ppermute(array, ("lat", "lon"), pairs)

    def by_c(self, array):
        return self.move(array, lambda z, y, x, c: (z, y, x, 1 - c))

    def by_x(self, array, k):
        return self.move(array, lambda z, y, x, c: (z, y, (x + k) % self.x, c))

    def by_y(self, array, k):
        return self.move(array, lambda z, y, x, c: (z, (y + k) % self.y, x, c))

    def by_z(self, array, bits):
        return self.move(array, lambda z, y, x, c: (z ^ bits, y, x, c))


def small_call(kernel, outs, name, *args):
    return pl.pallas_call(
        kernel,
        out_shape=outs,
        compiler_params=pltpu.CompilerParams(vmem_limit_bytes=32 * MIB),
        name=name,
    )(*args)


def total_over_devices(places, keep, send, ahead):
    shape = keep.shape[1:]
    bf = functools.partial(jax.ShapeDtypeStruct, dtype=jnp.bfloat16)
    got = places.by_c(send)
    own = jax.ShapeDtypeStruct((places.y, *shape), jnp.float32)
    own, *sends = small_call(first_add_kernel, (own,) + (bf((places.y, *shape)),) * (places.x - 1), "add_c", keep, got)
    got = [places.by_x(part, k + 1) for k, part in enumerate(sends)]
    nxt = jax.ShapeDtypeStruct((1, *shape), jnp.float32)
    own, *sends = pl.pallas_call(
        functools.partial(next_add_kernel, len(got), 1),
        out_shape=(nxt,) + (bf((1, *shape)),) * (places.y - 1),
        in_specs=[whole()] * (1 + len(got)) + [pl.BlockSpec(memory_space=pl.ANY)],
        compiler_params=pltpu.CompilerParams(vmem_limit_bytes=16 * MIB),
        name="add_x",
    )(own, *got, ahead)
    got = [places.by_y(part, k + 1) for k, part in enumerate(sends)]
    (mine,) = small_call(functools.partial(next_add_kernel, len(got), 0), (bf((1, *shape)),), "add_y", own, *got)
    for bits in {1: (), 2: (1,), 4: (1, 3), 8: (1, 2, 6)}[places.z]:
        other = places.by_z(mine, bits)
        mine = (mine.astype(jnp.float32) + other.astype(jnp.float32)).astype(jnp.bfloat16)
    mine = jnp.concatenate([mine] + [places.by_y(mine, -k) for k in range(1, places.y)], 0)
    mine = jnp.concatenate([mine] + [places.by_x(mine, -k) for k in range(1, places.x)], 0)
    return mine, places.by_c(mine)


def ring(array, lat, lon):
    n_lat, n_lon = lax.axis_size("lat"), lax.axis_size("lon")
    pairs = [
        (i * n_lon + j, (i + lat) % n_lat * n_lon + (j + lon) % n_lon) for i in range(n_lat) for j in range(n_lon)
    ]
    return lax.ppermute(array, ("lat", "lon"), pairs)


def local(*args):
    near = WINDOW // 2
    return lax.cond(
        args[3][0] >= WINDOW - near, functools.partial(layer, near), functools.partial(layer, WINDOW), *args
    )


def layer(n_top, saved_state, cotangent, row_mask, shifts, norm_gain, w_qkv, w_out, bias_table):
    n_rows, n_cols, n_chan = saved_state.shape
    n_head = bias_table.shape[0]
    n_proj = w_qkv.shape[1]
    n_tok = n_rows // 2 * n_cols
    places = Places()
    counts = (places.c, places.x, places.y)
    bf, f32 = jnp.bfloat16, jnp.float32

    smem = pl.BlockSpec(memory_space=pltpu.SMEM)
    tile = functools.partial(jax.ShapeDtypeStruct, dtype=bf)
    side, top, corner = pl.pallas_call(
        functools.partial(pack_kernel, n_top),
        out_shape=(
            tile((2, n_rows, WINDOW, n_chan)),
            tile((2, n_top, n_cols, n_chan)),
            tile((3, WINDOW, WINDOW, n_chan)),
        ),
        in_specs=[whole(), whole(), smem],
        compiler_params=pltpu.CompilerParams(vmem_limit_bytes=8 * MIB),
        name="pack",
    )(saved_state, cotangent, row_mask)
    side = ring(side, 0, 1)
    top = ring(top, 1, 0)
    corner = ring(corner, 1, 1)
    at = jnp.stack(places.mine()).astype(jnp.int32)
    gain = norm_gain.reshape(1, n_chan)
    bias, w_t = pl.pallas_call(
        prepare_kernel,
        out_shape=(jax.ShapeDtypeStruct((n_head, CELLS, LANES), f32), tile((n_proj, n_chan))),
        compiler_params=pltpu.CompilerParams(vmem_limit_bytes=16 * MIB),
        cost_estimate=pl.CostEstimate(flops=10**9, bytes_accessed=4 * MIB, transcendentals=0),
        name="prepare",
    )(bias_table, w_qkv)

    work = [
        pltpu.VMEM((n_tok, n_chan), f32),
        pltpu.VMEM((n_tok, n_chan), f32),
        pltpu.VMEM((n_proj, n_tok), bf),
        pltpu.VMEM((n_tok, 2 * n_chan), bf),
        pltpu.VMEM((n_chan, n_tok), bf),
    ]
    meta_inner = jnp.concatenate([shifts, at, jnp.zeros((WINDOW,), jnp.int32), row_mask])
    x_in, go_in, nrm_in, mix_in, gp_in, bsum_in = pl.pallas_call(
        functools.partial(inner_kernel, n_head),
        out_shape=(
            tile((n_tok, n_chan)),
            tile((n_tok, n_chan)),
            tile((n_chan, n_tok)),
            tile((n_chan, n_tok)),
            tile((n_proj, n_tok)),
            jax.ShapeDtypeStruct((n_head, CELLS, LANES), f32),
        ),
        in_specs=[smem] + [whole()] * 8,
        scratch_shapes=work,
        compiler_params=pltpu.CompilerParams(vmem_limit_bytes=24 * MIB),
        cost_estimate=pl.CostEstimate(flops=8 * 10**9, bytes_accessed=16 * MIB, transcendentals=2**19),
        name="inner",
    )(meta_inner, saved_state, cotangent, side, bias, gain, w_t, w_qkv, w_out)

    above = jnp.where(lax.axis_index("lat") > 0, corner[2, :, 0, 0].astype(jnp.int32), 0)
    meta = jnp.concatenate([shifts, at, above, row_mask])
    width = n_proj + n_chan + LANES
    rows = n_chan // math.prod(counts)
    half = math.prod(counts) // 2
    x_out, gp_out, keep, send = pl.pallas_call(
        functools.partial(outer_kernel, n_head, counts),
        out_shape=(
            tile((n_tok, n_chan)),
            tile((n_proj, n_tok)),
            jax.ShapeDtypeStruct((half, rows, width), f32),
            tile((half, rows, width)),
        ),
        in_specs=[smem] + [whole()] * 15,
        scratch_shapes=[
            pltpu.VMEM((n_tok, n_chan), bf),
            pltpu.VMEM((n_chan, n_tok), bf),
            pltpu.VMEM((n_chan, n_tok), bf),
            pltpu.VMEM((n_head, CELLS, LANES), f32),
            *work,
            pltpu.VMEM((n_chan, width), f32),
            pltpu.VMEM((n_head * CELLS, LANES), f32),
            pltpu.VMEM((n_head * CELLS, LANES), f32),
        ],
        compiler_params=pltpu.CompilerParams(vmem_limit_bytes=36 * MIB),
        cost_estimate=pl.CostEstimate(flops=10**10, bytes_accessed=24 * MIB, transcendentals=2**19),
        name="outer",
    )(meta, saved_state, cotangent, side, top, corner, bias, gain, w_t, w_qkv, w_out, go_in, nrm_in, mix_in, gp_in, bsum_in)

    base, top_grad, side_grad = pl.pallas_call(
        cells_kernel,
        out_shape=(
            tile((n_rows, n_cols, n_chan)),
            tile((n_top, n_cols + WINDOW, n_chan)),
            tile((n_rows, WINDOW, n_chan)),
        ),
        in_specs=[smem] + [whole()] * 7,
        scratch_shapes=[pltpu.VMEM((n_rows + WINDOW, n_cols + WINDOW, n_chan), f32)],
        compiler_params=pltpu.CompilerParams(vmem_limit_bytes=40 * MIB),
        cost_estimate=pl.CostEstimate(flops=16 * 10**8, bytes_accessed=12 * MIB, transcendentals=0),
        name="cells",
    )(meta, x_in, x_out, gp_in, gp_out, cotangent, gain, w_qkv)
    mine, other = total_over_devices(places, keep, send, side_grad)
    top_grad = ring(top_grad, -1, 0)
    side_grad = jnp.concatenate([side_grad[:-n_top], side_grad[-n_top:] + top_grad[:, :WINDOW]], 0)
    side_grad = ring(side_grad, 0, -1)
    edge = jnp.pad(top_grad[:, WINDOW:], ((n_rows - n_top, 0), (0, 0), (0, 0)))
    edge = edge + jnp.pad(side_grad, ((0, 0), (n_cols - WINDOW, 0), (0, 0)))
    state_grad = (base.astype(f32) + edge.astype(f32)).astype(bf)

    factor = 1.0 / math.sqrt(n_rows * places.n_lat * n_cols * places.n_lon)
    qkv_grad, out_grad, small = pl.pallas_call(
        functools.partial(unpack_kernel, counts, n_proj, factor),
        out_shape=(
            jax.ShapeDtypeStruct((n_chan, n_proj), f32),
            jax.ShapeDtypeStruct((n_chan, n_chan), f32),
            jax.ShapeDtypeStruct((n_chan, LANES), f32),
        ),
        in_specs=[smem] + [whole()] * 2,
        compiler_params=pltpu.CompilerParams(vmem_limit_bytes=32 * MIB),
        name="unpack",
    )(meta_inner, mine, other)
    bias_grad = jnp.concatenate([small[:n_head], small[n_head : 2 * n_head]], 1).reshape(n_head, 16, 16)
    span = 2 * WINDOW - 1
    return state_grad, qkv_grad, out_grad, small[:, LANES - 1], bias_grad[:, :span, :span].reshape(n_head, -1)


def solution(mesh):
    return jax.shard_map(
        local,
        mesh=mesh,
        in_specs=(P("lat", "lon", None), P("lat", "lon", None), P("lat"), P(), P(), P(), P(), P()),
        out_specs=(P("lat", "lon", None), P(), P(), P(), P()),
        check_vma=False,
    )
```

```python
import functools
import itertools
import math

import jax
import jax.numpy as jnp
from jax import lax
from jax.experimental import pallas as pl
from jax.experimental.pallas import tpu as pltpu
from jax.sharding import PartitionSpec as P

EPSILON = 1e-05


NT = (((1,), (1,)), ((), ()))
NN = (((1,), (0,)), ((), ()))
LANES = 128
WINDOW = 8
CELLS = WINDOW * WINDOW
TOKENS = 256
MIB = 1024 * 1024


def dot(a, b, dims=NN):
    return lax.dot_general(a, b, dims, preferred_element_type=jnp.float32)


def whole(*_):
    return pl.BlockSpec(memory_space=pltpu.VMEM)


def norm_stats(x):
    cen = x - jnp.mean(x, -1, keepdims=True)
    inv = lax.rsqrt(jnp.mean(cen * cen, -1, keepdims=True) + EPSILON)
    return cen * inv, inv


def project_chunk(n_chan, scale, gain, wt_ref, w_ref, wo_ref, xf, go_ref, nrm_t, proj_t, kv, gm_t, base):
    rows = slice(base, base + TOKENS)
    x_hat, _ = norm_stats(xf[rows])
    normed_f = x_hat * gain
    normed = normed_f.astype(jnp.bfloat16)
    nrm_t[:, rows] = normed_f.T.astype(jnp.bfloat16)
    proj_t[:n_chan, rows] = (dot(wt_ref[:n_chan], normed, NT) * scale).astype(jnp.bfloat16)
    proj_t[n_chan:, rows] = dot(wt_ref[n_chan:], normed, NT).astype(jnp.bfloat16)
    kv[rows] = dot(normed, w_ref[:, n_chan:]).astype(jnp.bfloat16)
    gm_t[:, rows] = dot(wo_ref[...], go_ref[rows], NT).astype(jnp.bfloat16)


def block_diag(block, step):
    blank = jnp.zeros((step, block.shape[1]), block.dtype)
    count = block.shape[0] // step
    columns = []
    for h in range(count):
        parts = [blank] * count
        parts[h] = block[h * step : (h + 1) * step]
        columns.append(jnp.concatenate(parts, 0))
    return jnp.concatenate(columns, 1)


def attention_unit(n_chan, dim, scale, bias_ref, mask, proj_t, kv, gm_t, mix_t, gp_t, bsum_ref, pair, group):
    lanes = pl.ds(pl.multiple_of(pair * LANES, LANES), LANES)
    c0 = pl.multiple_of(group * LANES, LANES)
    q_t = proj_t[pl.ds(c0, LANES), lanes]
    k_t = proj_t[pl.ds(n_chan + c0, LANES), lanes]
    v_t = proj_t[pl.ds(2 * n_chan + c0, LANES), lanes]
    g_t = gm_t[pl.ds(c0, LANES), lanes]
    k_tok = kv[lanes, pl.ds(c0, LANES)]
    v_tok = kv[lanes, pl.ds(n_chan + c0, LANES)]
    scores = dot(k_tok, block_diag(q_t, dim))
    grads = dot(v_tok, block_diag(g_t, dim))
    first = lax.broadcasted_iota(jnp.int32, (CELLS, LANES), 1) < CELLS
    heads = LANES // dim
    mixed, dq, dk, dv = [], [], [], []
    for h in range(heads):
        cut = slice(h * LANES, (h + 1) * LANES)
        rows = slice(h * dim, (h + 1) * dim)
        head = group * heads + h
        s = jnp.where(first, scores[:CELLS, cut], scores[CELLS:, cut]) + bias_ref[head] + mask
        e = jnp.exp(s - jnp.max(s, 0, keepdims=True))
        a = e * (1.0 / jnp.sum(e, 0, keepdims=True))
        d = jnp.where(first, grads[:CELLS, cut], grads[CELLS:, cut])
        ad = a * d
        ds = ad - a * jnp.sum(ad, 0, keepdims=True)
        bsum_ref[head] += ds
        zero = jnp.zeros_like(a)
        a2 = jnp.concatenate([jnp.where(first, a, zero), jnp.where(first, zero, a)], 0).astype(jnp.bfloat16)
        ds2 = jnp.concatenate([jnp.where(first, ds, zero), jnp.where(first, zero, ds)], 0).astype(jnp.bfloat16)
        mixed.append(dot(v_t[rows], a2))
        dv.append(dot(g_t[rows], a2, NT))
        dq.append(dot(k_t[rows], ds2) * scale)
        dk.append(dot(q_t[rows], ds2, NT))
    mix_t[pl.ds(c0, LANES), lanes] = jnp.concatenate(mixed, 0).astype(jnp.bfloat16)
    gp_t[pl.ds(c0, LANES), lanes] = jnp.concatenate(dq, 0).astype(jnp.bfloat16)
    gp_t[pl.ds(n_chan + c0, LANES), lanes] = jnp.concatenate(dk, 0).astype(jnp.bfloat16)
    gp_t[pl.ds(2 * n_chan + c0, LANES), lanes] = jnp.concatenate(dv, 0).astype(jnp.bfloat16)


def place_row(side, own, shift, out, r, live=None):
    line = jnp.concatenate([side.astype(jnp.float32), own.astype(jnp.float32)], 0).reshape(-1, WINDOW, own.shape[1])
    if live is not None:
        line = line * live
    line = pltpu.roll(line, WINDOW - shift, 1)
    head = lax.broadcasted_iota(jnp.int32, line.shape[1:], 0) < WINDOW - shift
    for w in range(line.shape[0] - 1):
        start = w * CELLS + r * WINDOW
        out[start : start + WINDOW] = jnp.where(head, line[w], line[w + 1])


def window_row(n_head, xf, cf, live, gain_ref, wt_ref, w_ref, wo_ref, bias_ref,
               x_out, go_ref, nrm_t, mix_t, gp_t, bsum_ref, proj_t, kv, gm_t):
    n_tok, n_chan = xf.shape
    dim = n_chan // n_head
    scale = dim ** (-0.5)
    x_out[...] = xf[...].astype(jnp.bfloat16)
    go_ref[...] = cf[...].astype(jnp.bfloat16)
    for base in range(0, n_tok, TOKENS):
        project_chunk(n_chan, scale, gain_ref[...], wt_ref, w_ref, wo_ref, xf, go_ref, nrm_t, proj_t, kv, gm_t, base)
    mask = jnp.concatenate([(live[r][:, :LANES] - 1.0) * 1e30 for r in range(WINDOW)], 0)
    groups = n_chan // LANES

    @pl.loop(0, n_tok // LANES * groups)
    def _(unit):
        attention_unit(n_chan, dim, scale, bias_ref, mask, proj_t, kv, gm_t, mix_t, gp_t, bsum_ref,
                       unit // groups, unit % groups)


def weight_sums(sums, nrm_t, gp_t, mix_t, go_ref, more):
    n_proj, n_chan = gp_t.shape[0], nrm_t.shape[0]
    for base in range(0, n_proj + n_chan, TOKENS):
        cols = slice(base, base + TOKENS)
        if base < n_proj:
            part = dot(nrm_t[...], gp_t[cols], NT)
        else:
            part = dot(mix_t[...], go_ref[:, base - n_proj : base - n_proj + TOKENS])
        sums[:, cols] = part if more is None else part + more[:, cols]


def inner_kernel(n_head, meta, x_ref, cot_ref, side_ref, bias_ref, gain_ref, wt_ref, w_ref, wo_ref,
                 x_out, gp_t, sums_ref, bsum_ref, go_ref, nrm_t, mix_t, xf, cf, proj_t, kv, gm_t):
    lat, lon = meta[0], meta[1]
    live = []
    for r in range(WINDOW):
        live.append(jnp.full((WINDOW, x_ref.shape[2]), meta[6 + lat + r].astype(jnp.float32)))
        place_row(side_ref[0, lat + r], x_ref[lat + r], lon, xf, r)
        place_row(side_ref[1, lat + r], cot_ref[lat + r], lon, cf, r, live[r])
    bsum_ref[...] = jnp.zeros_like(bsum_ref)
    window_row(n_head, xf, cf, live, gain_ref, wt_ref, w_ref, wo_ref, bias_ref,
               x_out, go_ref, nrm_t, mix_t, gp_t, bsum_ref, proj_t, kv, gm_t)
    weight_sums(sums_ref, nrm_t, gp_t, mix_t, go_ref, None)


def outer_kernel(n_head, counts, meta, x_ref, cot_ref, side_ref, top_ref, corner_ref, bias_ref, gain_ref, wt_ref, w_ref, wo_ref,
                 sums_in, bsum_in,
                 x_out, gp_t, keep_ref, send_ref,
                 go_ref, nrm_t, mix_t, bsum_ref, xf, cf, proj_t, kv, gm_t, sums, spread_a, spread_b):
    n_chan = gain_ref.shape[1]
    n_top = top_ref.shape[1]
    lat, lon = meta[0], meta[1]
    live = []
    for r in range(WINDOW):
        e = lat + r
        above = e < WINDOW
        up = jnp.clip(e - (WINDOW - n_top), 0, n_top - 1)
        own = jnp.maximum(e - WINDOW, 0)
        row_live = jnp.full((WINDOW, n_chan), meta[6 + own].astype(jnp.float32))
        up_live = corner_ref[2, jnp.minimum(e, WINDOW - 1)].astype(jnp.float32) * meta[5].astype(jnp.float32)
        live.append(jnp.where(above, up_live, row_live))
        side = [jnp.where(above, corner_ref[k, up], side_ref[k, own]) for k in range(2)]
        place_row(side[0], jnp.where(above, top_ref[0, up], x_ref[own]), lon, xf, r)
        place_row(side[1], jnp.where(above, top_ref[1, up], cot_ref[own]), lon, cf, r, live[r])
    bsum_ref[...] = bsum_in[...]
    window_row(n_head, xf, cf, live, gain_ref, wt_ref, w_ref, wo_ref, bias_ref,
               x_out, go_ref, nrm_t, mix_t, gp_t, bsum_ref, proj_t, kv, gm_t)

    n_proj = 3 * n_chan
    weight_sums(sums, nrm_t, gp_t, mix_t, go_ref, sums_in)
    gain_sum = jnp.sum(sums[:, :n_proj] * w_ref[...].astype(jnp.float32), 1, keepdims=True)

    width = 2 * LANES
    cell = lax.broadcasted_iota(jnp.int32, (LANES, width), 0) % CELLS
    lane = lax.broadcasted_iota(jnp.int32, (LANES, width), 1)
    place = (cell // WINDOW) * 16 + cell % WINDOW + 119
    onehot = (lane == place).astype(jnp.float32).astype(jnp.bfloat16)
    flat = bsum_ref[...].reshape(n_head * CELLS, LANES)
    high = flat.astype(jnp.bfloat16)
    low = (flat - high.astype(jnp.float32)).astype(jnp.bfloat16)
    spread = dot(high, onehot) + dot(low, onehot)
    spread_a[...] = spread[:, :LANES]
    spread_b[...] = spread[:, LANES:]
    bias_sum = jnp.zeros((n_head, width), jnp.float32)
    for j in range(CELLS):
        row = jnp.concatenate([ref[pl.ds(j, n_head, stride=CELLS), :] for ref in (spread_a, spread_b)], 1)
        by = (j // WINDOW) * 16 + j % WINDOW
        bias_sum += pltpu.roll(row, width - by, 1) if by else row
    tail = lax.broadcasted_iota(jnp.int32, (n_chan, LANES), 1) == LANES - 1
    bias_rows = jnp.concatenate(
        [bias_sum[:, :LANES], bias_sum[:, LANES:], jnp.zeros((n_chan - 2 * n_head, LANES), jnp.float32)], 0
    )
    sums[:, n_proj + n_chan :] = jnp.where(tail, gain_sum * (1.0 / gain_col(gain_ref)), bias_rows)

    n_c, n_x, n_y = counts
    rows = n_chan // (n_c * n_x * n_y)
    for c in range(n_c):
        for x in range(n_x):
            for y in range(n_y):
                chunk = sums[((c * n_x + x) * n_y + y) * rows : ((c * n_x + x) * n_y + y + 1) * rows]
                at = lax.rem(x - meta[3] + n_x, n_x) * n_y + lax.rem(y - meta[4] + n_y, n_y)

                @pl.when(meta[2] == c)
                def _():
                    keep_ref[at] = chunk

                @pl.when(meta[2] != c)
                def _():
                    send_ref[at] = chunk.astype(jnp.bfloat16)


def gain_col(gain_ref):
    n_chan = gain_ref.shape[1]
    return jnp.broadcast_to(gain_ref[...], (LANES, n_chan)).T[:, :1]


def cells_kernel(meta, xa_ref, xb_ref, gpa_ref, gpb_ref, cot_ref, gain_ref, w_ref, base_ref, top_ref, side_ref, corner_ref, ext):
    n_rows, n_cols, n_chan = cot_ref.shape
    lat, lon = meta[0], meta[1]
    ext[...] = jnp.zeros_like(ext)
    for part, (x_ref, gp_t) in enumerate(((xb_ref, gpb_ref), (xa_ref, gpa_ref))):
        n_tok = x_ref.shape[0]
        cells = []
        for base in range(0, n_tok, TOKENS):
            rows = slice(base, base + TOKENS)
            x_hat, inv = norm_stats(x_ref[rows].astype(jnp.float32))
            g = dot(w_ref[...], gp_t[:, rows]).T * gain_ref[...]
            cells.append(inv * (g - jnp.mean(g, -1, keepdims=True) - x_hat * jnp.mean(g * x_hat, -1, keepdims=True)))
        blank = jnp.zeros((1, WINDOW, n_chan), jnp.float32)
        head = lax.broadcasted_iota(jnp.int32, (WINDOW, n_chan), 0) < lon
        for r in range(WINDOW):
            row = jnp.stack(
                [
                    cells[w * CELLS // TOKENS][w * CELLS % TOKENS + r * WINDOW :][:WINDOW]
                    for w in range(n_tok // CELLS)
                ],
                0,
            )
            row = jnp.concatenate([blank, pltpu.roll(row, lon, 1), blank], 0)
            for t in range(row.shape[0] - 1):
                ext[lat + part * WINDOW + r, t * WINDOW : (t + 1) * WINDOW, :] = jnp.where(head, row[t], row[t + 1])
    for r in range(n_rows):
        base_ref[r] = (cot_ref[r].astype(jnp.float32) + ext[WINDOW + r, WINDOW:]).astype(jnp.bfloat16)
        side_ref[r] = ext[WINDOW + r, :WINDOW].astype(jnp.bfloat16)
    n_top = top_ref.shape[0]
    for r in range(n_top):
        top_ref[r] = ext[WINDOW - n_top + r, WINDOW:].astype(jnp.bfloat16)
        corner_ref[r] = ext[WINDOW - n_top + r, :WINDOW].astype(jnp.bfloat16)


def prepare_kernel(bias_ref, w_ref, full_ref, wt_ref):
    n_head, n_gap = bias_ref.shape
    span = 2 * WINDOW - 1
    width = 2 * LANES
    lane = lax.broadcasted_iota(jnp.int32, (width, LANES), 0)
    cell = lax.broadcasted_iota(jnp.int32, (width, LANES), 1) % CELLS
    place = cell // WINDOW * span + cell % WINDOW + n_gap // 2
    onehot = (lane == place).astype(jnp.float32).astype(jnp.bfloat16)
    table = jnp.concatenate([bias_ref[...], jnp.zeros((n_head, width - n_gap), jnp.float32)], 1)
    for h in range(n_head):
        line = jnp.broadcast_to(table[h : h + 1], (WINDOW, width))
        rows = [pltpu.roll(line, r * span, 1, stride=1, stride_axis=0) for r in range(WINDOW)]
        rest = jnp.concatenate(rows, 0)
        total = jnp.zeros((CELLS, LANES), jnp.float32)
        for _ in range(3):
            part = rest.astype(jnp.bfloat16)
            total += dot(part, onehot)
            rest = rest - part.astype(jnp.float32)
        full_ref[h] = total
    wt_ref[...] = w_ref[...].T


def pack_kernel(n_top, x_ref, cot_ref, mask, side_ref, top_ref, corner_ref):
    n_rows, n_cols, n_chan = x_ref.shape
    for k, ref in enumerate((x_ref, cot_ref)):
        for r in range(n_rows):
            edge = ref[r, n_cols - 2 * WINDOW :, :][WINDOW:]
            side_ref[k, r] = edge
            if r >= n_rows - n_top:
                top_ref[k, r - n_rows + n_top] = ref[r]
                corner_ref[k, r - n_rows + n_top] = edge
    for r in range(WINDOW):
        live = mask[n_rows - WINDOW + r].astype(jnp.float32)
        corner_ref[2, r] = jnp.broadcast_to(live, (WINDOW, n_chan)).astype(jnp.bfloat16)
    for k in range(2):
        for r in range(n_top, WINDOW):
            corner_ref[k, r] = jnp.zeros((WINDOW, n_chan), jnp.bfloat16)


def first_add_kernel(keep_ref, got_ref, own_ref, *send_refs):
    size = own_ref.shape[0]
    for k in range(len(send_refs) + 1):
        cut = slice(k * size, (k + 1) * size)
        total = keep_ref[cut] + got_ref[cut].astype(jnp.float32)
        if k:
            send_refs[k - 1][...] = total.astype(jnp.bfloat16)
        else:
            own_ref[...] = total


def next_add_kernel(n_got, n_more, own_ref, *refs):
    got, (out_ref, *send_refs) = refs[:n_got], refs[n_got + n_more :]
    size = out_ref.shape[0]
    for k in range(len(send_refs) + 1):
        cut = slice(k * size, (k + 1) * size)
        total = own_ref[cut]
        for ref in got:
            total = total + ref[cut].astype(jnp.float32)
        if k:
            send_refs[k - 1][...] = total.astype(jnp.bfloat16)
        else:
            out_ref[...] = total.astype(out_ref.dtype)


def pair_add_kernel(a_ref, b_ref, *refs):
    refs[-1][...] = (a_ref[...].astype(jnp.float32) + b_ref[...].astype(jnp.float32)).astype(jnp.bfloat16)


def unpack_kernel(counts, n_proj, factor, meta, *refs):
    n_c, n_x, n_y = counts
    mine, other = refs[:n_x], refs[n_x : 2 * n_x]
    qkv_ref, out_ref, gain_ref, bias_ref, small = refs[2 * n_x :]
    rows = mine[0].shape[1]
    n_chan = out_ref.shape[1]
    for half in range(2):
        c = meta[2] if half == 0 else 1 - meta[2]
        for k, ref in enumerate(other if half else mine):
            x = lax.rem(meta[3] + k, n_x)
            for j in range(n_y):
                y = lax.rem(meta[4] + j, n_y)
                chunk = ref[j].astype(jnp.float32) * factor
                to = pl.ds(pl.multiple_of(((c * n_x + x) * n_y + y) * rows, rows), rows)
                qkv_ref[to] = chunk[:, :n_proj]
                out_ref[to] = chunk[:, n_proj : n_proj + n_chan]
                small[to] = chunk[:, n_proj + n_chan :]
    gain_ref[...] = small[...].T[LANES - 1 :]
    n_head, n_gap = bias_ref.shape
    span = 2 * WINDOW - 1
    wide = jnp.concatenate([small[:n_head], small[n_head : 2 * n_head]], 1)
    lane = lax.broadcasted_iota(jnp.int32, wide.shape, 1)
    bias = jnp.zeros_like(wide)
    for k in range(span):
        moved = pltpu.roll(wide, 2 * LANES - k, 1) if k else wide
        bias = jnp.where((lane >= k * span) & (lane < (k + 1) * span), moved, bias)
    bias_ref[...] = bias[:, :n_gap]


class Places:
    def __init__(self):
        self.n_lat, self.n_lon = lax.axis_size("lat"), lax.axis_size("lon")
        self.c = 2
        self.x = min(4, self.n_lon // self.c)
        self.y_low = self.n_lon // (self.c * self.x)
        self.y_high = 2
        self.y = self.y_low * self.y_high
        self.z = self.n_lat // self.y_high

    def index(self, z, y, x, c):
        high, low = divmod(y, self.y_low)
        return (z * self.y_high + high) * self.n_lon + (low * self.x + x) * self.c + c

    def mine(self):
        lat, lon = lax.axis_index("lat"), lax.axis_index("lon")
        return (
            lon % self.c,
            lon // self.c % self.x,
            lat % self.y_high * self.y_low + lon // (self.c * self.x),
        )

    def move(self, array, to):
        every = itertools.product(range(self.z), range(self.y), range(self.x), range(self.c))
        pairs = [(self.index(*at), self.index(*to(*at))) for at in every]
        return lax.ppermute(array, ("lat", "lon"), pairs)

    def by_c(self, array):
        return self.move(array, lambda z, y, x, c: (z, y, x, 1 - c))

    def by_x(self, array, k):
        return self.move(array, lambda z, y, x, c: (z, y, (x + k) % self.x, c))

    def by_y(self, array, k):
        return self.move(array, lambda z, y, x, c: (z, (y + k) % self.y, x, c))

    def by_z(self, array, bits):
        return self.move(array, lambda z, y, x, c: (z ^ bits, y, x, c))


def small_call(kernel, outs, name, *args):
    return pl.pallas_call(
        kernel,
        out_shape=outs,
        compiler_params=pltpu.CompilerParams(vmem_limit_bytes=32 * MIB),
        name=name,
    )(*args)


def total_over_devices(places, keep, send, ahead, behind):
    shape = keep.shape[1:]
    bf = functools.partial(jax.ShapeDtypeStruct, dtype=jnp.bfloat16)
    got = places.by_c(send)
    own = jax.ShapeDtypeStruct((places.y, *shape), jnp.float32)
    own, *sends = small_call(first_add_kernel, (own,) + (bf((places.y, *shape)),) * (places.x - 1), "add_c", keep, got)
    got = [places.by_x(part, k + 1) for k, part in enumerate(sends)]
    nxt = jax.ShapeDtypeStruct((1, *shape), jnp.float32)
    own, *sends = pl.pallas_call(
        functools.partial(next_add_kernel, len(got), 1),
        out_shape=(nxt,) + (bf((1, *shape)),) * (places.y - 1),
        in_specs=[whole()] * (1 + len(got)) + [pl.BlockSpec(memory_space=pl.ANY)],
        compiler_params=pltpu.CompilerParams(vmem_limit_bytes=16 * MIB),
        name="add_x",
    )(own, *got, ahead)
    got = [places.by_y(part, k + 1) for k, part in enumerate(sends)]
    (mine,) = small_call(functools.partial(next_add_kernel, len(got), 0), (bf((1, *shape)),), "add_y", own, *got)
    for bits in {1: (), 2: (1,), 4: (1, 3), 8: (1, 2, 6)}[places.z]:
        other = places.by_z(mine, bits)
        last = bits == 6
        mine = pl.pallas_call(
            pair_add_kernel,
            out_shape=bf((1, *shape)),
            in_specs=[whole()] * 2 + [pl.BlockSpec(memory_space=pl.ANY)] * (len(behind) if last else 0),
            compiler_params=pltpu.CompilerParams(vmem_limit_bytes=4 * MIB),
            name="add_z",
        )(mine, other, *(behind if last else ()))
    mine = jnp.concatenate([mine] + [places.by_y(mine, -k) for k in range(1, places.y)], 0)
    mine = [mine] + [places.by_x(mine, -k) for k in range(1, places.x)]
    return mine, [places.by_c(part) for part in mine]


def ring(array, lat, lon):
    n_lat, n_lon = lax.axis_size("lat"), lax.axis_size("lon")
    pairs = [
        (i * n_lon + j, (i + lat) % n_lat * n_lon + (j + lon) % n_lon) for i in range(n_lat) for j in range(n_lon)
    ]
    return lax.ppermute(array, ("lat", "lon"), pairs)


def local(saved_state, cotangent, row_mask, shifts, norm_gain, w_qkv, w_out, bias_table):
    n_rows, n_cols, n_chan = saved_state.shape
    n_head = bias_table.shape[0]
    n_proj = w_qkv.shape[1]
    n_tok = n_rows // 2 * n_cols
    n_top = WINDOW - 1
    places = Places()
    counts = (places.c, places.x, places.y)
    bf, f32 = jnp.bfloat16, jnp.float32

    smem = pl.BlockSpec(memory_space=pltpu.SMEM)
    tile = functools.partial(jax.ShapeDtypeStruct, dtype=bf)
    side, top, corner = pl.pallas_call(
        functools.partial(pack_kernel, n_top),
        out_shape=(
            tile((2, n_rows, WINDOW, n_chan)),
            tile((2, n_top, n_cols, n_chan)),
            tile((3, WINDOW, WINDOW, n_chan)),
        ),
        in_specs=[whole(), whole(), smem],
        compiler_params=pltpu.CompilerParams(vmem_limit_bytes=8 * MIB),
        name="pack",
    )(saved_state, cotangent, row_mask)
    side = ring(side, 0, 1)
    top = ring(top, 1, 0)
    corner = ring(corner, 1, 1)
    at = jnp.stack(places.mine()).astype(jnp.int32)
    gain = norm_gain.reshape(1, n_chan)
    bias, w_t = pl.pallas_call(
        prepare_kernel,
        out_shape=(jax.ShapeDtypeStruct((n_head, CELLS, LANES), f32), tile((n_proj, n_chan))),
        compiler_params=pltpu.CompilerParams(vmem_limit_bytes=16 * MIB),
        cost_estimate=pl.CostEstimate(flops=10**9, bytes_accessed=4 * MIB, transcendentals=0),
        name="prepare",
    )(bias_table, w_qkv)

    keep_back = [
        pltpu.VMEM((n_tok, n_chan), bf),
        pltpu.VMEM((n_chan, n_tok), bf),
        pltpu.VMEM((n_chan, n_tok), bf),
    ]
    work = [
        pltpu.VMEM((n_tok, n_chan), f32),
        pltpu.VMEM((n_tok, n_chan), f32),
        pltpu.VMEM((n_proj, n_tok), bf),
        pltpu.VMEM((n_tok, 2 * n_chan), bf),
        pltpu.VMEM((n_chan, n_tok), bf),
    ]
    below = jnp.minimum(lax.axis_index("lat"), 1).astype(jnp.int32).reshape(1)
    meta = jnp.concatenate([shifts, at, below, row_mask])
    x_in, gp_in, sums_in, bsum_in = pl.pallas_call(
        functools.partial(inner_kernel, n_head),
        out_shape=(
            tile((n_tok, n_chan)),
            tile((n_proj, n_tok)),
            jax.ShapeDtypeStruct((n_chan, n_proj + n_chan), f32),
            jax.ShapeDtypeStruct((n_head, CELLS, LANES), f32),
        ),
        in_specs=[smem] + [whole()] * 8,
        scratch_shapes=keep_back + work,
        compiler_params=pltpu.CompilerParams(vmem_limit_bytes=24 * MIB),
        cost_estimate=pl.CostEstimate(flops=8 * 10**9, bytes_accessed=16 * MIB, transcendentals=2**19),
        name="inner",
    )(meta, saved_state, cotangent, side, bias, gain, w_t, w_qkv, w_out)

    width = n_proj + n_chan + LANES
    rows = n_chan // math.prod(counts)
    half = math.prod(counts) // 2
    x_out, gp_out, keep, send = pl.pallas_call(
        functools.partial(outer_kernel, n_head, counts),
        out_shape=(
            tile((n_tok, n_chan)),
            tile((n_proj, n_tok)),
            jax.ShapeDtypeStruct((half, rows, width), f32),
            tile((half, rows, width)),
        ),
        in_specs=[smem] + [whole()] * 12,
        scratch_shapes=[
            *keep_back,
            pltpu.VMEM((n_head, CELLS, LANES), f32),
            *work,
            pltpu.VMEM((n_chan, width), f32),
            pltpu.VMEM((n_head * CELLS, LANES), f32),
            pltpu.VMEM((n_head * CELLS, LANES), f32),
        ],
        compiler_params=pltpu.CompilerParams(vmem_limit_bytes=36 * MIB),
        cost_estimate=pl.CostEstimate(flops=10**10, bytes_accessed=24 * MIB, transcendentals=2**19),
        name="outer",
    )(meta, saved_state, cotangent, side, top, corner, bias, gain, w_t, w_qkv, w_out, sums_in, bsum_in)

    base, *edges = pl.pallas_call(
        cells_kernel,
        out_shape=(
            tile((n_rows, n_cols, n_chan)),
            tile((n_top, n_cols, n_chan)),
            tile((n_rows, WINDOW, n_chan)),
            tile((n_top, WINDOW, n_chan)),
        ),
        in_specs=[smem] + [whole()] * 7,
        scratch_shapes=[pltpu.VMEM((n_rows + WINDOW, n_cols + WINDOW, n_chan), f32)],
        compiler_params=pltpu.CompilerParams(vmem_limit_bytes=40 * MIB),
        cost_estimate=pl.CostEstimate(flops=16 * 10**8, bytes_accessed=12 * MIB, transcendentals=0),
        name="cells",
    )(meta, x_in, x_out, gp_in, gp_out, cotangent, gain, w_qkv)
    top_back, side_back, corner_back = ring(edges[0], -1, 0), ring(edges[1], 0, -1), ring(edges[2], -1, -1)
    mine, other = total_over_devices(places, keep, send, edges[2], (top_back, side_back, corner_back))
    edge = jnp.pad(top_back, ((n_rows - n_top, 0), (0, 0), (0, 0)))
    edge = edge + jnp.pad(side_back, ((0, 0), (n_cols - WINDOW, 0), (0, 0)))
    edge = edge + jnp.pad(corner_back, ((n_rows - n_top, 0), (n_cols - WINDOW, 0), (0, 0)))
    state_grad = (base.astype(f32) + edge.astype(f32)).astype(bf)

    factor = 1.0 / math.sqrt(n_rows * places.n_lat * n_cols * places.n_lon)
    qkv_grad, out_grad, gain_grad, bias_grad = pl.pallas_call(
        functools.partial(unpack_kernel, counts, n_proj, factor),
        out_shape=(
            jax.ShapeDtypeStruct((n_chan, n_proj), f32),
            jax.ShapeDtypeStruct((n_chan, n_chan), f32),
            jax.ShapeDtypeStruct((1, n_chan), f32),
            jax.ShapeDtypeStruct(bias_table.shape, f32),
        ),
        in_specs=[smem] + [whole()] * (2 * places.x),
        scratch_shapes=[pltpu.VMEM((n_chan, LANES), f32)],
        compiler_params=pltpu.CompilerParams(vmem_limit_bytes=32 * MIB),
        name="unpack",
    )(meta, *mine, *other)
    return state_grad, qkv_grad, out_grad, gain_grad.reshape(n_chan), bias_grad


def solution(mesh):
    return jax.shard_map(
        local,
        mesh=mesh,
        in_specs=(P("lat", "lon", None), P("lat", "lon", None), P("lat"), P(), P(), P(), P(), P()),
        out_specs=(P("lat", "lon", None), P(), P(), P(), P()),
        check_vma=False,
    )
```

```python
import functools
import itertools
import math

import jax
import jax.numpy as jnp
from jax import lax
from jax.experimental import pallas as pl
from jax.experimental.pallas import tpu as pltpu
from jax.sharding import PartitionSpec as P

EPSILON = 1e-05


NT = (((1,), (1,)), ((), ()))
NN = (((1,), (0,)), ((), ()))
LANES = 128
WINDOW = 8
CELLS = WINDOW * WINDOW
TOKENS = 256
MIB = 1024 * 1024


def dot(a, b, dims=NN):
    return lax.dot_general(a, b, dims, preferred_element_type=jnp.float32)


def whole(*_):
    return pl.BlockSpec(memory_space=pltpu.VMEM)


def norm_stats(x):
    cen = x - jnp.mean(x, -1, keepdims=True)
    inv = lax.rsqrt(jnp.mean(cen * cen, -1, keepdims=True) + EPSILON)
    return cen * inv, inv


def project_chunk(n_chan, scale, gain, wt_ref, w_ref, wo_ref, xf, go_ref, nrm_t, proj_t, kv, gm_t, base):
    rows = slice(base, base + TOKENS)
    x_hat, _ = norm_stats(xf[rows])
    normed_f = x_hat * gain
    normed = normed_f.astype(jnp.bfloat16)
    nrm_t[:, rows] = normed_f.T.astype(jnp.bfloat16)
    proj_t[:n_chan, rows] = (dot(wt_ref[:n_chan], normed, NT) * scale).astype(jnp.bfloat16)
    proj_t[n_chan:, rows] = dot(wt_ref[n_chan:], normed, NT).astype(jnp.bfloat16)
    kv[rows] = dot(normed, w_ref[:, n_chan:]).astype(jnp.bfloat16)
    gm_t[:, rows] = dot(wo_ref[...], go_ref[rows], NT).astype(jnp.bfloat16)


def block_diag(block, step):
    blank = jnp.zeros((step, block.shape[1]), block.dtype)
    count = block.shape[0] // step
    columns = []
    for h in range(count):
        parts = [blank] * count
        parts[h] = block[h * step : (h + 1) * step]
        columns.append(jnp.concatenate(parts, 0))
    return jnp.concatenate(columns, 1)


def attention_unit(n_chan, dim, scale, bias_ref, mask, proj_t, kv, gm_t, mix_t, gp_t, bsum_ref, pair, group):
    lanes = pl.ds(pl.multiple_of(pair * LANES, LANES), LANES)
    c0 = group * LANES
    q_t = proj_t[pl.ds(c0, LANES), lanes]
    k_t = proj_t[pl.ds(n_chan + c0, LANES), lanes]
    v_t = proj_t[pl.ds(2 * n_chan + c0, LANES), lanes]
    g_t = gm_t[pl.ds(c0, LANES), lanes]
    k_tok = kv[lanes, pl.ds(c0, LANES)]
    v_tok = kv[lanes, pl.ds(n_chan + c0, LANES)]
    scores = dot(k_tok, block_diag(q_t, dim))
    grads = dot(v_tok, block_diag(g_t, dim))
    first = lax.broadcasted_iota(jnp.int32, (CELLS, LANES), 1) < CELLS
    heads = LANES // dim
    mixed, dq, dk, dv = [], [], [], []
    for h in range(heads):
        cut = slice(h * LANES, (h + 1) * LANES)
        rows = slice(h * dim, (h + 1) * dim)
        head = group * heads + h
        s = jnp.where(first, scores[:CELLS, cut], scores[CELLS:, cut]) + bias_ref[head] + mask
        e = jnp.exp(s - jnp.max(s, 0, keepdims=True))
        a = e * (1.0 / jnp.sum(e, 0, keepdims=True))
        d = jnp.where(first, grads[:CELLS, cut], grads[CELLS:, cut])
        ad = a * d
        ds = ad - a * jnp.sum(ad, 0, keepdims=True)
        bsum_ref[head] += ds
        zero = jnp.zeros_like(a)
        a2 = jnp.concatenate([jnp.where(first, a, zero), jnp.where(first, zero, a)], 0).astype(jnp.bfloat16)
        ds2 = jnp.concatenate([jnp.where(first, ds, zero), jnp.where(first, zero, ds)], 0).astype(jnp.bfloat16)
        mixed.append(dot(v_t[rows], a2))
        dv.append(dot(g_t[rows], a2, NT))
        dq.append(dot(k_t[rows], ds2) * scale)
        dk.append(dot(q_t[rows], ds2, NT))
    mix_t[pl.ds(c0, LANES), lanes] = jnp.concatenate(mixed, 0).astype(jnp.bfloat16)
    gp_t[pl.ds(c0, LANES), lanes] = jnp.concatenate(dq, 0).astype(jnp.bfloat16)
    gp_t[pl.ds(n_chan + c0, LANES), lanes] = jnp.concatenate(dk, 0).astype(jnp.bfloat16)
    gp_t[pl.ds(2 * n_chan + c0, LANES), lanes] = jnp.concatenate(dv, 0).astype(jnp.bfloat16)


def place_row(line, shift, out, r, live=None):
    line = line.astype(jnp.float32).reshape(-1, WINDOW, line.shape[1])
    if live is not None:
        line = line * live
    line = pltpu.roll(line, WINDOW - shift, 1)
    head = lax.broadcasted_iota(jnp.int32, line.shape[1:], 0) < WINDOW - shift
    for w in range(line.shape[0] - 1):
        start = w * CELLS + r * WINDOW
        out[start : start + WINDOW] = jnp.where(head, line[w], line[w + 1])


def window_row(n_head, xf, cf, live, gain_ref, wt_ref, w_ref, wo_ref, bias_ref,
               x_out, go_ref, nrm_t, mix_t, gp_t, bsum_ref, proj_t, kv, gm_t):
    n_tok, n_chan = xf.shape
    dim = n_chan // n_head
    scale = dim ** (-0.5)
    x_out[...] = xf[...].astype(jnp.bfloat16)
    go_ref[...] = cf[...].astype(jnp.bfloat16)
    for base in range(0, n_tok, TOKENS):
        project_chunk(n_chan, scale, gain_ref[...], wt_ref, w_ref, wo_ref, xf, go_ref, nrm_t, proj_t, kv, gm_t, base)
    mask = jnp.concatenate([(live[r][:, :LANES] - 1.0) * 1e30 for r in range(WINDOW)], 0)
    groups = n_chan // LANES

    @pl.loop(0, n_tok // LANES)
    def _(pair):
        for group in range(groups):
            attention_unit(n_chan, dim, scale, bias_ref, mask, proj_t, kv, gm_t, mix_t, gp_t, bsum_ref, pair, group)


def weight_sums(sums, nrm_t, gp_t, mix_t, go_ref, more):
    n_proj, n_chan = gp_t.shape[0], nrm_t.shape[0]
    for base in range(0, n_proj + n_chan, TOKENS):
        cols = slice(base, base + TOKENS)
        if base < n_proj:
            part = dot(nrm_t[...], gp_t[cols], NT)
        else:
            part = dot(mix_t[...], go_ref[:, base - n_proj : base - n_proj + TOKENS])
        sums[:, cols] = part if more is None else part + more[:, cols]


def inner_kernel(n_head, left, meta, x_ref, cot_ref, bias_ref, gain_ref, wt_ref, w_ref, wo_ref, *refs):
    if left:
        side_ref, sums_in, bsum_in, *refs = refs
    _, *refs = refs
    x_out, gp_t, sums_ref, bsum_ref, go_ref, nrm_t, mix_t, xf, cf, proj_t, kv, gm_t = refs
    lat, lon = meta[0], meta[1]
    half = x_ref.shape[1] // 2
    live = []
    for r in range(WINDOW):
        live.append(jnp.full((WINDOW, x_ref.shape[2]), meta[6 + lat + r].astype(jnp.float32)))
        for k, (grid, out) in enumerate(((x_ref, xf), (cot_ref, cf))):
            line = grid[lat + r].astype(jnp.float32)
            if left:
                line = jnp.concatenate([side_ref[k, lat + r].astype(jnp.float32), line[:half]], 0)
            else:
                line = line[half - WINDOW :]
            place_row(line, lon, out, r, live[r] if k else None)
    bsum_ref[...] = bsum_in[...] if left else jnp.zeros_like(bsum_ref)
    window_row(n_head, xf, cf, live, gain_ref, wt_ref, w_ref, wo_ref, bias_ref,
               x_out, go_ref, nrm_t, mix_t, gp_t, bsum_ref, proj_t, kv, gm_t)
    weight_sums(sums_ref, nrm_t, gp_t, mix_t, go_ref, sums_in if left else None)


def outer_kernel(n_head, counts, meta, x_ref, cot_ref, side_ref, top_x, top_c, corner_ref, bias_ref, gain_ref, wt_ref, w_ref, wo_ref,
                 sums_in, bsum_in,
                 x_out, gp_t, keep_ref, send_ref,
                 go_ref, nrm_t, mix_t, bsum_ref, xf, cf, proj_t, kv, gm_t, sums, spread_a, spread_b):
    n_chan = gain_ref.shape[1]
    n_top = top_x.shape[0]
    lat, lon = meta[0], meta[1]
    up_mask = corner_ref[0, WINDOW - 1].astype(jnp.float32) * meta[5].astype(jnp.float32)
    line_of = lax.broadcasted_iota(jnp.int32, up_mask.shape, 0)
    live = []
    for r in range(WINDOW):
        e = lat + r
        above = e < WINDOW
        up = jnp.clip(e - (WINDOW - n_top), 0, n_top - 1)
        own = jnp.maximum(e - WINDOW, 0)
        row_live = jnp.full((WINDOW, n_chan), meta[6 + own].astype(jnp.float32))
        up_live = jnp.sum(jnp.where(line_of == e, up_mask, 0.0), 0, keepdims=True)
        live.append(jnp.where(above, jnp.broadcast_to(up_live, row_live.shape), row_live))
        side = [jnp.where(above, corner_ref[k, up], side_ref[k, own]) for k in range(2)]
        for k, (top, grid, out) in enumerate(((top_x, x_ref, xf), (top_c, cot_ref, cf))):
            line = jnp.where(above, top[up], grid[own]).astype(jnp.float32)
            line = jnp.concatenate([side[k].astype(jnp.float32), line], 0)
            place_row(line, lon, out, r, live[r] if k else None)
    bsum_ref[...] = bsum_in[...]
    window_row(n_head, xf, cf, live, gain_ref, wt_ref, w_ref, wo_ref, bias_ref,
               x_out, go_ref, nrm_t, mix_t, gp_t, bsum_ref, proj_t, kv, gm_t)

    n_proj = 3 * n_chan
    weight_sums(sums, nrm_t, gp_t, mix_t, go_ref, sums_in)
    gain_sum = jnp.sum(sums[:, :n_proj] * w_ref[...].astype(jnp.float32), 1, keepdims=True)

    width = 2 * LANES
    cell = lax.broadcasted_iota(jnp.int32, (LANES, width), 0) % CELLS
    lane = lax.broadcasted_iota(jnp.int32, (LANES, width), 1)
    place = (cell // WINDOW) * 16 + cell % WINDOW + 119
    onehot = (lane == place).astype(jnp.float32).astype(jnp.bfloat16)
    flat = bsum_ref[...].reshape(n_head * CELLS, LANES)
    high = flat.astype(jnp.bfloat16)
    low = (flat - high.astype(jnp.float32)).astype(jnp.bfloat16)
    spread = dot(high, onehot) + dot(low, onehot)
    spread_a[...] = spread[:, :LANES]
    spread_b[...] = spread[:, LANES:]
    bias_sum = jnp.zeros((n_head, width), jnp.float32)
    for j in range(CELLS):
        row = jnp.concatenate([ref[pl.ds(j, n_head, stride=CELLS), :] for ref in (spread_a, spread_b)], 1)
        by = (j // WINDOW) * 16 + j % WINDOW
        bias_sum += pltpu.roll(row, width - by, 1) if by else row
    tail = lax.broadcasted_iota(jnp.int32, (n_chan, LANES), 1) == LANES - 1
    bias_rows = jnp.concatenate(
        [bias_sum[:, :LANES], bias_sum[:, LANES:], jnp.zeros((n_chan - 2 * n_head, LANES), jnp.float32)], 0
    )
    sums[:, n_proj + n_chan :] = jnp.where(tail, gain_sum * (1.0 / gain_col(gain_ref)), bias_rows)

    n_c, n_x, n_y = counts
    rows = n_chan // (n_c * n_x * n_y)
    for c in range(n_c):
        for x in range(n_x):
            for y in range(n_y):
                chunk = sums[((c * n_x + x) * n_y + y) * rows : ((c * n_x + x) * n_y + y + 1) * rows]
                at = lax.rem(x - meta[3] + n_x, n_x) * n_y + lax.rem(y - meta[4] + n_y, n_y)

                @pl.when(meta[2] == c)
                def _():
                    keep_ref[at] = chunk

                @pl.when(meta[2] != c)
                def _():
                    send_ref[at] = chunk.astype(jnp.bfloat16)


def gain_col(gain_ref):
    n_chan = gain_ref.shape[1]
    return jnp.broadcast_to(gain_ref[...], (LANES, n_chan)).T[:, :1]


def cells_kernel(meta, xl_ref, xr_ref, xo_ref, gpl_ref, gpr_ref, gpo_ref, cot_ref, gain_ref, w_ref, base_ref, top_ref, side_ref, corner_ref, ext):
    n_rows, n_cols, n_chan = cot_ref.shape
    lat, lon = meta[0], meta[1]
    ext[...] = jnp.zeros_like(ext)
    for part, pieces in enumerate((((xo_ref, gpo_ref),), ((xl_ref, gpl_ref), (xr_ref, gpr_ref)))):
        n_tok = n_cols * WINDOW
        cells = []
        for x_ref, gp_t, base in [(*piece, base) for piece in pieces for base in range(0, piece[0].shape[0], TOKENS)]:
            rows = slice(base, base + TOKENS)
            x_hat, inv = norm_stats(x_ref[rows].astype(jnp.float32))
            g = dot(w_ref[...], gp_t[:, rows]).T * gain_ref[...]
            cells.append(inv * (g - jnp.mean(g, -1, keepdims=True) - x_hat * jnp.mean(g * x_hat, -1, keepdims=True)))
        blank = jnp.zeros((1, WINDOW, n_chan), jnp.float32)
        head = lax.broadcasted_iota(jnp.int32, (WINDOW, n_chan), 0) < lon
        for r in range(WINDOW):
            row = jnp.stack(
                [
                    cells[w * CELLS // TOKENS][w * CELLS % TOKENS + r * WINDOW :][:WINDOW]
                    for w in range(n_tok // CELLS)
                ],
                0,
            )
            row = jnp.concatenate([blank, pltpu.roll(row, lon, 1), blank], 0)
            for t in range(row.shape[0] - 1):
                ext[lat + part * WINDOW + r, t * WINDOW : (t + 1) * WINDOW, :] = jnp.where(head, row[t], row[t + 1])
    for r in range(n_rows):
        base_ref[r] = (cot_ref[r].astype(jnp.float32) + ext[WINDOW + r, WINDOW:]).astype(jnp.bfloat16)
        side_ref[r] = ext[WINDOW + r, :WINDOW].astype(jnp.bfloat16)
    n_top = top_ref.shape[0]
    for r in range(n_top):
        top_ref[r] = ext[WINDOW - n_top + r, WINDOW:].astype(jnp.bfloat16)
        corner_ref[r] = ext[WINDOW - n_top + r, :WINDOW].astype(jnp.bfloat16)


def prepare_kernel(bias_ref, w_ref, full_ref, wt_ref):
    n_head, n_gap = bias_ref.shape
    span = 2 * WINDOW - 1
    width = 2 * LANES
    lane = lax.broadcasted_iota(jnp.int32, (width, LANES), 0)
    cell = lax.broadcasted_iota(jnp.int32, (width, LANES), 1) % CELLS
    place = cell // WINDOW * span + cell % WINDOW + n_gap // 2
    onehot = (lane == place).astype(jnp.float32).astype(jnp.bfloat16)
    table = jnp.concatenate([bias_ref[...], jnp.zeros((n_head, width - n_gap), jnp.float32)], 1)
    for h in range(n_head):
        line = jnp.broadcast_to(table[h : h + 1], (WINDOW, width))
        rows = [pltpu.roll(line, r * span, 1, stride=1, stride_axis=0) for r in range(WINDOW)]
        rest = jnp.concatenate(rows, 0)
        total = jnp.zeros((CELLS, LANES), jnp.float32)
        for _ in range(3):
            part = rest.astype(jnp.bfloat16)
            total += dot(part, onehot)
            rest = rest - part.astype(jnp.float32)
        full_ref[h] = total
    wt_ref[...] = w_ref[...].T


def pack_kernel(n_top, x_ref, cot_ref, mask, side_ref, top_x, top_c, corner_ref):
    n_rows, n_cols, n_chan = x_ref.shape
    for k, (ref, top) in enumerate(((x_ref, top_x), (cot_ref, top_c))):
        for r in range(n_rows):
            edge = ref[r, n_cols - 2 * WINDOW :, :][WINDOW:]
            side_ref[k, r] = edge
            at = r - n_rows + n_top
            if at >= 0:
                top[at] = ref[r]
                corner_ref[k, at] = edge
    line = lax.broadcasted_iota(jnp.int32, (WINDOW, n_chan), 0)
    live = jnp.zeros((WINDOW, n_chan), jnp.float32)
    for r in range(WINDOW):
        live = jnp.where(line == r, mask[n_rows - WINDOW + r].astype(jnp.float32), live)
    corner_ref[0, n_top] = live.astype(jnp.bfloat16)
    corner_ref[1, n_top] = live.astype(jnp.bfloat16)


def first_add_kernel(keep_ref, got_ref, own_ref, *send_refs):
    size = own_ref.shape[0]
    for k in range(len(send_refs) + 1):
        cut = slice(k * size, (k + 1) * size)
        total = keep_ref[cut] + got_ref[cut].astype(jnp.float32)
        if k:
            send_refs[k - 1][...] = total.astype(jnp.bfloat16)
        else:
            own_ref[...] = total


def next_add_kernel(n_got, n_more, own_ref, *refs):
    got, (out_ref, *send_refs) = refs[:n_got], refs[n_got + n_more :]
    size = out_ref.shape[0]
    for k in range(len(send_refs) + 1):
        cut = slice(k * size, (k + 1) * size)
        total = own_ref[cut]
        for ref in got:
            total = total + ref[cut].astype(jnp.float32)
        if k:
            send_refs[k - 1][...] = total.astype(jnp.bfloat16)
        else:
            out_ref[...] = total.astype(out_ref.dtype)


def join_kernel(n_got, *refs):
    for k in range(n_got):
        refs[-1][k : k + 1] = refs[k][...]


def after_kernel(*refs):
    pass


def after(array, other):
    here = pl.BlockSpec(memory_space=pl.ANY)
    return pl.pallas_call(
        after_kernel,
        out_shape=jax.ShapeDtypeStruct(array.shape, array.dtype),
        in_specs=[here, here],
        out_specs=here,
        input_output_aliases={0: 0},
        name="after",
    )(array, other)


def pair_add_kernel(a_ref, b_ref, *refs):
    refs[-1][...] = (a_ref[...].astype(jnp.float32) + b_ref[...].astype(jnp.float32)).astype(jnp.bfloat16)


def unpack_kernel(counts, n_proj, factor, meta, *refs):
    n_c, n_x, n_y = counts
    mine, other = refs[:n_x], refs[n_x : 2 * n_x]
    qkv_ref, out_ref, gain_ref, bias_ref, small = refs[2 * n_x :]
    rows = mine[0].shape[1]
    n_chan = out_ref.shape[1]
    for half in range(2):
        c = meta[2] if half == 0 else 1 - meta[2]
        for k, ref in enumerate(other if half else mine):
            x = lax.rem(meta[3] + k, n_x)
            for j in range(n_y):
                y = lax.rem(meta[4] + j, n_y)
                chunk = ref[j].astype(jnp.float32) * factor
                to = pl.ds(pl.multiple_of(((c * n_x + x) * n_y + y) * rows, rows), rows)
                qkv_ref[to] = chunk[:, :n_proj]
                out_ref[to] = chunk[:, n_proj : n_proj + n_chan]
                small[to] = chunk[:, n_proj + n_chan :]
    gain_ref[...] = small[...].T[LANES - 1 :]
    n_head, n_gap = bias_ref.shape
    span = 2 * WINDOW - 1
    wide = jnp.concatenate([small[:n_head], small[n_head : 2 * n_head]], 1)
    lane = lax.broadcasted_iota(jnp.int32, wide.shape, 1)
    bias = jnp.zeros_like(wide)
    for k in range(span):
        moved = pltpu.roll(wide, 2 * LANES - k, 1) if k else wide
        bias = jnp.where((lane >= k * span) & (lane < (k + 1) * span), moved, bias)
    bias_ref[...] = bias[:, :n_gap]


class Places:
    def __init__(self):
        self.n_lat, self.n_lon = lax.axis_size("lat"), lax.axis_size("lon")
        self.c = 2
        self.x = min(4, self.n_lon // self.c)
        self.y_low = self.n_lon // (self.c * self.x)
        self.y_high = 2
        self.y = self.y_low * self.y_high
        self.z = self.n_lat // self.y_high

    def index(self, z, y, x, c):
        high, low = divmod(y, self.y_low)
        return (z * self.y_high + high) * self.n_lon + (low * self.x + x) * self.c + c

    def mine(self):
        lat, lon = lax.axis_index("lat"), lax.axis_index("lon")
        return (
            lon % self.c,
            lon // self.c % self.x,
            lat % self.y_high * self.y_low + lon // (self.c * self.x),
        )

    def move(self, array, to):
        every = itertools.product(range(self.z), range(self.y), range(self.x), range(self.c))
        pairs = [(self.index(*at), self.index(*to(*at))) for at in every]
        return lax.ppermute(array, ("lat", "lon"), pairs)

    def by_c(self, array):
        return self.move(array, lambda z, y, x, c: (z, y, x, 1 - c))

    def by_x(self, array, k):
        return self.move(array, lambda z, y, x, c: (z, y, (x + k) % self.x, c))

    def by_y(self, array, k):
        return self.move(array, lambda z, y, x, c: (z, (y + k) % self.y, x, c))

    def first_half_way(self, array):
        return self.move(array, lambda z, y, x, c: (z, (y - 1) % self.y, x, c))

    def second_half_way(self, array):
        def to(z, y, x, c):
            high, low = divmod((y + 1) % self.y, self.y_low)
            band = (z * self.y_high + high + 1) % self.n_lat
            return band // self.y_high, band % self.y_high * self.y_low + low, x, c

        return self.move(array, to)

    def by_z(self, array, bits):
        return self.move(array, lambda z, y, x, c: (z ^ bits, y, x, c))


def small_call(kernel, outs, name, *args):
    return pl.pallas_call(
        kernel,
        out_shape=outs,
        compiler_params=pltpu.CompilerParams(vmem_limit_bytes=32 * MIB),
        name=name,
    )(*args)


def total_over_devices(places, keep, send, ahead, behind):
    shape = keep.shape[1:]
    bf = functools.partial(jax.ShapeDtypeStruct, dtype=jnp.bfloat16)
    got = places.by_c(send)
    own = jax.ShapeDtypeStruct((places.y, *shape), jnp.float32)
    own, *sends = small_call(first_add_kernel, (own,) + (bf((places.y, *shape)),) * (places.x - 1), "add_c", keep, got)
    got = [places.by_x(part, k + 1) for k, part in enumerate(sends)]
    nxt = jax.ShapeDtypeStruct((1, *shape), jnp.float32)
    own, *sends = pl.pallas_call(
        functools.partial(next_add_kernel, len(got), 1),
        out_shape=(nxt,) + (bf((1, *shape)),) * (places.y - 1),
        in_specs=[whole()] * (1 + len(got)) + [pl.BlockSpec(memory_space=pl.ANY)],
        compiler_params=pltpu.CompilerParams(vmem_limit_bytes=16 * MIB),
        name="add_x",
    )(own, *got, ahead)
    got = [places.by_y(part, k + 1) for k, part in enumerate(sends)]
    (mine,) = small_call(functools.partial(next_add_kernel, len(got), 0), (bf((1, *shape)),), "add_y", own, *got)
    for bits in {1: (), 2: (1,), 4: (1, 3), 8: (1, 2, 6)}[places.z]:
        other = places.by_z(mine, bits)
        mine = small_call(pair_add_kernel, bf((1, *shape)), "add_z", mine, other)
    parts = [mine] + [places.by_y(mine, -k) for k in range(1, places.y)]
    mine = pl.pallas_call(
        functools.partial(join_kernel, len(parts)),
        out_shape=bf((places.y, *shape)),
        in_specs=[whole()] * len(parts) + [pl.BlockSpec(memory_space=pl.ANY)] * len(behind),
        compiler_params=pltpu.CompilerParams(vmem_limit_bytes=4 * MIB),
        name="join",
    )(*parts, *behind)
    mine = [mine] + [places.by_x(mine, -k) for k in range(1, places.x)]
    return mine, [places.by_c(part) for part in mine]


def ring(array, lat, lon):
    n_lat, n_lon = lax.axis_size("lat"), lax.axis_size("lon")
    pairs = [
        (i * n_lon + j, (i + lat) % n_lat * n_lon + (j + lon) % n_lon) for i in range(n_lat) for j in range(n_lon)
    ]
    return lax.ppermute(array, ("lat", "lon"), pairs)


def local(saved_state, cotangent, row_mask, shifts, norm_gain, w_qkv, w_out, bias_table):
    n_rows, n_cols, n_chan = saved_state.shape
    n_head = bias_table.shape[0]
    n_proj = w_qkv.shape[1]
    n_tok = n_rows // 2 * n_cols
    n_top = WINDOW - 1
    places = Places()
    counts = (places.c, places.x, places.y)
    bf, f32 = jnp.bfloat16, jnp.float32

    smem = pl.BlockSpec(memory_space=pltpu.SMEM)
    tile = functools.partial(jax.ShapeDtypeStruct, dtype=bf)
    side, top_x, top_c, corner = pl.pallas_call(
        functools.partial(pack_kernel, n_top),
        out_shape=(
            tile((2, n_rows, WINDOW, n_chan)),
            tile((n_top, n_cols, n_chan)),
            tile((n_top, n_cols, n_chan)),
            tile((2, WINDOW, WINDOW, n_chan)),
        ),
        in_specs=[whole(), whole(), smem],
        compiler_params=pltpu.CompilerParams(vmem_limit_bytes=8 * MIB),
        name="pack",
    )(saved_state, cotangent, row_mask)
    side = ring(side, 0, 1)
    top_x = ring(top_x, 1, 0)
    half_way = places.first_half_way(top_c)
    corner = ring(corner, 1, 1)
    at = jnp.stack(places.mine()).astype(jnp.int32)
    gain = norm_gain.reshape(1, n_chan)
    bias, w_t = pl.pallas_call(
        prepare_kernel,
        out_shape=(jax.ShapeDtypeStruct((n_head, CELLS, LANES), f32), tile((n_proj, n_chan))),
        compiler_params=pltpu.CompilerParams(vmem_limit_bytes=16 * MIB),
        cost_estimate=pl.CostEstimate(flops=10**9, bytes_accessed=4 * MIB, transcendentals=0),
        name="prepare",
    )(bias_table, w_qkv)

    def work(tokens):
        return [
            pltpu.VMEM((tokens, n_chan), bf),
            pltpu.VMEM((n_chan, tokens), bf),
            pltpu.VMEM((n_chan, tokens), bf),
        ], [
            pltpu.VMEM((tokens, n_chan), f32),
            pltpu.VMEM((tokens, n_chan), f32),
            pltpu.VMEM((n_proj, tokens), bf),
            pltpu.VMEM((tokens, 2 * n_chan), bf),
            pltpu.VMEM((n_chan, tokens), bf),
        ]

    below = jnp.minimum(lax.axis_index("lat"), 1).astype(jnp.int32).reshape(1)
    meta = jnp.concatenate([shifts, at, below, row_mask])
    n_half = n_tok // 2

    def inner(name, *more):
        left = len(more) > 1
        first, second = work(n_half)
        return pl.pallas_call(
            functools.partial(inner_kernel, n_head, left),
            out_shape=(
                tile((n_half, n_chan)),
                tile((n_proj, n_half)),
                jax.ShapeDtypeStruct((n_chan, n_proj + n_chan), f32),
                jax.ShapeDtypeStruct((n_head, CELLS, LANES), f32),
            ),
            in_specs=[smem] + [whole()] * (6 + len(more)) + [pl.BlockSpec(memory_space=pl.ANY)],
            scratch_shapes=first + second,
            compiler_params=pltpu.CompilerParams(vmem_limit_bytes=20 * MIB),
            cost_estimate=pl.CostEstimate(flops=10**8 if left else 10**10, bytes_accessed=MIB, transcendentals=0),
            name=name,
        )(meta, saved_state, cotangent, bias, gain, w_t, w_qkv, w_out, *more)

    x_right, gp_right, sums_in, bsum_in = inner("inner_right", side)
    half_way = after(half_way, x_right)
    top_c = places.second_half_way(half_way)
    x_left, gp_left, sums_in, bsum_in = inner("inner_left", side, sums_in, bsum_in, half_way)

    width = n_proj + n_chan + LANES
    rows = n_chan // math.prod(counts)
    half = math.prod(counts) // 2
    x_out, gp_out, keep, send = pl.pallas_call(
        functools.partial(outer_kernel, n_head, counts),
        out_shape=(
            tile((n_tok, n_chan)),
            tile((n_proj, n_tok)),
            jax.ShapeDtypeStruct((half, rows, width), f32),
            tile((half, rows, width)),
        ),
        in_specs=[smem] + [whole()] * 13,
        scratch_shapes=[
            *work(n_tok)[0],
            pltpu.VMEM((n_head, CELLS, LANES), f32),
            *work(n_tok)[1],
            pltpu.VMEM((n_chan, width), f32),
            pltpu.VMEM((n_head * CELLS, LANES), f32),
            pltpu.VMEM((n_head * CELLS, LANES), f32),
        ],
        compiler_params=pltpu.CompilerParams(vmem_limit_bytes=30 * MIB),
        cost_estimate=pl.CostEstimate(flops=10**10, bytes_accessed=24 * MIB, transcendentals=2**19),
        name="outer",
    )(meta, saved_state, cotangent, side, top_x, top_c, corner, bias, gain, w_t, w_qkv, w_out, sums_in, bsum_in)

    base, *edges = pl.pallas_call(
        cells_kernel,
        out_shape=(
            tile((n_rows, n_cols, n_chan)),
            tile((n_top, n_cols, n_chan)),
            tile((n_rows, WINDOW, n_chan)),
            tile((n_top, WINDOW, n_chan)),
        ),
        in_specs=[smem] + [whole()] * 9,
        scratch_shapes=[pltpu.VMEM((n_rows + WINDOW, n_cols + WINDOW, n_chan), f32)],
        compiler_params=pltpu.CompilerParams(vmem_limit_bytes=40 * MIB),
        cost_estimate=pl.CostEstimate(flops=16 * 10**8, bytes_accessed=12 * MIB, transcendentals=0),
        name="cells",
    )(meta, x_left, x_right, x_out, gp_left, gp_right, gp_out, cotangent, gain, w_qkv)
    top_back, side_back, corner_back = ring(edges[0], -1, 0), ring(edges[1], 0, -1), ring(edges[2], -1, -1)
    mine, other = total_over_devices(places, keep, send, edges[2], (top_back, side_back, corner_back))
    edge = jnp.pad(top_back, ((n_rows - n_top, 0), (0, 0), (0, 0)))
    edge = edge + jnp.pad(side_back, ((0, 0), (n_cols - WINDOW, 0), (0, 0)))
    edge = edge + jnp.pad(corner_back, ((n_rows - n_top, 0), (n_cols - WINDOW, 0), (0, 0)))
    state_grad = (base.astype(f32) + edge.astype(f32)).astype(bf)

    factor = 1.0 / math.sqrt(n_rows * places.n_lat * n_cols * places.n_lon)
    qkv_grad, out_grad, gain_grad, bias_grad = pl.pallas_call(
        functools.partial(unpack_kernel, counts, n_proj, factor),
        out_shape=(
            jax.ShapeDtypeStruct((n_chan, n_proj), f32),
            jax.ShapeDtypeStruct((n_chan, n_chan), f32),
            jax.ShapeDtypeStruct((1, n_chan), f32),
            jax.ShapeDtypeStruct(bias_table.shape, f32),
        ),
        in_specs=[smem] + [whole()] * (2 * places.x),
        scratch_shapes=[pltpu.VMEM((n_chan, LANES), f32)],
        compiler_params=pltpu.CompilerParams(vmem_limit_bytes=32 * MIB),
        name="unpack",
    )(meta, *mine, *other)
    return state_grad, qkv_grad, out_grad, gain_grad.reshape(n_chan), bias_grad


def solution(mesh):
    return jax.shard_map(
        local,
        mesh=mesh,
        in_specs=(P("lat", "lon", None), P("lat", "lon", None), P("lat"), P(), P(), P(), P(), P()),
        out_specs=(P("lat", "lon", None), P(), P(), P(), P()),
        check_vma=False,
    )
```

```python
import functools
import itertools
import math

import jax
import jax.numpy as jnp
from jax import lax
from jax.experimental import pallas as pl
from jax.experimental.pallas import tpu as pltpu
from jax.sharding import PartitionSpec as P

EPSILON = 1e-05


NT = (((1,), (1,)), ((), ()))
NN = (((1,), (0,)), ((), ()))
LANES = 128
WINDOW = 8
CELLS = WINDOW * WINDOW
TOKENS = 256
MIB = 1024 * 1024


def dot(a, b, dims=NN):
    return lax.dot_general(a, b, dims, preferred_element_type=jnp.float32)


def whole(*_):
    return pl.BlockSpec(memory_space=pltpu.VMEM)


def norm_stats(x):
    cen = x - jnp.mean(x, -1, keepdims=True)
    inv = lax.rsqrt(jnp.mean(cen * cen, -1, keepdims=True) + EPSILON)
    return cen * inv, inv


def project_chunk(n_chan, scale, gain, wt_ref, w_ref, wo_ref, xf, go_ref, nrm_t, proj_t, kv, gm_t, base):
    rows = slice(base, base + TOKENS)
    x_hat, _ = norm_stats(xf[rows])
    normed_f = x_hat * gain
    normed = normed_f.astype(jnp.bfloat16)
    nrm_t[:, rows] = normed_f.T.astype(jnp.bfloat16)
    proj_t[:n_chan, rows] = (dot(wt_ref[:n_chan], normed, NT) * scale).astype(jnp.bfloat16)
    proj_t[n_chan:, rows] = dot(wt_ref[n_chan:], normed, NT).astype(jnp.bfloat16)
    kv[rows] = dot(normed, w_ref[:, n_chan:]).astype(jnp.bfloat16)
    gm_t[:, rows] = dot(wo_ref[...], go_ref[rows], NT).astype(jnp.bfloat16)


def block_diag(block, step):
    blank = jnp.zeros((step, block.shape[1]), block.dtype)
    count = block.shape[0] // step
    columns = []
    for h in range(count):
        parts = [blank] * count
        parts[h] = block[h * step : (h + 1) * step]
        columns.append(jnp.concatenate(parts, 0))
    return jnp.concatenate(columns, 1)


def attention_unit(n_chan, dim, scale, bias_ref, mask, proj_t, kv, gm_t, mix_t, gp_t, bsum_ref, pair, group):
    lanes = pl.ds(pl.multiple_of(pair * LANES, LANES), LANES)
    c0 = group * LANES
    q_t = proj_t[pl.ds(c0, LANES), lanes]
    k_t = proj_t[pl.ds(n_chan + c0, LANES), lanes]
    v_t = proj_t[pl.ds(2 * n_chan + c0, LANES), lanes]
    g_t = gm_t[pl.ds(c0, LANES), lanes]
    k_tok = kv[lanes, pl.ds(c0, LANES)]
    v_tok = kv[lanes, pl.ds(n_chan + c0, LANES)]
    scores = dot(k_tok, block_diag(q_t, dim))
    grads = dot(v_tok, block_diag(g_t, dim))
    first = lax.broadcasted_iota(jnp.int32, (CELLS, LANES), 1) < CELLS
    heads = LANES // dim
    mixed, dq, dk, dv = [], [], [], []
    for h in range(heads):
        cut = slice(h * LANES, (h + 1) * LANES)
        rows = slice(h * dim, (h + 1) * dim)
        head = group * heads + h
        s = jnp.where(first, scores[:CELLS, cut], scores[CELLS:, cut]) + bias_ref[head] + mask
        e = jnp.exp(s - jnp.max(s, 0, keepdims=True))
        a = e * (1.0 / jnp.sum(e, 0, keepdims=True))
        d = jnp.where(first, grads[:CELLS, cut], grads[CELLS:, cut])
        ad = a * d
        ds = ad - a * jnp.sum(ad, 0, keepdims=True)
        bsum_ref[head] += ds
        zero = jnp.zeros_like(a)
        a2 = jnp.concatenate([jnp.where(first, a, zero), jnp.where(first, zero, a)], 0).astype(jnp.bfloat16)
        ds2 = jnp.concatenate([jnp.where(first, ds, zero), jnp.where(first, zero, ds)], 0).astype(jnp.bfloat16)
        mixed.append(dot(v_t[rows], a2))
        dv.append(dot(g_t[rows], a2, NT))
        dq.append(dot(k_t[rows], ds2) * scale)
        dk.append(dot(q_t[rows], ds2, NT))
    mix_t[pl.ds(c0, LANES), lanes] = jnp.concatenate(mixed, 0).astype(jnp.bfloat16)
    gp_t[pl.ds(c0, LANES), lanes] = jnp.concatenate(dq, 0).astype(jnp.bfloat16)
    gp_t[pl.ds(n_chan + c0, LANES), lanes] = jnp.concatenate(dk, 0).astype(jnp.bfloat16)
    gp_t[pl.ds(2 * n_chan + c0, LANES), lanes] = jnp.concatenate(dv, 0).astype(jnp.bfloat16)


def place_row(line, shift, out, r, live=None):
    line = line.astype(jnp.float32).reshape(-1, WINDOW, line.shape[1])
    if live is not None:
        line = line * live
    line = pltpu.roll(line, WINDOW - shift, 1)
    head = lax.broadcasted_iota(jnp.int32, line.shape[1:], 0) < WINDOW - shift
    for w in range(line.shape[0] - 1):
        start = w * CELLS + r * WINDOW
        out[start : start + WINDOW] = jnp.where(head, line[w], line[w + 1])


def window_row(n_head, xf, cf, live, gain_ref, wt_ref, w_ref, wo_ref, bias_ref,
               x_out, go_ref, nrm_t, mix_t, gp_t, bsum_ref, proj_t, kv, gm_t):
    n_tok, n_chan = xf.shape
    dim = n_chan // n_head
    scale = dim ** (-0.5)
    x_out[...] = xf[...].astype(jnp.bfloat16)
    go_ref[...] = cf[...].astype(jnp.bfloat16)
    for base in range(0, n_tok, TOKENS):
        project_chunk(n_chan, scale, gain_ref[...], wt_ref, w_ref, wo_ref, xf, go_ref, nrm_t, proj_t, kv, gm_t, base)
    mask = jnp.concatenate([(live[r][:, :LANES] - 1.0) * 1e30 for r in range(WINDOW)], 0)
    groups = n_chan // LANES

    @pl.loop(0, n_tok // LANES)
    def _(pair):
        for group in range(groups):
            attention_unit(n_chan, dim, scale, bias_ref, mask, proj_t, kv, gm_t, mix_t, gp_t, bsum_ref, pair, group)


def weight_sums(sums, nrm_t, gp_t, mix_t, go_ref, more):
    n_proj, n_chan = gp_t.shape[0], nrm_t.shape[0]
    for base in range(0, n_proj + n_chan, TOKENS):
        cols = slice(base, base + TOKENS)
        if base < n_proj:
            part = dot(nrm_t[...], gp_t[cols], NT)
        else:
            part = dot(mix_t[...], go_ref[:, base - n_proj : base - n_proj + TOKENS])
        sums[:, cols] = part if more is None else part + more[:, cols]


def inner_kernel(n_head, left, meta, x_ref, cot_ref, bias_ref, gain_ref, wt_ref, w_ref, wo_ref, *refs):
    if left:
        side_ref, sums_in, bsum_in, *refs = refs
    _, *refs = refs
    x_out, gp_t, sums_ref, bsum_ref, go_ref, nrm_t, mix_t, xf, cf, proj_t, kv, gm_t = refs
    lat, lon = meta[0], meta[1]
    half = x_ref.shape[1] // 2
    live = []
    for r in range(WINDOW):
        live.append(jnp.full((WINDOW, x_ref.shape[2]), meta[6 + lat + r].astype(jnp.float32)))
        for k, (grid, out) in enumerate(((x_ref, xf), (cot_ref, cf))):
            line = grid[lat + r].astype(jnp.float32)
            if left:
                line = jnp.concatenate([side_ref[k, lat + r].astype(jnp.float32), line[:half]], 0)
            else:
                line = line[half - WINDOW :]
            place_row(line, lon, out, r, live[r] if k else None)
    bsum_ref[...] = bsum_in[...] if left else jnp.zeros_like(bsum_ref)
    window_row(n_head, xf, cf, live, gain_ref, wt_ref, w_ref, wo_ref, bias_ref,
               x_out, go_ref, nrm_t, mix_t, gp_t, bsum_ref, proj_t, kv, gm_t)
    weight_sums(sums_ref, nrm_t, gp_t, mix_t, go_ref, sums_in if left else None)


def outer_kernel(n_head, counts, meta, x_ref, cot_ref, side_ref, top_x, top_c, corner_ref, bias_ref, gain_ref, wt_ref, w_ref, wo_ref,
                 sums_in, bsum_in,
                 x_out, gp_t, keep_ref, send_ref,
                 go_ref, nrm_t, mix_t, bsum_ref, xf, cf, proj_t, kv, gm_t, sums, spread_a, spread_b):
    n_chan = gain_ref.shape[1]
    n_top = top_x.shape[0]
    lat, lon = meta[0], meta[1]
    up_mask = corner_ref[0, WINDOW - 1].astype(jnp.float32) * meta[5].astype(jnp.float32)
    line_of = lax.broadcasted_iota(jnp.int32, up_mask.shape, 0)
    live = []
    for r in range(WINDOW):
        e = lat + r
        above = e < WINDOW
        up = jnp.clip(e - (WINDOW - n_top), 0, n_top - 1)
        own = jnp.maximum(e - WINDOW, 0)
        row_live = jnp.full((WINDOW, n_chan), meta[6 + own].astype(jnp.float32))
        up_live = jnp.sum(jnp.where(line_of == e, up_mask, 0.0), 0, keepdims=True)
        live.append(jnp.where(above, jnp.broadcast_to(up_live, row_live.shape), row_live))
        side = [jnp.where(above, corner_ref[k, up], side_ref[k, own]) for k in range(2)]
        for k, (top, grid, out) in enumerate(((top_x, x_ref, xf), (top_c, cot_ref, cf))):
            line = jnp.where(above, top[up], grid[own]).astype(jnp.float32)
            line = jnp.concatenate([side[k].astype(jnp.float32), line], 0)
            place_row(line, lon, out, r, live[r] if k else None)
    bsum_ref[...] = bsum_in[...]
    window_row(n_head, xf, cf, live, gain_ref, wt_ref, w_ref, wo_ref, bias_ref,
               x_out, go_ref, nrm_t, mix_t, gp_t, bsum_ref, proj_t, kv, gm_t)

    n_proj = 3 * n_chan
    weight_sums(sums, nrm_t, gp_t, mix_t, go_ref, sums_in)
    gain_sum = jnp.sum(sums[:, :n_proj] * w_ref[...].astype(jnp.float32), 1, keepdims=True)

    width = 2 * LANES
    cell = lax.broadcasted_iota(jnp.int32, (LANES, width), 0) % CELLS
    lane = lax.broadcasted_iota(jnp.int32, (LANES, width), 1)
    place = (cell // WINDOW) * 16 + cell % WINDOW + 119
    onehot = (lane == place).astype(jnp.float32).astype(jnp.bfloat16)
    flat = bsum_ref[...].reshape(n_head * CELLS, LANES)
    high = flat.astype(jnp.bfloat16)
    low = (flat - high.astype(jnp.float32)).astype(jnp.bfloat16)
    spread = dot(high, onehot) + dot(low, onehot)
    spread_a[...] = spread[:, :LANES]
    spread_b[...] = spread[:, LANES:]
    bias_sum = jnp.zeros((n_head, width), jnp.float32)
    for j in range(CELLS):
        row = jnp.concatenate([ref[pl.ds(j, n_head, stride=CELLS), :] for ref in (spread_a, spread_b)], 1)
        by = (j // WINDOW) * 16 + j % WINDOW
        bias_sum += pltpu.roll(row, width - by, 1) if by else row
    tail = lax.broadcasted_iota(jnp.int32, (n_chan, LANES), 1) == LANES - 1
    bias_rows = jnp.concatenate(
        [bias_sum[:, :LANES], bias_sum[:, LANES:], jnp.zeros((n_chan - 2 * n_head, LANES), jnp.float32)], 0
    )
    sums[:, n_proj + n_chan :] = jnp.where(tail, gain_sum * (1.0 / gain_col(gain_ref)), bias_rows)

    n_c, n_x, n_y = counts
    rows = n_chan // (n_c * n_x * n_y)
    for c in range(n_c):
        for x in range(n_x):
            for y in range(n_y):
                chunk = sums[((c * n_x + x) * n_y + y) * rows : ((c * n_x + x) * n_y + y + 1) * rows]
                at = lax.rem(x - meta[3] + n_x, n_x) * n_y + lax.rem(y - meta[4] + n_y, n_y)

                @pl.when(meta[2] == c)
                def _():
                    keep_ref[at] = chunk

                @pl.when(meta[2] != c)
                def _():
                    send_ref[at] = chunk.astype(jnp.bfloat16)


def gain_col(gain_ref):
    n_chan = gain_ref.shape[1]
    return jnp.broadcast_to(gain_ref[...], (LANES, n_chan)).T[:, :1]


def cells_kernel(meta, xl_ref, xr_ref, xo_ref, gpl_ref, gpr_ref, gpo_ref, cot_ref, gain_ref, w_ref, base_ref, top_ref, side_ref, corner_ref, ext):
    n_rows, n_cols, n_chan = cot_ref.shape
    lat, lon = meta[0], meta[1]
    ext[...] = jnp.zeros_like(ext)
    for part, pieces in enumerate((((xo_ref, gpo_ref),), ((xl_ref, gpl_ref), (xr_ref, gpr_ref)))):
        n_tok = n_cols * WINDOW
        cells = []
        for x_ref, gp_t, base in [(*piece, base) for piece in pieces for base in range(0, piece[0].shape[0], TOKENS)]:
            rows = slice(base, base + TOKENS)
            x_hat, inv = norm_stats(x_ref[rows].astype(jnp.float32))
            g = dot(w_ref[...], gp_t[:, rows]).T * gain_ref[...]
            cells.append(inv * (g - jnp.mean(g, -1, keepdims=True) - x_hat * jnp.mean(g * x_hat, -1, keepdims=True)))
        blank = jnp.zeros((1, WINDOW, n_chan), jnp.float32)
        head = lax.broadcasted_iota(jnp.int32, (WINDOW, n_chan), 0) < lon
        for r in range(WINDOW):
            row = jnp.stack(
                [
                    cells[w * CELLS // TOKENS][w * CELLS % TOKENS + r * WINDOW :][:WINDOW]
                    for w in range(n_tok // CELLS)
                ],
                0,
            )
            row = jnp.concatenate([blank, pltpu.roll(row, lon, 1), blank], 0)
            for t in range(row.shape[0] - 1):
                ext[lat + part * WINDOW + r, t * WINDOW : (t + 1) * WINDOW, :] = jnp.where(head, row[t], row[t + 1])
    for r in range(n_rows):
        base_ref[r] = (cot_ref[r].astype(jnp.float32) + ext[WINDOW + r, WINDOW:]).astype(jnp.bfloat16)
        side_ref[r] = ext[WINDOW + r, :WINDOW].astype(jnp.bfloat16)
    n_top = top_ref.shape[0]
    for r in range(n_top):
        top_ref[r] = ext[WINDOW - n_top + r, WINDOW:].astype(jnp.bfloat16)
        corner_ref[r] = ext[WINDOW - n_top + r, :WINDOW].astype(jnp.bfloat16)


def prepare_kernel(bias_ref, w_ref, full_ref, wt_ref):
    n_head, n_gap = bias_ref.shape
    span = 2 * WINDOW - 1
    width = 2 * LANES
    lane = lax.broadcasted_iota(jnp.int32, (width, LANES), 0)
    cell = lax.broadcasted_iota(jnp.int32, (width, LANES), 1) % CELLS
    place = cell // WINDOW * span + cell % WINDOW + n_gap // 2
    onehot = (lane == place).astype(jnp.float32).astype(jnp.bfloat16)
    table = jnp.concatenate([bias_ref[...], jnp.zeros((n_head, width - n_gap), jnp.float32)], 1)
    for h in range(n_head):
        line = jnp.broadcast_to(table[h : h + 1], (WINDOW, width))
        rows = [pltpu.roll(line, r * span, 1, stride=1, stride_axis=0) for r in range(WINDOW)]
        rest = jnp.concatenate(rows, 0)
        total = jnp.zeros((CELLS, LANES), jnp.float32)
        for _ in range(3):
            part = rest.astype(jnp.bfloat16)
            total += dot(part, onehot)
            rest = rest - part.astype(jnp.float32)
        full_ref[h] = total
    wt_ref[...] = w_ref[...].T


def pack_kernel(n_top, x_ref, cot_ref, mask, side_ref, top_x, top_c, corner_ref, edges, sems):
    n_rows, n_cols, n_chan = x_ref.shape
    copies = []
    for k, (ref, top) in enumerate(((x_ref, top_x), (cot_ref, top_c))):
        copies.append(pltpu.make_async_copy(ref.at[:, pl.ds(n_cols - 2 * WINDOW, 2 * WINDOW)], edges.at[k], sems.at[2 * k]))
        copies.append(pltpu.make_async_copy(ref.at[pl.ds(n_rows - n_top, n_top)], top, sems.at[2 * k + 1]))
    for copy in copies:
        copy.start()
    for k in range(2):
        copies[2 * k].wait()
        for r in range(n_rows):
            edge = edges[k, r][WINDOW:]
            side_ref[k, r] = edge
            at = r - n_rows + n_top
            if at >= 0:
                corner_ref[k, at] = edge
    line = lax.broadcasted_iota(jnp.int32, (WINDOW, n_chan), 0)
    live = jnp.zeros((WINDOW, n_chan), jnp.float32)
    for r in range(WINDOW):
        live = jnp.where(line == r, mask[n_rows - WINDOW + r].astype(jnp.float32), live)
    corner_ref[0, n_top] = live.astype(jnp.bfloat16)
    corner_ref[1, n_top] = live.astype(jnp.bfloat16)
    copies[1].wait()
    copies[3].wait()


def first_add_kernel(keep_ref, got_ref, own_ref, *send_refs):
    size = own_ref.shape[0]
    for k in range(len(send_refs) + 1):
        cut = slice(k * size, (k + 1) * size)
        total = keep_ref[cut] + got_ref[cut].astype(jnp.float32)
        if k:
            send_refs[k - 1][...] = total.astype(jnp.bfloat16)
        else:
            own_ref[...] = total


def next_add_kernel(n_got, n_more, own_ref, *refs):
    got, (out_ref, *send_refs) = refs[:n_got], refs[n_got + n_more :]
    size = out_ref.shape[0]
    for k in range(len(send_refs) + 1):
        cut = slice(k * size, (k + 1) * size)
        total = own_ref[cut]
        for ref in got:
            total = total + ref[cut].astype(jnp.float32)
        if k:
            send_refs[k - 1][...] = total.astype(jnp.bfloat16)
        else:
            out_ref[...] = total.astype(out_ref.dtype)


def join_kernel(n_got, *refs):
    for k in range(n_got):
        refs[-1][k : k + 1] = refs[k][...]


def after_kernel(*refs):
    pass


def after(array, other):
    here = pl.BlockSpec(memory_space=pl.ANY)
    return pl.pallas_call(
        after_kernel,
        out_shape=jax.ShapeDtypeStruct(array.shape, array.dtype),
        in_specs=[here, here],
        out_specs=here,
        input_output_aliases={0: 0},
        compiler_params=pltpu.CompilerParams(vmem_limit_bytes=MIB),
        name="after",
    )(array, other)


def pair_add_kernel(a_ref, b_ref, *refs):
    refs[-1][...] = (a_ref[...].astype(jnp.float32) + b_ref[...].astype(jnp.float32)).astype(jnp.bfloat16)


def unpack_kernel(counts, n_proj, factor, meta, *refs):
    n_c, n_x, n_y = counts
    mine, other = refs[:n_x], refs[n_x : 2 * n_x]
    qkv_ref, out_ref, gain_ref, bias_ref, small = refs[2 * n_x :]
    rows = mine[0].shape[1]
    n_chan = out_ref.shape[1]
    for half in range(2):
        c = meta[2] if half == 0 else 1 - meta[2]
        for k, ref in enumerate(other if half else mine):
            x = lax.rem(meta[3] + k, n_x)
            for j in range(n_y):
                y = lax.rem(meta[4] + j, n_y)
                chunk = ref[j].astype(jnp.float32) * factor
                to = pl.ds(pl.multiple_of(((c * n_x + x) * n_y + y) * rows, rows), rows)
                qkv_ref[to] = chunk[:, :n_proj]
                out_ref[to] = chunk[:, n_proj : n_proj + n_chan]
                small[to] = chunk[:, n_proj + n_chan :]
    gain_ref[...] = small[...].T[LANES - 1 :]
    n_head, n_gap = bias_ref.shape
    span = 2 * WINDOW - 1
    wide = jnp.concatenate([small[:n_head], small[n_head : 2 * n_head]], 1)
    lane = lax.broadcasted_iota(jnp.int32, wide.shape, 1)
    bias = jnp.zeros_like(wide)
    for k in range(span):
        moved = pltpu.roll(wide, 2 * LANES - k, 1) if k else wide
        bias = jnp.where((lane >= k * span) & (lane < (k + 1) * span), moved, bias)
    bias_ref[...] = bias[:, :n_gap]


class Places:
    def __init__(self):
        self.n_lat, self.n_lon = lax.axis_size("lat"), lax.axis_size("lon")
        self.c = 2
        self.x = min(4, self.n_lon // self.c)
        self.y_low = self.n_lon // (self.c * self.x)
        self.y_high = 2
        self.y = self.y_low * self.y_high
        self.z = self.n_lat // self.y_high

    def index(self, z, y, x, c):
        high, low = divmod(y, self.y_low)
        return (z * self.y_high + high) * self.n_lon + (low * self.x + x) * self.c + c

    def mine(self):
        lat, lon = lax.axis_index("lat"), lax.axis_index("lon")
        return (
            lon % self.c,
            lon // self.c % self.x,
            lat % self.y_high * self.y_low + lon // (self.c * self.x),
        )

    def move(self, array, to):
        every = itertools.product(range(self.z), range(self.y), range(self.x), range(self.c))
        pairs = [(self.index(*at), self.index(*to(*at))) for at in every]
        return lax.ppermute(array, ("lat", "lon"), pairs)

    def by_c(self, array):
        return self.move(array, lambda z, y, x, c: (z, y, x, 1 - c))

    def by_x(self, array, k):
        return self.move(array, lambda z, y, x, c: (z, y, (x + k) % self.x, c))

    def by_y(self, array, k):
        return self.move(array, lambda z, y, x, c: (z, (y + k) % self.y, x, c))

    def first_half_way(self, array):
        return self.move(array, lambda z, y, x, c: (z, (y - 1) % self.y, x, c))

    def second_half_way(self, array):
        def to(z, y, x, c):
            high, low = divmod((y + 1) % self.y, self.y_low)
            band = (z * self.y_high + high + 1) % self.n_lat
            return band // self.y_high, band % self.y_high * self.y_low + low, x, c

        return self.move(array, to)

    def by_z(self, array, bits):
        return self.move(array, lambda z, y, x, c: (z ^ bits, y, x, c))


def small_call(kernel, outs, name, limit, *args):
    return pl.pallas_call(
        kernel,
        out_shape=outs,
        compiler_params=pltpu.CompilerParams(vmem_limit_bytes=limit * MIB),
        name=name,
    )(*args)


def total_over_devices(places, keep, send, ahead, behind):
    shape = keep.shape[1:]
    bf = functools.partial(jax.ShapeDtypeStruct, dtype=jnp.bfloat16)
    got = places.by_c(send)
    own = jax.ShapeDtypeStruct((places.y, *shape), jnp.float32)
    own, *sends = small_call(first_add_kernel, (own,) + (bf((places.y, *shape)),) * (places.x - 1), "add_c", 12, keep, got)
    got = [places.by_x(part, k + 1) for k, part in enumerate(sends)]
    nxt = jax.ShapeDtypeStruct((1, *shape), jnp.float32)
    own, *sends = pl.pallas_call(
        functools.partial(next_add_kernel, len(got), 1),
        out_shape=(nxt,) + (bf((1, *shape)),) * (places.y - 1),
        in_specs=[whole()] * (1 + len(got)) + [pl.BlockSpec(memory_space=pl.ANY)],
        compiler_params=pltpu.CompilerParams(vmem_limit_bytes=6 * MIB),
        name="add_x",
    )(own, *got, ahead)
    got = [places.by_y(part, k + 1) for k, part in enumerate(sends)]
    (mine,) = small_call(functools.partial(next_add_kernel, len(got), 0), (bf((1, *shape)),), "add_y", 4, own, *got)
    for bits in {1: (), 2: (1,), 4: (1, 3), 8: (1, 2, 6)}[places.z]:
        other = places.by_z(mine, bits)
        mine = small_call(pair_add_kernel, bf((1, *shape)), "add_z", 2, mine, other)
    parts = [mine] + [places.by_y(mine, -k) for k in range(1, places.y)]
    mine = pl.pallas_call(
        functools.partial(join_kernel, len(parts)),
        out_shape=bf((places.y, *shape)),
        in_specs=[whole()] * len(parts) + [pl.BlockSpec(memory_space=pl.ANY)] * len(behind),
        compiler_params=pltpu.CompilerParams(vmem_limit_bytes=4 * MIB),
        name="join",
    )(*parts, *behind)
    mine = [mine] + [places.by_x(mine, -k) for k in range(1, places.x)]
    return mine, [places.by_c(part) for part in mine]


def ring(array, lat, lon):
    n_lat, n_lon = lax.axis_size("lat"), lax.axis_size("lon")
    pairs = [
        (i * n_lon + j, (i + lat) % n_lat * n_lon + (j + lon) % n_lon) for i in range(n_lat) for j in range(n_lon)
    ]
    return lax.ppermute(array, ("lat", "lon"), pairs)


def local(saved_state, cotangent, row_mask, shifts, norm_gain, w_qkv, w_out, bias_table):
    n_rows, n_cols, n_chan = saved_state.shape
    n_head = bias_table.shape[0]
    n_proj = w_qkv.shape[1]
    n_tok = n_rows // 2 * n_cols
    n_top = WINDOW - 1
    places = Places()
    counts = (places.c, places.x, places.y)
    bf, f32 = jnp.bfloat16, jnp.float32

    smem = pl.BlockSpec(memory_space=pltpu.SMEM)
    tile = functools.partial(jax.ShapeDtypeStruct, dtype=bf)
    side, top_x, top_c, corner = pl.pallas_call(
        functools.partial(pack_kernel, n_top),
        out_shape=(
            tile((2, n_rows, WINDOW, n_chan)),
            tile((n_top, n_cols, n_chan)),
            tile((n_top, n_cols, n_chan)),
            tile((2, WINDOW, WINDOW, n_chan)),
        ),
        in_specs=[pl.BlockSpec(memory_space=pltpu.HBM), pl.BlockSpec(memory_space=pltpu.HBM), smem],
        out_specs=(whole(), pl.BlockSpec(memory_space=pl.ANY), pl.BlockSpec(memory_space=pl.ANY), whole()),
        scratch_shapes=[pltpu.VMEM((2, n_rows, 2 * WINDOW, n_chan), bf), pltpu.SemaphoreType.DMA((4,))],
        compiler_params=pltpu.CompilerParams(vmem_limit_bytes=58 * MIB),
        name="pack",
    )(saved_state, cotangent, row_mask)
    side = ring(side, 0, 1)
    top_x = ring(top_x, 1, 0)
    half_way = places.first_half_way(top_c)
    corner = ring(corner, 1, 1)
    at = jnp.stack(places.mine()).astype(jnp.int32)
    gain = norm_gain.reshape(1, n_chan)
    bias, w_t = pl.pallas_call(
        prepare_kernel,
        out_shape=(jax.ShapeDtypeStruct((n_head, CELLS, LANES), f32), tile((n_proj, n_chan))),
        compiler_params=pltpu.CompilerParams(vmem_limit_bytes=16 * MIB),
        cost_estimate=pl.CostEstimate(flops=10**9, bytes_accessed=4 * MIB, transcendentals=0),
        name="prepare",
    )(bias_table, w_qkv)

    def work(tokens):
        return [
            pltpu.VMEM((tokens, n_chan), bf),
            pltpu.VMEM((n_chan, tokens), bf),
            pltpu.VMEM((n_chan, tokens), bf),
        ], [
            pltpu.VMEM((tokens, n_chan), f32),
            pltpu.VMEM((tokens, n_chan), f32),
            pltpu.VMEM((n_proj, tokens), bf),
            pltpu.VMEM((tokens, 2 * n_chan), bf),
            pltpu.VMEM((n_chan, tokens), bf),
        ]

    below = jnp.minimum(lax.axis_index("lat"), 1).astype(jnp.int32).reshape(1)
    meta = jnp.concatenate([shifts, at, below, row_mask])
    n_half = n_tok // 2

    def inner(name, *more):
        left = len(more) > 1
        first, second = work(n_half)
        return pl.pallas_call(
            functools.partial(inner_kernel, n_head, left),
            out_shape=(
                tile((n_half, n_chan)),
                tile((n_proj, n_half)),
                jax.ShapeDtypeStruct((n_chan, n_proj + n_chan), f32),
                jax.ShapeDtypeStruct((n_head, CELLS, LANES), f32),
            ),
            in_specs=[smem] + [whole()] * (6 + len(more)) + [pl.BlockSpec(memory_space=pl.ANY)],
            scratch_shapes=first + second,
            compiler_params=pltpu.CompilerParams(vmem_limit_bytes=20 * MIB),
            cost_estimate=pl.CostEstimate(flops=10**8 if left else 10**10, bytes_accessed=MIB, transcendentals=0),
            name=name,
        )(meta, saved_state, cotangent, bias, gain, w_t, w_qkv, w_out, *more)

    x_right, gp_right, sums_in, bsum_in = inner("inner_right", side)
    half_way = after(half_way, x_right)
    top_c = places.second_half_way(half_way)
    x_left, gp_left, sums_in, bsum_in = inner("inner_left", side, sums_in, bsum_in, half_way)

    width = n_proj + n_chan + LANES
    rows = n_chan // math.prod(counts)
    half = math.prod(counts) // 2
    x_out, gp_out, keep, send = pl.pallas_call(
        functools.partial(outer_kernel, n_head, counts),
        out_shape=(
            tile((n_tok, n_chan)),
            tile((n_proj, n_tok)),
            jax.ShapeDtypeStruct((half, rows, width), f32),
            tile((half, rows, width)),
        ),
        in_specs=[smem] + [whole()] * 13,
        scratch_shapes=[
            *work(n_tok)[0],
            pltpu.VMEM((n_head, CELLS, LANES), f32),
            *work(n_tok)[1],
            pltpu.VMEM((n_chan, width), f32),
            pltpu.VMEM((n_head * CELLS, LANES), f32),
            pltpu.VMEM((n_head * CELLS, LANES), f32),
        ],
        compiler_params=pltpu.CompilerParams(vmem_limit_bytes=30 * MIB),
        cost_estimate=pl.CostEstimate(flops=10**10, bytes_accessed=24 * MIB, transcendentals=2**19),
        name="outer",
    )(meta, saved_state, cotangent, side, top_x, top_c, corner, bias, gain, w_t, w_qkv, w_out, sums_in, bsum_in)

    base, *edges = pl.pallas_call(
        cells_kernel,
        out_shape=(
            tile((n_rows, n_cols, n_chan)),
            tile((n_top, n_cols, n_chan)),
            tile((n_rows, WINDOW, n_chan)),
            tile((n_top, WINDOW, n_chan)),
        ),
        in_specs=[smem] + [whole()] * 9,
        scratch_shapes=[pltpu.VMEM((n_rows + WINDOW, n_cols + WINDOW, n_chan), f32)],
        compiler_params=pltpu.CompilerParams(vmem_limit_bytes=24 * MIB),
        cost_estimate=pl.CostEstimate(flops=16 * 10**8, bytes_accessed=12 * MIB, transcendentals=0),
        name="cells",
    )(meta, x_left, x_right, x_out, gp_left, gp_right, gp_out, cotangent, gain, w_qkv)
    top_back, side_back, corner_back = ring(edges[0], -1, 0), ring(edges[1], 0, -1), ring(edges[2], -1, -1)
    mine, other = total_over_devices(places, keep, send, edges[2], (top_back, side_back, corner_back))
    edge = jnp.pad(top_back, ((n_rows - n_top, 0), (0, 0), (0, 0)))
    edge = edge + jnp.pad(side_back, ((0, 0), (n_cols - WINDOW, 0), (0, 0)))
    edge = edge + jnp.pad(corner_back, ((n_rows - n_top, 0), (n_cols - WINDOW, 0), (0, 0)))
    state_grad = (base.astype(f32) + edge.astype(f32)).astype(bf)

    factor = 1.0 / math.sqrt(n_rows * places.n_lat * n_cols * places.n_lon)
    qkv_grad, out_grad, gain_grad, bias_grad = pl.pallas_call(
        functools.partial(unpack_kernel, counts, n_proj, factor),
        out_shape=(
            jax.ShapeDtypeStruct((n_chan, n_proj), f32),
            jax.ShapeDtypeStruct((n_chan, n_chan), f32),
            jax.ShapeDtypeStruct((1, n_chan), f32),
            jax.ShapeDtypeStruct(bias_table.shape, f32),
        ),
        in_specs=[smem] + [whole()] * (2 * places.x),
        scratch_shapes=[pltpu.VMEM((n_chan, LANES), f32)],
        compiler_params=pltpu.CompilerParams(vmem_limit_bytes=16 * MIB),
        name="unpack",
    )(meta, *mine, *other)
    return state_grad, qkv_grad, out_grad, gain_grad.reshape(n_chan), bias_grad


def solution(mesh):
    return jax.shard_map(
        local,
        mesh=mesh,
        in_specs=(P("lat", "lon", None), P("lat", "lon", None), P("lat"), P(), P(), P(), P(), P()),
        out_specs=(P("lat", "lon", None), P(), P(), P(), P()),
        check_vma=False,
    )
```

```python
import functools
import itertools
import math

import jax
import jax.numpy as jnp
from jax import lax
from jax.experimental import pallas as pl
from jax.experimental.pallas import tpu as pltpu
from jax.sharding import PartitionSpec as P

EPSILON = 1e-05


NT = (((1,), (1,)), ((), ()))
NN = (((1,), (0,)), ((), ()))
LANES = 128
WINDOW = 8
CELLS = WINDOW * WINDOW
TOKENS = 256
MIB = 1024 * 1024


def dot(a, b, dims=NN):
    return lax.dot_general(a, b, dims, preferred_element_type=jnp.float32)


def whole(*_):
    return pl.BlockSpec(memory_space=pltpu.VMEM)


def norm_stats(x):
    cen = x - jnp.mean(x, -1, keepdims=True)
    inv = lax.rsqrt(jnp.mean(cen * cen, -1, keepdims=True) + EPSILON)
    return cen * inv, inv


def project_cells(scale, gain, wt_ref, w_ref, xf, x_out, nrm_t, proj_t, kv):
    n_tok, n_chan = xf.shape
    x_out[...] = xf[...].astype(jnp.bfloat16)
    for base in range(0, n_tok, TOKENS):
        rows = slice(base, base + TOKENS)
        x_hat, _ = norm_stats(xf[rows])
        normed_f = x_hat * gain
        normed = normed_f.astype(jnp.bfloat16)
        nrm_t[:, rows] = normed_f.T.astype(jnp.bfloat16)
        proj_t[:n_chan, rows] = (dot(wt_ref[:n_chan], normed, NT) * scale).astype(jnp.bfloat16)
        proj_t[n_chan:, rows] = dot(wt_ref[n_chan:], normed, NT).astype(jnp.bfloat16)
        kv[rows] = dot(normed, w_ref[:, n_chan:]).astype(jnp.bfloat16)


def block_diag(block, step):
    blank = jnp.zeros((step, block.shape[1]), block.dtype)
    count = block.shape[0] // step
    columns = []
    for h in range(count):
        parts = [blank] * count
        parts[h] = block[h * step : (h + 1) * step]
        columns.append(jnp.concatenate(parts, 0))
    return jnp.concatenate(columns, 1)


def attention_unit(n_chan, dim, scale, bias_ref, mask, proj_t, kv, gm_t, mix_t, gp_t, bsum_ref, pair, group):
    lanes = pl.ds(pl.multiple_of(pair * LANES, LANES), LANES)
    c0 = group * LANES
    q_t = proj_t[pl.ds(c0, LANES), lanes]
    k_t = proj_t[pl.ds(n_chan + c0, LANES), lanes]
    v_t = proj_t[pl.ds(2 * n_chan + c0, LANES), lanes]
    g_t = gm_t[pl.ds(c0, LANES), lanes]
    k_tok = kv[lanes, pl.ds(c0, LANES)]
    v_tok = kv[lanes, pl.ds(n_chan + c0, LANES)]
    scores = dot(k_tok, block_diag(q_t, dim))
    grads = dot(v_tok, block_diag(g_t, dim))
    first = lax.broadcasted_iota(jnp.int32, (CELLS, LANES), 1) < CELLS
    heads = LANES // dim
    mixed, dq, dk, dv = [], [], [], []
    for h in range(heads):
        cut = slice(h * LANES, (h + 1) * LANES)
        rows = slice(h * dim, (h + 1) * dim)
        head = group * heads + h
        s = jnp.where(first, scores[:CELLS, cut], scores[CELLS:, cut]) + bias_ref[head] + mask
        e = jnp.exp(s - jnp.max(s, 0, keepdims=True))
        a = e * (1.0 / jnp.sum(e, 0, keepdims=True))
        d = jnp.where(first, grads[:CELLS, cut], grads[CELLS:, cut])
        ad = a * d
        ds = ad - a * jnp.sum(ad, 0, keepdims=True)
        bsum_ref[head] += ds
        zero = jnp.zeros_like(a)
        a2 = jnp.concatenate([jnp.where(first, a, zero), jnp.where(first, zero, a)], 0).astype(jnp.bfloat16)
        ds2 = jnp.concatenate([jnp.where(first, ds, zero), jnp.where(first, zero, ds)], 0).astype(jnp.bfloat16)
        mixed.append(dot(v_t[rows], a2))
        dv.append(dot(g_t[rows], a2, NT))
        dq.append(dot(k_t[rows], ds2) * scale)
        dk.append(dot(q_t[rows], ds2, NT))
    mix_t[pl.ds(c0, LANES), lanes] = jnp.concatenate(mixed, 0).astype(jnp.bfloat16)
    gp_t[pl.ds(c0, LANES), lanes] = jnp.concatenate(dq, 0).astype(jnp.bfloat16)
    gp_t[pl.ds(n_chan + c0, LANES), lanes] = jnp.concatenate(dk, 0).astype(jnp.bfloat16)
    gp_t[pl.ds(2 * n_chan + c0, LANES), lanes] = jnp.concatenate(dv, 0).astype(jnp.bfloat16)


def place_row(line, shift, out, r, live=None):
    line = line.astype(jnp.float32).reshape(-1, WINDOW, line.shape[1])
    if live is not None:
        line = line * live
    line = pltpu.roll(line, WINDOW - shift, 1)
    head = lax.broadcasted_iota(jnp.int32, line.shape[1:], 0) < WINDOW - shift
    for w in range(line.shape[0] - 1):
        start = w * CELLS + r * WINDOW
        out[start : start + WINDOW] = jnp.where(head, line[w], line[w + 1])


def window_row(n_head, cf, live, wo_ref, bias_ref, go_ref, mix_t, gp_t, bsum_ref, proj_t, kv, gm_t):
    n_tok, n_chan = cf.shape
    dim = n_chan // n_head
    scale = dim ** (-0.5)
    go_ref[...] = cf[...].astype(jnp.bfloat16)
    for base in range(0, n_tok, TOKENS):
        rows = slice(base, base + TOKENS)
        gm_t[:, rows] = dot(wo_ref[...], go_ref[rows], NT).astype(jnp.bfloat16)
    mask = jnp.concatenate([(live[r][:, :LANES] - 1.0) * 1e30 for r in range(WINDOW)], 0)
    groups = n_chan // LANES

    @pl.loop(0, n_tok // LANES)
    def _(pair):
        for group in range(groups):
            attention_unit(n_chan, dim, scale, bias_ref, mask, proj_t, kv, gm_t, mix_t, gp_t, bsum_ref, pair, group)


def weight_sums(sums, nrm_t, gp_t, mix_t, go_ref, more):
    n_proj, n_chan = gp_t.shape[0], nrm_t.shape[0]
    for base in range(0, n_proj + n_chan, TOKENS):
        cols = slice(base, base + TOKENS)
        if base < n_proj:
            part = dot(nrm_t[...], gp_t[cols], NT)
        else:
            part = dot(mix_t[...], go_ref[:, base - n_proj : base - n_proj + TOKENS])
        sums[:, cols] = part if more is None else part + more[:, cols]


def inner_kernel(n_head, meta, x_ref, cot_ref, side_ref, bias_ref, gain_ref, wt_ref, w_ref, wo_ref,
                 x_out, gp_t, sums_ref, bsum_ref, go_ref, nrm_t, mix_t, xf, cf, proj_t, kv, gm_t):
    scale = (x_ref.shape[2] // n_head) ** (-0.5)
    lat, lon = meta[0], meta[1]
    live = []
    for r in range(WINDOW):
        live.append(jnp.full((WINDOW, x_ref.shape[2]), meta[6 + lat + r].astype(jnp.float32)))
        for k, (grid, out) in enumerate(((x_ref, xf), (cot_ref, cf))):
            line = jnp.concatenate([part.astype(jnp.float32) for part in (side_ref[k, lat + r], grid[lat + r])], 0)
            place_row(line, lon, out, r, live[r] if k else None)
    bsum_ref[...] = jnp.zeros_like(bsum_ref)
    project_cells(scale, gain_ref[...], wt_ref, w_ref, xf, x_out, nrm_t, proj_t, kv)
    window_row(n_head, cf, live, wo_ref, bias_ref, go_ref, mix_t, gp_t, bsum_ref, proj_t, kv, gm_t)
    weight_sums(sums_ref, nrm_t, gp_t, mix_t, go_ref, None)


def outer_line(k, e, grid, side_ref, top, corner_ref):
    n_top = top.shape[0]
    above = e < WINDOW
    up = jnp.clip(e - (WINDOW - n_top), 0, n_top - 1)
    own = jnp.maximum(e - WINDOW, 0)
    parts = jnp.where(above, corner_ref[k, up], side_ref[k, own]), jnp.where(above, top[up], grid[own])
    return jnp.concatenate([part.astype(jnp.float32) for part in parts], 0)


def front_kernel(n_head, meta, x_ref, side_ref, top, corner_ref, gain_ref, wt_ref, w_ref, _, x_out, nrm_t, proj_t, kv, xf):
    scale = (x_ref.shape[2] // n_head) ** (-0.5)
    for r in range(WINDOW):
        place_row(outer_line(0, meta[0] + r, x_ref, side_ref, top, corner_ref), meta[1], xf, r)
    project_cells(scale, gain_ref[...], wt_ref, w_ref, xf, x_out, nrm_t, proj_t, kv)


def outer_kernel(n_head, counts, meta, cot_ref, side_ref, top, corner_ref, bias_ref, gain_ref, w_ref, wo_ref,
                 nrm_t, proj_t, kv, sums_in, bsum_in,
                 gp_t, keep_ref, send_ref,
                 go_ref, mix_t, bsum_ref, cf, gm_t, sums, spread_a, spread_b):
    n_chan = gain_ref.shape[1]
    up_mask = corner_ref[0, WINDOW - 1].astype(jnp.float32) * meta[5].astype(jnp.float32)
    line_of = lax.broadcasted_iota(jnp.int32, up_mask.shape, 0)
    live = []
    for r in range(WINDOW):
        e = meta[0] + r
        row_live = jnp.full((WINDOW, n_chan), meta[6 + jnp.maximum(e - WINDOW, 0)].astype(jnp.float32))
        up_live = jnp.sum(jnp.where(line_of == e, up_mask, 0.0), 0, keepdims=True)
        live.append(jnp.where(e < WINDOW, jnp.broadcast_to(up_live, row_live.shape), row_live))
        place_row(outer_line(1, e, cot_ref, side_ref, top, corner_ref), meta[1], cf, r, live[r])
    bsum_ref[...] = bsum_in[...]
    window_row(n_head, cf, live, wo_ref, bias_ref, go_ref, mix_t, gp_t, bsum_ref, proj_t, kv, gm_t)

    n_proj = 3 * n_chan
    weight_sums(sums, nrm_t, gp_t, mix_t, go_ref, sums_in)
    gain_sum = jnp.sum(sums[:, :n_proj] * w_ref[...].astype(jnp.float32), 1, keepdims=True)

    width = 2 * LANES
    cell = lax.broadcasted_iota(jnp.int32, (LANES, width), 0) % CELLS
    lane = lax.broadcasted_iota(jnp.int32, (LANES, width), 1)
    place = (cell // WINDOW) * 16 + cell % WINDOW + 119
    onehot = (lane == place).astype(jnp.float32).astype(jnp.bfloat16)
    flat = bsum_ref[...].reshape(n_head * CELLS, LANES)
    high = flat.astype(jnp.bfloat16)
    low = (flat - high.astype(jnp.float32)).astype(jnp.bfloat16)
    spread = dot(high, onehot) + dot(low, onehot)
    spread_a[...] = spread[:, :LANES]
    spread_b[...] = spread[:, LANES:]
    bias_sum = jnp.zeros((n_head, width), jnp.float32)
    for j in range(CELLS):
        row = jnp.concatenate([ref[pl.ds(j, n_head, stride=CELLS), :] for ref in (spread_a, spread_b)], 1)
        by = (j // WINDOW) * 16 + j % WINDOW
        bias_sum += pltpu.roll(row, width - by, 1) if by else row
    tail = lax.broadcasted_iota(jnp.int32, (n_chan, LANES), 1) == LANES - 1
    bias_rows = jnp.concatenate(
        [bias_sum[:, :LANES], bias_sum[:, LANES:], jnp.zeros((n_chan - 2 * n_head, LANES), jnp.float32)], 0
    )
    sums[:, n_proj + n_chan :] = jnp.where(tail, gain_sum * (1.0 / gain_col(gain_ref)), bias_rows)

    n_c, n_x, n_y = counts
    rows = n_chan // (n_c * n_x * n_y)
    for c in range(n_c):
        for x in range(n_x):
            for y in range(n_y):
                chunk = sums[((c * n_x + x) * n_y + y) * rows : ((c * n_x + x) * n_y + y + 1) * rows]
                at = lax.rem(x - meta[3] + n_x, n_x) * n_y + lax.rem(y - meta[4] + n_y, n_y)

                @pl.when(meta[2] == c)
                def _():
                    keep_ref[at] = chunk

                @pl.when(meta[2] != c)
                def _():
                    send_ref[at] = chunk.astype(jnp.bfloat16)


def gain_col(gain_ref):
    n_chan = gain_ref.shape[1]
    return jnp.broadcast_to(gain_ref[...], (LANES, n_chan)).T[:, :1]


def cells_kernel(meta, xi_ref, xo_ref, gpi_ref, gpo_ref, cot_ref, gain_ref, w_ref, base_ref, top_ref, side_ref, corner_ref, ext):
    n_rows, n_cols, n_chan = cot_ref.shape
    lat, lon = meta[0], meta[1]
    ext[...] = jnp.zeros_like(ext)
    for part, (x_ref, gp_t) in enumerate(((xo_ref, gpo_ref), (xi_ref, gpi_ref))):
        n_tok = x_ref.shape[0]
        cells = []
        for base in range(0, n_tok, TOKENS):
            rows = slice(base, base + TOKENS)
            x_hat, inv = norm_stats(x_ref[rows].astype(jnp.float32))
            g = dot(w_ref[...], gp_t[:, rows]).T * gain_ref[...]
            cells.append(inv * (g - jnp.mean(g, -1, keepdims=True) - x_hat * jnp.mean(g * x_hat, -1, keepdims=True)))
        blank = jnp.zeros((1, WINDOW, n_chan), jnp.float32)
        head = lax.broadcasted_iota(jnp.int32, (WINDOW, n_chan), 0) < lon
        for r in range(WINDOW):
            row = jnp.stack(
                [
                    cells[w * CELLS // TOKENS][w * CELLS % TOKENS + r * WINDOW :][:WINDOW]
                    for w in range(n_tok // CELLS)
                ],
                0,
            )
            row = jnp.concatenate([blank, pltpu.roll(row, lon, 1), blank], 0)
            for t in range(row.shape[0] - 1):
                ext[lat + part * WINDOW + r, t * WINDOW : (t + 1) * WINDOW, :] = jnp.where(head, row[t], row[t + 1])
    for r in range(n_rows):
        base_ref[r] = (cot_ref[r].astype(jnp.float32) + ext[WINDOW + r, WINDOW:]).astype(jnp.bfloat16)
        side_ref[r] = ext[WINDOW + r, :WINDOW].astype(jnp.bfloat16)
    n_top = top_ref.shape[0]
    for r in range(n_top):
        top_ref[r] = ext[WINDOW - n_top + r, WINDOW:].astype(jnp.bfloat16)
        corner_ref[r] = ext[WINDOW - n_top + r, :WINDOW].astype(jnp.bfloat16)


def prepare_kernel(bias_ref, w_ref, full_ref, wt_ref):
    n_head, n_gap = bias_ref.shape
    span = 2 * WINDOW - 1
    width = 2 * LANES
    lane = lax.broadcasted_iota(jnp.int32, (width, LANES), 0)
    cell = lax.broadcasted_iota(jnp.int32, (width, LANES), 1) % CELLS
    place = cell // WINDOW * span + cell % WINDOW + n_gap // 2
    onehot = (lane == place).astype(jnp.float32).astype(jnp.bfloat16)
    table = jnp.concatenate([bias_ref[...], jnp.zeros((n_head, width - n_gap), jnp.float32)], 1)
    for h in range(n_head):
        line = jnp.broadcast_to(table[h : h + 1], (WINDOW, width))
        rows = [pltpu.roll(line, r * span, 1, stride=1, stride_axis=0) for r in range(WINDOW)]
        rest = jnp.concatenate(rows, 0)
        total = jnp.zeros((CELLS, LANES), jnp.float32)
        for _ in range(3):
            part = rest.astype(jnp.bfloat16)
            total += dot(part, onehot)
            rest = rest - part.astype(jnp.float32)
        full_ref[h] = total
    wt_ref[...] = w_ref[...].T


def pack_kernel(n_top, x_ref, cot_ref, mask, side_ref, top_x, top_c, corner_ref, edges, sems):
    n_rows, n_cols, n_chan = x_ref.shape
    copies = []
    for k, (ref, top) in enumerate(((x_ref, top_x), (cot_ref, top_c))):
        copies.append(pltpu.make_async_copy(ref.at[:, pl.ds(n_cols - 2 * WINDOW, 2 * WINDOW)], edges.at[k], sems.at[2 * k]))
        copies.append(pltpu.make_async_copy(ref.at[pl.ds(n_rows - n_top, n_top)], top, sems.at[2 * k + 1]))
    for copy in copies:
        copy.start()
    for k in range(2):
        copies[2 * k].wait()
        for r in range(n_rows):
            edge = edges[k, r][WINDOW:]
            side_ref[k, r] = edge
            at = r - n_rows + n_top
            if at >= 0:
                corner_ref[k, at] = edge
    line = lax.broadcasted_iota(jnp.int32, (WINDOW, n_chan), 0)
    live = jnp.zeros((WINDOW, n_chan), jnp.float32)
    for r in range(WINDOW):
        live = jnp.where(line == r, mask[n_rows - WINDOW + r].astype(jnp.float32), live)
    corner_ref[0, n_top] = live.astype(jnp.bfloat16)
    corner_ref[1, n_top] = live.astype(jnp.bfloat16)
    copies[1].wait()
    copies[3].wait()


def first_add_kernel(keep_ref, got_ref, own_ref, *send_refs):
    size = own_ref.shape[0]
    for k in range(len(send_refs) + 1):
        cut = slice(k * size, (k + 1) * size)
        total = keep_ref[cut] + got_ref[cut].astype(jnp.float32)
        if k:
            send_refs[k - 1][...] = total.astype(jnp.bfloat16)
        else:
            own_ref[...] = total


def next_add_kernel(n_got, n_more, own_ref, *refs):
    got, (out_ref, *send_refs) = refs[:n_got], refs[n_got + n_more :]
    size = out_ref.shape[0]
    for k in range(len(send_refs) + 1):
        cut = slice(k * size, (k + 1) * size)
        total = own_ref[cut]
        for ref in got:
            total = total + ref[cut].astype(jnp.float32)
        if k:
            send_refs[k - 1][...] = total.astype(jnp.bfloat16)
        else:
            out_ref[...] = total.astype(out_ref.dtype)


def join_kernel(n_got, *refs):
    for k in range(n_got):
        refs[-1][k : k + 1] = refs[k][...]


def pair_add_kernel(a_ref, b_ref, *refs):
    refs[-1][...] = (a_ref[...].astype(jnp.float32) + b_ref[...].astype(jnp.float32)).astype(jnp.bfloat16)


def unpack_kernel(counts, n_proj, factor, meta, *refs):
    n_c, n_x, n_y = counts
    mine, other = refs[:n_x], refs[n_x : 2 * n_x]
    qkv_ref, out_ref, gain_ref, bias_ref, small = refs[2 * n_x :]
    rows = mine[0].shape[1]
    n_chan = out_ref.shape[1]
    for half in range(2):
        c = meta[2] if half == 0 else 1 - meta[2]
        for k, ref in enumerate(other if half else mine):
            x = lax.rem(meta[3] + k, n_x)
            for j in range(n_y):
                y = lax.rem(meta[4] + j, n_y)
                chunk = ref[j].astype(jnp.float32) * factor
                to = pl.ds(pl.multiple_of(((c * n_x + x) * n_y + y) * rows, rows), rows)
                qkv_ref[to] = chunk[:, :n_proj]
                out_ref[to] = chunk[:, n_proj : n_proj + n_chan]
                small[to] = chunk[:, n_proj + n_chan :]
    gain_ref[...] = small[...].T[LANES - 1 :]
    n_head, n_gap = bias_ref.shape
    span = 2 * WINDOW - 1
    wide = jnp.concatenate([small[:n_head], small[n_head : 2 * n_head]], 1)
    lane = lax.broadcasted_iota(jnp.int32, wide.shape, 1)
    bias = jnp.zeros_like(wide)
    for k in range(span):
        moved = pltpu.roll(wide, 2 * LANES - k, 1) if k else wide
        bias = jnp.where((lane >= k * span) & (lane < (k + 1) * span), moved, bias)
    bias_ref[...] = bias[:, :n_gap]


class Places:
    def __init__(self):
        self.n_lat, self.n_lon = lax.axis_size("lat"), lax.axis_size("lon")
        self.c = 2
        self.x = min(4, self.n_lon // self.c)
        self.y_low = self.n_lon // (self.c * self.x)
        self.y_high = 2
        self.y = self.y_low * self.y_high
        self.z = self.n_lat // self.y_high

    def index(self, z, y, x, c):
        high, low = divmod(y, self.y_low)
        return (z * self.y_high + high) * self.n_lon + (low * self.x + x) * self.c + c

    def mine(self):
        lat, lon = lax.axis_index("lat"), lax.axis_index("lon")
        return (
            lon % self.c,
            lon // self.c % self.x,
            lat % self.y_high * self.y_low + lon // (self.c * self.x),
        )

    def move(self, array, to):
        every = itertools.product(range(self.z), range(self.y), range(self.x), range(self.c))
        pairs = [(self.index(*at), self.index(*to(*at))) for at in every]
        return lax.ppermute(array, ("lat", "lon"), pairs)

    def by_c(self, array):
        return self.move(array, lambda z, y, x, c: (z, y, x, 1 - c))

    def by_x(self, array, k):
        return self.move(array, lambda z, y, x, c: (z, y, (x + k) % self.x, c))

    def by_y(self, array, k):
        return self.move(array, lambda z, y, x, c: (z, (y + k) % self.y, x, c))

    def by_z(self, array, bits):
        return self.move(array, lambda z, y, x, c: (z ^ bits, y, x, c))


def small_call(kernel, outs, name, limit, *args):
    return pl.pallas_call(
        kernel,
        out_shape=outs,
        compiler_params=pltpu.CompilerParams(vmem_limit_bytes=limit * MIB),
        name=name,
    )(*args)


def total_over_devices(places, keep, send, ahead, behind):
    shape = keep.shape[1:]
    bf = functools.partial(jax.ShapeDtypeStruct, dtype=jnp.bfloat16)
    got = places.by_c(send)
    own = jax.ShapeDtypeStruct((places.y, *shape), jnp.float32)
    own, *sends = small_call(first_add_kernel, (own,) + (bf((places.y, *shape)),) * (places.x - 1), "add_c", 12, keep, got)
    got = [places.by_x(part, k + 1) for k, part in enumerate(sends)]
    nxt = jax.ShapeDtypeStruct((1, *shape), jnp.float32)
    own, *sends = pl.pallas_call(
        functools.partial(next_add_kernel, len(got), 1),
        out_shape=(nxt,) + (bf((1, *shape)),) * (places.y - 1),
        in_specs=[whole()] * (1 + len(got)) + [pl.BlockSpec(memory_space=pl.ANY)],
        compiler_params=pltpu.CompilerParams(vmem_limit_bytes=6 * MIB),
        name="add_x",
    )(own, *got, ahead)
    got = [places.by_y(part, k + 1) for k, part in enumerate(sends)]
    (mine,) = small_call(functools.partial(next_add_kernel, len(got), 0), (bf((1, *shape)),), "add_y", 4, own, *got)
    for bits in {1: (), 2: (1,), 4: (1, 3), 8: (1, 2, 6)}[places.z]:
        other = places.by_z(mine, bits)
        mine = small_call(pair_add_kernel, bf((1, *shape)), "add_z", 2, mine, other)
    parts = [mine] + [places.by_y(mine, -k) for k in range(1, places.y)]
    mine = pl.pallas_call(
        functools.partial(join_kernel, len(parts)),
        out_shape=bf((places.y, *shape)),
        in_specs=[whole()] * len(parts) + [pl.BlockSpec(memory_space=pl.ANY)] * len(behind),
        compiler_params=pltpu.CompilerParams(vmem_limit_bytes=4 * MIB),
        name="join",
    )(*parts, *behind)
    mine = [mine] + [places.by_x(mine, -k) for k in range(1, places.x)]
    return mine, [places.by_c(part) for part in mine]


def ring(array, lat, lon):
    n_lat, n_lon = lax.axis_size("lat"), lax.axis_size("lon")
    pairs = [
        (i * n_lon + j, (i + lat) % n_lat * n_lon + (j + lon) % n_lon) for i in range(n_lat) for j in range(n_lon)
    ]
    return lax.ppermute(array, ("lat", "lon"), pairs)


def local(saved_state, cotangent, row_mask, shifts, norm_gain, w_qkv, w_out, bias_table):
    n_rows, n_cols, n_chan = saved_state.shape
    n_head = bias_table.shape[0]
    n_proj = w_qkv.shape[1]
    n_tok = n_rows // 2 * n_cols
    n_top = WINDOW - 1
    places = Places()
    counts = (places.c, places.x, places.y)
    bf, f32 = jnp.bfloat16, jnp.float32

    smem = pl.BlockSpec(memory_space=pltpu.SMEM)
    tile = functools.partial(jax.ShapeDtypeStruct, dtype=bf)
    side, top_x, top_c, corner = pl.pallas_call(
        functools.partial(pack_kernel, n_top),
        out_shape=(
            tile((2, n_rows, WINDOW, n_chan)),
            tile((n_top, n_cols, n_chan)),
            tile((n_top, n_cols, n_chan)),
            tile((2, WINDOW, WINDOW, n_chan)),
        ),
        in_specs=[pl.BlockSpec(memory_space=pltpu.HBM), pl.BlockSpec(memory_space=pltpu.HBM), smem],
        scratch_shapes=[pltpu.VMEM((2, n_rows, 2 * WINDOW, n_chan), bf), pltpu.SemaphoreType.DMA((4,))],
        compiler_params=pltpu.CompilerParams(vmem_limit_bytes=58 * MIB),
        name="pack",
    )(saved_state, cotangent, row_mask)
    side = ring(side, 0, 1)
    top_x = ring(top_x, 1, 0)
    top_c = ring(top_c, 1, 0)
    corner = ring(corner, 1, 1)
    at = jnp.stack(places.mine()).astype(jnp.int32)
    gain = norm_gain.reshape(1, n_chan)
    bias, w_t = pl.pallas_call(
        prepare_kernel,
        out_shape=(jax.ShapeDtypeStruct((n_head, CELLS, LANES), f32), tile((n_proj, n_chan))),
        compiler_params=pltpu.CompilerParams(vmem_limit_bytes=16 * MIB),
        cost_estimate=pl.CostEstimate(flops=10**9, bytes_accessed=4 * MIB, transcendentals=0),
        name="prepare",
    )(bias_table, w_qkv)

    below = jnp.minimum(lax.axis_index("lat"), 1).astype(jnp.int32).reshape(1)
    meta = jnp.concatenate([shifts, at, below, row_mask])
    cells_f, cells_t = pltpu.VMEM((n_tok, n_chan), f32), pltpu.VMEM((n_chan, n_tok), bf)
    x_in, gp_in, sums_in, bsum_in = pl.pallas_call(
        functools.partial(inner_kernel, n_head),
        out_shape=(
            tile((n_tok, n_chan)),
            tile((n_proj, n_tok)),
            jax.ShapeDtypeStruct((n_chan, n_proj + n_chan), f32),
            jax.ShapeDtypeStruct((n_head, CELLS, LANES), f32),
        ),
        in_specs=[smem] + [whole()] * 8,
        scratch_shapes=[
            pltpu.VMEM((n_tok, n_chan), bf),
            cells_t,
            cells_t,
            cells_f,
            cells_f,
            pltpu.VMEM((n_proj, n_tok), bf),
            pltpu.VMEM((n_tok, 2 * n_chan), bf),
            cells_t,
        ],
        compiler_params=pltpu.CompilerParams(vmem_limit_bytes=24 * MIB),
        cost_estimate=pl.CostEstimate(flops=8 * 10**9, bytes_accessed=16 * MIB, transcendentals=2**19),
        name="inner",
    )(meta, saved_state, cotangent, side, bias, gain, w_t, w_qkv, w_out)
    x_out, nrm_out, proj_out, kv_out = pl.pallas_call(
        functools.partial(front_kernel, n_head),
        out_shape=(tile((n_tok, n_chan)), tile((n_chan, n_tok)), tile((n_proj, n_tok)), tile((n_tok, 2 * n_chan))),
        in_specs=[smem] + [whole()] * 7 + [pl.BlockSpec(memory_space=pl.ANY)],
        scratch_shapes=[cells_f],
        compiler_params=pltpu.CompilerParams(vmem_limit_bytes=14 * MIB),
        cost_estimate=pl.CostEstimate(flops=3 * 10**9, bytes_accessed=8 * MIB, transcendentals=0),
        name="front",
    )(meta, saved_state, side, top_x, corner, gain, w_t, w_qkv, bsum_in)

    width = n_proj + n_chan + LANES
    rows = n_chan // math.prod(counts)
    half = math.prod(counts) // 2
    gp_out, keep, send = pl.pallas_call(
        functools.partial(outer_kernel, n_head, counts),
        out_shape=(
            tile((n_proj, n_tok)),
            jax.ShapeDtypeStruct((half, rows, width), f32),
            tile((half, rows, width)),
        ),
        in_specs=[smem] + [whole()] * 13,
        scratch_shapes=[
            pltpu.VMEM((n_tok, n_chan), bf),
            cells_t,
            pltpu.VMEM((n_head, CELLS, LANES), f32),
            cells_f,
            cells_t,
            pltpu.VMEM((n_chan, width), f32),
            pltpu.VMEM((n_head * CELLS, LANES), f32),
            pltpu.VMEM((n_head * CELLS, LANES), f32),
        ],
        compiler_params=pltpu.CompilerParams(vmem_limit_bytes=30 * MIB),
        cost_estimate=pl.CostEstimate(flops=10**10, bytes_accessed=24 * MIB, transcendentals=2**19),
        name="outer",
    )(meta, cotangent, side, top_c, corner, bias, gain, w_qkv, w_out, nrm_out, proj_out, kv_out, sums_in, bsum_in)

    base, *edges = pl.pallas_call(
        cells_kernel,
        out_shape=(
            tile((n_rows, n_cols, n_chan)),
            tile((n_top, n_cols, n_chan)),
            tile((n_rows, WINDOW, n_chan)),
            tile((n_top, WINDOW, n_chan)),
        ),
        in_specs=[smem] + [whole()] * 7,
        scratch_shapes=[pltpu.VMEM((n_rows + WINDOW, n_cols + WINDOW, n_chan), f32)],
        compiler_params=pltpu.CompilerParams(vmem_limit_bytes=24 * MIB),
        cost_estimate=pl.CostEstimate(flops=16 * 10**8, bytes_accessed=12 * MIB, transcendentals=0),
        name="cells",
    )(meta, x_in, x_out, gp_in, gp_out, cotangent, gain, w_qkv)
    top_back, side_back, corner_back = ring(edges[0], -1, 0), ring(edges[1], 0, -1), ring(edges[2], -1, -1)
    mine, other = total_over_devices(places, keep, send, edges[2], (top_back, side_back, corner_back))
    edge = jnp.pad(top_back, ((n_rows - n_top, 0), (0, 0), (0, 0)))
    edge = edge + jnp.pad(side_back, ((0, 0), (n_cols - WINDOW, 0), (0, 0)))
    edge = edge + jnp.pad(corner_back, ((n_rows - n_top, 0), (n_cols - WINDOW, 0), (0, 0)))
    state_grad = (base.astype(f32) + edge.astype(f32)).astype(bf)

    factor = 1.0 / math.sqrt(n_rows * places.n_lat * n_cols * places.n_lon)
    qkv_grad, out_grad, gain_grad, bias_grad = pl.pallas_call(
        functools.partial(unpack_kernel, counts, n_proj, factor),
        out_shape=(
            jax.ShapeDtypeStruct((n_chan, n_proj), f32),
            jax.ShapeDtypeStruct((n_chan, n_chan), f32),
            jax.ShapeDtypeStruct((1, n_chan), f32),
            jax.ShapeDtypeStruct(bias_table.shape, f32),
        ),
        in_specs=[smem] + [whole()] * (2 * places.x),
        scratch_shapes=[pltpu.VMEM((n_chan, LANES), f32)],
        compiler_params=pltpu.CompilerParams(vmem_limit_bytes=16 * MIB),
        name="unpack",
    )(meta, *mine, *other)
    return state_grad, qkv_grad, out_grad, gain_grad.reshape(n_chan), bias_grad


def solution(mesh):
    return jax.shard_map(
        local,
        mesh=mesh,
        in_specs=(P("lat", "lon", None), P("lat", "lon", None), P("lat"), P(), P(), P(), P(), P()),
        out_specs=(P("lat", "lon", None), P(), P(), P(), P()),
        check_vma=False,
    )
```

```python
import functools
import itertools
import math

import jax
import jax.numpy as jnp
from jax import lax
from jax.experimental import pallas as pl
from jax.experimental.pallas import tpu as pltpu
from jax.sharding import PartitionSpec as P

EPSILON = 1e-05


NT = (((1,), (1,)), ((), ()))
NN = (((1,), (0,)), ((), ()))
LANES = 128
WINDOW = 8
CELLS = WINDOW * WINDOW
TOKENS = 256
MIB = 1024 * 1024


def dot(a, b, dims=NN):
    return lax.dot_general(a, b, dims, preferred_element_type=jnp.float32)


def whole(*_):
    return pl.BlockSpec(memory_space=pltpu.VMEM)


def norm_stats(x):
    cen = x - jnp.mean(x, -1, keepdims=True)
    inv = lax.rsqrt(jnp.mean(cen * cen, -1, keepdims=True) + EPSILON)
    return cen * inv, inv


def project_cells(scale, gain, wt_ref, w_ref, xf, x_out, nrm_t, proj_t, kv):
    n_tok, n_chan = xf.shape
    x_out[...] = xf[...].astype(jnp.bfloat16)
    for base in range(0, n_tok, TOKENS):
        rows = slice(base, base + TOKENS)
        x_hat, _ = norm_stats(xf[rows])
        normed_f = x_hat * gain
        normed = normed_f.astype(jnp.bfloat16)
        nrm_t[:, rows] = normed_f.T.astype(jnp.bfloat16)
        proj_t[:n_chan, rows] = (dot(wt_ref[:n_chan], normed, NT) * scale).astype(jnp.bfloat16)
        proj_t[n_chan:, rows] = dot(wt_ref[n_chan:], normed, NT).astype(jnp.bfloat16)
        kv[rows] = dot(normed, w_ref[:, n_chan:]).astype(jnp.bfloat16)


def block_diag(block, step):
    blank = jnp.zeros((step, block.shape[1]), block.dtype)
    count = block.shape[0] // step
    columns = []
    for h in range(count):
        parts = [blank] * count
        parts[h] = block[h * step : (h + 1) * step]
        columns.append(jnp.concatenate(parts, 0))
    return jnp.concatenate(columns, 1)


def attention_unit(n_chan, dim, scale, bias_ref, mask, proj_t, kv, gm_t, mix_t, gp_t, bsum_ref, pair, group):
    lanes = pl.ds(pl.multiple_of(pair * LANES, LANES), LANES)
    c0 = group * LANES
    q_t = proj_t[pl.ds(c0, LANES), lanes]
    k_t = proj_t[pl.ds(n_chan + c0, LANES), lanes]
    v_t = proj_t[pl.ds(2 * n_chan + c0, LANES), lanes]
    g_t = gm_t[pl.ds(c0, LANES), lanes]
    k_tok = kv[lanes, pl.ds(c0, LANES)]
    v_tok = kv[lanes, pl.ds(n_chan + c0, LANES)]
    scores = dot(k_tok, block_diag(q_t, dim))
    grads = dot(v_tok, block_diag(g_t, dim))
    first = lax.broadcasted_iota(jnp.int32, (CELLS, LANES), 1) < CELLS
    heads = LANES // dim
    mixed, dq, dk, dv = [], [], [], []
    for h in range(heads):
        cut = slice(h * LANES, (h + 1) * LANES)
        rows = slice(h * dim, (h + 1) * dim)
        head = group * heads + h
        s = jnp.where(first, scores[:CELLS, cut], scores[CELLS:, cut]) + bias_ref[head] + mask
        e = jnp.exp(s - jnp.max(s, 0, keepdims=True))
        a = e * (1.0 / jnp.sum(e, 0, keepdims=True))
        d = jnp.where(first, grads[:CELLS, cut], grads[CELLS:, cut])
        ad = a * d
        ds = ad - a * jnp.sum(ad, 0, keepdims=True)
        bsum_ref[head] += ds
        zero = jnp.zeros_like(a)
        a2 = jnp.concatenate([jnp.where(first, a, zero), jnp.where(first, zero, a)], 0).astype(jnp.bfloat16)
        ds2 = jnp.concatenate([jnp.where(first, ds, zero), jnp.where(first, zero, ds)], 0).astype(jnp.bfloat16)
        mixed.append(dot(v_t[rows], a2))
        dv.append(dot(g_t[rows], a2, NT))
        dq.append(dot(k_t[rows], ds2) * scale)
        dk.append(dot(q_t[rows], ds2, NT))
    mix_t[pl.ds(c0, LANES), lanes] = jnp.concatenate(mixed, 0).astype(jnp.bfloat16)
    gp_t[pl.ds(c0, LANES), lanes] = jnp.concatenate(dq, 0).astype(jnp.bfloat16)
    gp_t[pl.ds(n_chan + c0, LANES), lanes] = jnp.concatenate(dk, 0).astype(jnp.bfloat16)
    gp_t[pl.ds(2 * n_chan + c0, LANES), lanes] = jnp.concatenate(dv, 0).astype(jnp.bfloat16)


def place_row(line, shift, out, r, live=None):
    line = line.astype(jnp.float32).reshape(-1, WINDOW, line.shape[1])
    if live is not None:
        line = line * live
    line = pltpu.roll(line, WINDOW - shift, 1)
    head = lax.broadcasted_iota(jnp.int32, line.shape[1:], 0) < WINDOW - shift
    for w in range(line.shape[0] - 1):
        start = w * CELLS + r * WINDOW
        out[start : start + WINDOW] = jnp.where(head, line[w], line[w + 1])


def window_row(n_head, cf, live, wo_ref, bias_ref, go_ref, mix_t, gp_t, bsum_ref, proj_t, kv, gm_t):
    n_tok, n_chan = cf.shape
    dim = n_chan // n_head
    scale = dim ** (-0.5)
    go_ref[...] = cf[...].astype(jnp.bfloat16)
    for base in range(0, n_tok, TOKENS):
        rows = slice(base, base + TOKENS)
        gm_t[:, rows] = dot(wo_ref[...], go_ref[rows], NT).astype(jnp.bfloat16)
    mask = jnp.concatenate([(live[r][:, :LANES] - 1.0) * 1e30 for r in range(WINDOW)], 0)
    groups = n_chan // LANES

    @pl.loop(0, n_tok // LANES)
    def _(pair):
        for group in range(groups):
            attention_unit(n_chan, dim, scale, bias_ref, mask, proj_t, kv, gm_t, mix_t, gp_t, bsum_ref, pair, group)


def weight_sums(sums, nrm_t, gp_t, mix_t, go_ref, more):
    n_proj, n_chan = gp_t.shape[0], nrm_t.shape[0]
    for base in range(0, n_proj + n_chan, TOKENS):
        cols = slice(base, base + TOKENS)
        if base < n_proj:
            part = dot(nrm_t[...], gp_t[cols], NT)
        else:
            part = dot(mix_t[...], go_ref[:, base - n_proj : base - n_proj + TOKENS])
        sums[:, cols] = part if more is None else part + more[:, cols]


def inner_kernel(n_head, meta, x_ref, cot_ref, side_ref, bias_ref, gain_ref, wt_ref, w_ref, wo_ref,
                 x_out, gp_t, sums_ref, bsum_ref, go_ref, nrm_t, mix_t, xf, cf, proj_t, kv, gm_t):
    scale = (x_ref.shape[2] // n_head) ** (-0.5)
    lat, lon = meta[0], meta[1]
    live = []
    for r in range(WINDOW):
        live.append(jnp.full((WINDOW, x_ref.shape[2]), meta[6 + lat + r].astype(jnp.float32)))
        for k, (grid, out) in enumerate(((x_ref, xf), (cot_ref, cf))):
            line = jnp.concatenate([part.astype(jnp.float32) for part in (side_ref[k, lat + r], grid[lat + r])], 0)
            place_row(line, lon, out, r, live[r] if k else None)
    bsum_ref[...] = jnp.zeros_like(bsum_ref)
    project_cells(scale, gain_ref[...], wt_ref, w_ref, xf, x_out, nrm_t, proj_t, kv)
    window_row(n_head, cf, live, wo_ref, bias_ref, go_ref, mix_t, gp_t, bsum_ref, proj_t, kv, gm_t)
    weight_sums(sums_ref, nrm_t, gp_t, mix_t, go_ref, None)


def outer_line(k, e, grid, side_ref, top, corner_ref):
    n_top = top.shape[0]
    above = e < WINDOW
    up = jnp.clip(e - (WINDOW - n_top), 0, n_top - 1)
    own = jnp.maximum(e - WINDOW, 0)
    parts = jnp.where(above, corner_ref[k, up], side_ref[k, own]), jnp.where(above, top[up], grid[own])
    return jnp.concatenate([part.astype(jnp.float32) for part in parts], 0)


def front_kernel(n_head, meta, x_ref, side_ref, top, corner_ref, gain_ref, wt_ref, w_ref, _, x_out, nrm_t, proj_t, kv, xf):
    scale = (x_ref.shape[2] // n_head) ** (-0.5)
    for r in range(WINDOW):
        place_row(outer_line(0, meta[0] + r, x_ref, side_ref, top, corner_ref), meta[1], xf, r)
    project_cells(scale, gain_ref[...], wt_ref, w_ref, xf, x_out, nrm_t, proj_t, kv)


def outer_kernel(n_head, counts, meta, cot_ref, side_ref, top, corner_ref, bias_ref, gain_ref, w_ref, wo_ref,
                 nrm_t, proj_t, kv, sums_in, bsum_in,
                 gp_t, keep_ref, send_ref,
                 go_ref, mix_t, bsum_ref, cf, gm_t, sums, spread_a, spread_b):
    n_chan = gain_ref.shape[1]
    up_mask = corner_ref[0, WINDOW - 1].astype(jnp.float32) * meta[5].astype(jnp.float32)
    line_of = lax.broadcasted_iota(jnp.int32, up_mask.shape, 0)
    live = []
    for r in range(WINDOW):
        e = meta[0] + r
        row_live = jnp.full((WINDOW, n_chan), meta[6 + jnp.maximum(e - WINDOW, 0)].astype(jnp.float32))
        up_live = jnp.sum(jnp.where(line_of == e, up_mask, 0.0), 0, keepdims=True)
        live.append(jnp.where(e < WINDOW, jnp.broadcast_to(up_live, row_live.shape), row_live))
        place_row(outer_line(1, e, cot_ref, side_ref, top, corner_ref), meta[1], cf, r, live[r])
    bsum_ref[...] = bsum_in[...]
    window_row(n_head, cf, live, wo_ref, bias_ref, go_ref, mix_t, gp_t, bsum_ref, proj_t, kv, gm_t)

    n_proj = 3 * n_chan
    weight_sums(sums, nrm_t, gp_t, mix_t, go_ref, sums_in)
    gain_sum = jnp.sum(sums[:, :n_proj] * w_ref[...].astype(jnp.float32), 1, keepdims=True)

    width = 2 * LANES
    cell = lax.broadcasted_iota(jnp.int32, (LANES, width), 0) % CELLS
    lane = lax.broadcasted_iota(jnp.int32, (LANES, width), 1)
    place = (cell // WINDOW) * 16 + cell % WINDOW + 119
    onehot = (lane == place).astype(jnp.float32).astype(jnp.bfloat16)
    flat = bsum_ref[...].reshape(n_head * CELLS, LANES)
    high = flat.astype(jnp.bfloat16)
    low = (flat - high.astype(jnp.float32)).astype(jnp.bfloat16)
    spread = dot(high, onehot) + dot(low, onehot)
    spread_a[...] = spread[:, :LANES]
    spread_b[...] = spread[:, LANES:]
    bias_sum = jnp.zeros((n_head, width), jnp.float32)
    for j in range(CELLS):
        row = jnp.concatenate([ref[pl.ds(j, n_head, stride=CELLS), :] for ref in (spread_a, spread_b)], 1)
        by = (j // WINDOW) * 16 + j % WINDOW
        bias_sum += pltpu.roll(row, width - by, 1) if by else row
    tail = lax.broadcasted_iota(jnp.int32, (n_chan, LANES), 1) == LANES - 1
    bias_rows = jnp.concatenate(
        [bias_sum[:, :LANES], bias_sum[:, LANES:], jnp.zeros((n_chan - 2 * n_head, LANES), jnp.float32)], 0
    )
    sums[:, n_proj + n_chan :] = jnp.where(tail, gain_sum * (1.0 / gain_col(gain_ref)), bias_rows)

    n_c, n_x, n_y = counts
    rows = n_chan // (n_c * n_x * n_y)
    for c in range(n_c):
        for x in range(n_x):
            for y in range(n_y):
                chunk = sums[((c * n_x + x) * n_y + y) * rows : ((c * n_x + x) * n_y + y + 1) * rows]
                at = lax.rem(x - meta[3] + n_x, n_x) * n_y + lax.rem(y - meta[4] + n_y, n_y)

                @pl.when(meta[2] == c)
                def _():
                    keep_ref[at] = chunk

                @pl.when(meta[2] != c)
                def _():
                    send_ref[at] = chunk.astype(jnp.bfloat16)


def gain_col(gain_ref):
    n_chan = gain_ref.shape[1]
    return jnp.broadcast_to(gain_ref[...], (LANES, n_chan)).T[:, :1]


def cells_kernel(meta, xi_ref, xo_ref, gpi_ref, gpo_ref, cot_ref, gain_ref, w_ref, _, base_ref, top_ref, side_ref, ext):
    n_rows, n_cols, n_chan = cot_ref.shape
    lat, lon = meta[0], meta[1]
    ext[...] = jnp.zeros_like(ext)
    for part, (x_ref, gp_t) in enumerate(((xo_ref, gpo_ref), (xi_ref, gpi_ref))):
        n_tok = x_ref.shape[0]
        cells = []
        for base in range(0, n_tok, TOKENS):
            rows = slice(base, base + TOKENS)
            x_hat, inv = norm_stats(x_ref[rows].astype(jnp.float32))
            g = dot(w_ref[...], gp_t[:, rows]).T * gain_ref[...]
            cells.append(inv * (g - jnp.mean(g, -1, keepdims=True) - x_hat * jnp.mean(g * x_hat, -1, keepdims=True)))
        blank = jnp.zeros((1, WINDOW, n_chan), jnp.float32)
        head = lax.broadcasted_iota(jnp.int32, (WINDOW, n_chan), 0) < lon
        for r in range(WINDOW):
            row = jnp.stack(
                [
                    cells[w * CELLS // TOKENS][w * CELLS % TOKENS + r * WINDOW :][:WINDOW]
                    for w in range(n_tok // CELLS)
                ],
                0,
            )
            row = jnp.concatenate([blank, pltpu.roll(row, lon, 1), blank], 0)
            for t in range(row.shape[0] - 1):
                ext[lat + part * WINDOW + r, t * WINDOW : (t + 1) * WINDOW, :] = jnp.where(head, row[t], row[t + 1])
    for r in range(n_rows):
        base_ref[r] = (cot_ref[r].astype(jnp.float32) + ext[WINDOW + r, WINDOW:]).astype(jnp.bfloat16)
        side_ref[r] = ext[WINDOW + r, :WINDOW].astype(jnp.bfloat16)
    n_top = top_ref.shape[0]
    for r in range(n_top):
        top_ref[r] = ext[WINDOW - n_top + r].astype(jnp.bfloat16)


def edge_kernel(side_ref, top_ref, _, out_ref):
    n_rows, n_top = side_ref.shape[0], top_ref.shape[0]
    for r in range(n_rows):
        edge = side_ref[r].astype(jnp.float32)
        at = r - n_rows + n_top
        if at >= 0:
            edge = edge + top_ref[at].astype(jnp.float32)[:WINDOW]
        out_ref[r] = edge.astype(jnp.bfloat16)


def prepare_kernel(bias_ref, w_ref, full_ref, wt_ref):
    n_head, n_gap = bias_ref.shape
    span = 2 * WINDOW - 1
    width = 2 * LANES
    lane = lax.broadcasted_iota(jnp.int32, (width, LANES), 0)
    cell = lax.broadcasted_iota(jnp.int32, (width, LANES), 1) % CELLS
    place = cell // WINDOW * span + cell % WINDOW + n_gap // 2
    onehot = (lane == place).astype(jnp.float32).astype(jnp.bfloat16)
    table = jnp.concatenate([bias_ref[...], jnp.zeros((n_head, width - n_gap), jnp.float32)], 1)
    for h in range(n_head):
        line = jnp.broadcast_to(table[h : h + 1], (WINDOW, width))
        rows = [pltpu.roll(line, r * span, 1, stride=1, stride_axis=0) for r in range(WINDOW)]
        rest = jnp.concatenate(rows, 0)
        total = jnp.zeros((CELLS, LANES), jnp.float32)
        for _ in range(3):
            part = rest.astype(jnp.bfloat16)
            total += dot(part, onehot)
            rest = rest - part.astype(jnp.float32)
        full_ref[h] = total
    wt_ref[...] = w_ref[...].T


def pack_kernel(n_top, x_ref, cot_ref, mask, side_ref, top_x, top_c, corner_ref, edges, sems):
    n_rows, n_cols, n_chan = x_ref.shape
    copies = []
    for k, (ref, top) in enumerate(((x_ref, top_x), (cot_ref, top_c))):
        copies.append(pltpu.make_async_copy(ref.at[:, pl.ds(n_cols - 2 * WINDOW, 2 * WINDOW)], edges.at[k], sems.at[2 * k]))
        copies.append(pltpu.make_async_copy(ref.at[pl.ds(n_rows - n_top, n_top)], top, sems.at[2 * k + 1]))
    for copy in copies:
        copy.start()
    for k in range(2):
        copies[2 * k].wait()
        for r in range(n_rows):
            edge = edges[k, r][WINDOW:]
            side_ref[k, r] = edge
            at = r - n_rows + n_top
            if at >= 0:
                corner_ref[k, at] = edge
    line = lax.broadcasted_iota(jnp.int32, (WINDOW, n_chan), 0)
    live = jnp.zeros((WINDOW, n_chan), jnp.float32)
    for r in range(WINDOW):
        live = jnp.where(line == r, mask[n_rows - WINDOW + r].astype(jnp.float32), live)
    corner_ref[0, n_top] = live.astype(jnp.bfloat16)
    corner_ref[1, n_top] = live.astype(jnp.bfloat16)
    copies[1].wait()
    copies[3].wait()


def first_add_kernel(keep_ref, got_ref, own_ref, *send_refs):
    size = own_ref.shape[0]
    for k in range(len(send_refs) + 1):
        cut = slice(k * size, (k + 1) * size)
        total = keep_ref[cut] + got_ref[cut].astype(jnp.float32)
        if k:
            send_refs[k - 1][...] = total.astype(jnp.bfloat16)
        else:
            own_ref[...] = total


def next_add_kernel(n_got, n_more, own_ref, *refs):
    got, (out_ref, *send_refs) = refs[:n_got], refs[n_got + n_more :]
    size = out_ref.shape[0]
    for k in range(len(send_refs) + 1):
        cut = slice(k * size, (k + 1) * size)
        total = own_ref[cut]
        for ref in got:
            total = total + ref[cut].astype(jnp.float32)
        if k:
            send_refs[k - 1][...] = total.astype(jnp.bfloat16)
        else:
            out_ref[...] = total.astype(out_ref.dtype)


def join_kernel(n_got, *refs):
    for k in range(n_got):
        refs[-1][k : k + 1] = refs[k][...]


def tree_add_kernel(*refs):
    parts = [ref[...].astype(jnp.float32) for ref in refs[:-1]]
    while len(parts) > 1:
        parts = [parts[k] + parts[k + 1] for k in range(0, len(parts), 2)]
    refs[-1][...] = parts[0].astype(jnp.bfloat16)


def unpack_kernel(counts, n_proj, factor, meta, *refs):
    n_c, n_x, n_y = counts
    mine, other = refs[:n_x], refs[n_x : 2 * n_x]
    qkv_ref, out_ref, gain_ref, bias_ref, small = refs[2 * n_x :]
    rows = mine[0].shape[1]
    n_chan = out_ref.shape[1]
    for half in range(2):
        c = meta[2] if half == 0 else 1 - meta[2]
        for k, ref in enumerate(other if half else mine):
            x = lax.rem(meta[3] + k, n_x)
            for j in range(n_y):
                y = lax.rem(meta[4] + j, n_y)
                chunk = ref[j].astype(jnp.float32) * factor
                to = pl.ds(pl.multiple_of(((c * n_x + x) * n_y + y) * rows, rows), rows)
                qkv_ref[to] = chunk[:, :n_proj]
                out_ref[to] = chunk[:, n_proj : n_proj + n_chan]
                small[to] = chunk[:, n_proj + n_chan :]
    gain_ref[...] = small[...].T[LANES - 1 :]
    n_head, n_gap = bias_ref.shape
    span = 2 * WINDOW - 1
    wide = jnp.concatenate([small[:n_head], small[n_head : 2 * n_head]], 1)
    lane = lax.broadcasted_iota(jnp.int32, wide.shape, 1)
    bias = jnp.zeros_like(wide)
    for k in range(span):
        moved = pltpu.roll(wide, 2 * LANES - k, 1) if k else wide
        bias = jnp.where((lane >= k * span) & (lane < (k + 1) * span), moved, bias)
    bias_ref[...] = bias[:, :n_gap]


class Places:
    def __init__(self):
        self.n_lat, self.n_lon = lax.axis_size("lat"), lax.axis_size("lon")
        self.c = 2
        self.x = min(4, self.n_lon // self.c)
        self.y_low = self.n_lon // (self.c * self.x)
        self.y_high = 2
        self.y = self.y_low * self.y_high
        self.z = self.n_lat // self.y_high

    def index(self, z, y, x, c):
        high, low = divmod(y, self.y_low)
        return (z * self.y_high + high) * self.n_lon + (low * self.x + x) * self.c + c

    def mine(self):
        lat, lon = lax.axis_index("lat"), lax.axis_index("lon")
        return (
            lon % self.c,
            lon // self.c % self.x,
            lat % self.y_high * self.y_low + lon // (self.c * self.x),
        )

    def move(self, array, to):
        every = itertools.product(range(self.z), range(self.y), range(self.x), range(self.c))
        pairs = [(self.index(*at), self.index(*to(*at))) for at in every]
        return lax.ppermute(array, ("lat", "lon"), pairs)

    def by_c(self, array):
        return self.move(array, lambda z, y, x, c: (z, y, x, 1 - c))

    def by_x(self, array, k):
        return self.move(array, lambda z, y, x, c: (z, y, (x + k) % self.x, c))

    def by_y(self, array, k):
        return self.move(array, lambda z, y, x, c: (z, (y + k) % self.y, x, c))

    def by_z(self, array, bits):
        return self.move(array, lambda z, y, x, c: (z ^ bits, y, x, c))


def small_call(kernel, outs, name, limit, *args):
    return pl.pallas_call(
        kernel,
        out_shape=outs,
        compiler_params=pltpu.CompilerParams(vmem_limit_bytes=limit * MIB),
        name=name,
    )(*args)


def total_over_devices(places, keep, send, beside):
    shape = keep.shape[1:]
    bf = functools.partial(jax.ShapeDtypeStruct, dtype=jnp.bfloat16)
    got = places.by_c(send)
    own = jax.ShapeDtypeStruct((places.y, *shape), jnp.float32)
    own, *sends = small_call(first_add_kernel, (own,) + (bf((places.y, *shape)),) * (places.x - 1), "add_c", 12, keep, got)
    got = [places.by_x(part, k + 1) for k, part in enumerate(sends)]
    nxt = jax.ShapeDtypeStruct((1, *shape), jnp.float32)
    ahead, finish = beside(own)
    own, *sends = pl.pallas_call(
        functools.partial(next_add_kernel, len(got), 1),
        out_shape=(nxt,) + (bf((1, *shape)),) * (places.y - 1),
        in_specs=[whole()] * (1 + len(got)) + [pl.BlockSpec(memory_space=pl.ANY)],
        compiler_params=pltpu.CompilerParams(vmem_limit_bytes=6 * MIB),
        name="add_x",
    )(own, *got, ahead)
    got = [places.by_y(part, k + 1) for k, part in enumerate(sends)]
    (mine,) = small_call(functools.partial(next_add_kernel, len(got), 0), (bf((1, *shape)),), "add_y", 4, own, *got)
    for group in {1: (), 2: ((1,),), 4: ((1, 2, 3),), 8: ((1, 2, 3), (6,))}[places.z]:
        others = [places.by_z(mine, bits) for bits in group]
        mine = small_call(tree_add_kernel, bf((1, *shape)), "add_z", 2, mine, *others)
    parts = [mine] + [places.by_y(mine, -k) for k in range(1, places.y)]
    mine = small_call(functools.partial(join_kernel, len(parts)), bf((places.y, *shape)), "join", 4, *parts)
    result = finish(mine)
    mine = [mine] + [places.by_x(mine, -k) for k in range(1, places.x)]
    return mine, [places.by_c(part) for part in mine], result


def ring(array, lat, lon):
    n_lat, n_lon = lax.axis_size("lat"), lax.axis_size("lon")
    pairs = [
        (i * n_lon + j, (i + lat) % n_lat * n_lon + (j + lon) % n_lon) for i in range(n_lat) for j in range(n_lon)
    ]
    return lax.ppermute(array, ("lat", "lon"), pairs)


def local(saved_state, cotangent, row_mask, shifts, norm_gain, w_qkv, w_out, bias_table):
    n_rows, n_cols, n_chan = saved_state.shape
    n_head = bias_table.shape[0]
    n_proj = w_qkv.shape[1]
    n_tok = n_rows // 2 * n_cols
    n_top = WINDOW - 1
    places = Places()
    counts = (places.c, places.x, places.y)
    bf, f32 = jnp.bfloat16, jnp.float32

    smem = pl.BlockSpec(memory_space=pltpu.SMEM)
    tile = functools.partial(jax.ShapeDtypeStruct, dtype=bf)
    side, top_x, top_c, corner = pl.pallas_call(
        functools.partial(pack_kernel, n_top),
        out_shape=(
            tile((2, n_rows, WINDOW, n_chan)),
            tile((n_top, n_cols, n_chan)),
            tile((n_top, n_cols, n_chan)),
            tile((2, WINDOW, WINDOW, n_chan)),
        ),
        in_specs=[pl.BlockSpec(memory_space=pltpu.HBM), pl.BlockSpec(memory_space=pltpu.HBM), smem],
        scratch_shapes=[pltpu.VMEM((2, n_rows, 2 * WINDOW, n_chan), bf), pltpu.SemaphoreType.DMA((4,))],
        compiler_params=pltpu.CompilerParams(vmem_limit_bytes=58 * MIB),
        name="pack",
    )(saved_state, cotangent, row_mask)
    side = ring(side, 0, 1)
    top_x = ring(top_x, 1, 0)
    top_c = ring(top_c, 1, 0)
    corner = ring(corner, 1, 1)
    at = jnp.stack(places.mine()).astype(jnp.int32)
    gain = norm_gain.reshape(1, n_chan)
    bias, w_t = pl.pallas_call(
        prepare_kernel,
        out_shape=(jax.ShapeDtypeStruct((n_head, CELLS, LANES), f32), tile((n_proj, n_chan))),
        compiler_params=pltpu.CompilerParams(vmem_limit_bytes=16 * MIB),
        cost_estimate=pl.CostEstimate(flops=10**9, bytes_accessed=4 * MIB, transcendentals=0),
        name="prepare",
    )(bias_table, w_qkv)

    below = jnp.minimum(lax.axis_index("lat"), 1).astype(jnp.int32).reshape(1)
    meta = jnp.concatenate([shifts, at, below, row_mask])
    cells_f, cells_t = pltpu.VMEM((n_tok, n_chan), f32), pltpu.VMEM((n_chan, n_tok), bf)
    x_in, gp_in, sums_in, bsum_in = pl.pallas_call(
        functools.partial(inner_kernel, n_head),
        out_shape=(
            tile((n_tok, n_chan)),
            tile((n_proj, n_tok)),
            jax.ShapeDtypeStruct((n_chan, n_proj + n_chan), f32),
            jax.ShapeDtypeStruct((n_head, CELLS, LANES), f32),
        ),
        in_specs=[smem] + [whole()] * 8,
        scratch_shapes=[
            pltpu.VMEM((n_tok, n_chan), bf),
            cells_t,
            cells_t,
            cells_f,
            cells_f,
            pltpu.VMEM((n_proj, n_tok), bf),
            pltpu.VMEM((n_tok, 2 * n_chan), bf),
            cells_t,
        ],
        compiler_params=pltpu.CompilerParams(vmem_limit_bytes=24 * MIB),
        cost_estimate=pl.CostEstimate(flops=8 * 10**9, bytes_accessed=16 * MIB, transcendentals=2**19),
        name="inner",
    )(meta, saved_state, cotangent, side, bias, gain, w_t, w_qkv, w_out)
    x_out, nrm_out, proj_out, kv_out = pl.pallas_call(
        functools.partial(front_kernel, n_head),
        out_shape=(tile((n_tok, n_chan)), tile((n_chan, n_tok)), tile((n_proj, n_tok)), tile((n_tok, 2 * n_chan))),
        in_specs=[smem] + [whole()] * 7 + [pl.BlockSpec(memory_space=pl.ANY)],
        scratch_shapes=[cells_f],
        compiler_params=pltpu.CompilerParams(vmem_limit_bytes=14 * MIB),
        cost_estimate=pl.CostEstimate(flops=3 * 10**9, bytes_accessed=8 * MIB, transcendentals=0),
        name="front",
    )(meta, saved_state, side, top_x, corner, gain, w_t, w_qkv, bsum_in)

    width = n_proj + n_chan + LANES
    rows = n_chan // math.prod(counts)
    half = math.prod(counts) // 2
    gp_out, keep, send = pl.pallas_call(
        functools.partial(outer_kernel, n_head, counts),
        out_shape=(
            tile((n_proj, n_tok)),
            jax.ShapeDtypeStruct((half, rows, width), f32),
            tile((half, rows, width)),
        ),
        in_specs=[smem] + [whole()] * 13,
        scratch_shapes=[
            pltpu.VMEM((n_tok, n_chan), bf),
            cells_t,
            pltpu.VMEM((n_head, CELLS, LANES), f32),
            cells_f,
            cells_t,
            pltpu.VMEM((n_chan, width), f32),
            pltpu.VMEM((n_head * CELLS, LANES), f32),
            pltpu.VMEM((n_head * CELLS, LANES), f32),
        ],
        compiler_params=pltpu.CompilerParams(vmem_limit_bytes=30 * MIB),
        cost_estimate=pl.CostEstimate(flops=10**10, bytes_accessed=24 * MIB, transcendentals=2**19),
        name="outer",
    )(meta, cotangent, side, top_c, corner, bias, gain, w_qkv, w_out, nrm_out, proj_out, kv_out, sums_in, bsum_in)

    def input_grad(start):
        base, *edges = pl.pallas_call(
            cells_kernel,
            out_shape=(
                tile((n_rows, n_cols, n_chan)),
                tile((n_top, n_cols + WINDOW, n_chan)),
                tile((n_rows, WINDOW, n_chan)),
            ),
            in_specs=[smem] + [whole()] * 7 + [pl.BlockSpec(memory_space=pl.ANY)],
            scratch_shapes=[pltpu.VMEM((n_rows + WINDOW, n_cols + WINDOW, n_chan), f32)],
            compiler_params=pltpu.CompilerParams(vmem_limit_bytes=24 * MIB),
            cost_estimate=pl.CostEstimate(flops=16 * 10**8, bytes_accessed=12 * MIB, transcendentals=0),
            name="cells",
        )(meta, x_in, x_out, gp_in, gp_out, cotangent, gain, w_qkv, start)
        top_back = ring(edges[0], -1, 0)

        def finish(later):
            side = pl.pallas_call(
                edge_kernel,
                out_shape=tile((n_rows, WINDOW, n_chan)),
                in_specs=[whole()] * 2 + [pl.BlockSpec(memory_space=pl.ANY)],
                compiler_params=pltpu.CompilerParams(vmem_limit_bytes=4 * MIB),
                name="edge",
            )(edges[1], top_back, later)
            return base, top_back, ring(side, 0, -1)

        return edges[1], finish

    mine, other, (base, top_back, side_back) = total_over_devices(places, keep, send, input_grad)
    edge = jnp.pad(top_back[:, WINDOW:], ((n_rows - n_top, 0), (0, 0), (0, 0)))
    edge = edge + jnp.pad(side_back, ((0, 0), (n_cols - WINDOW, 0), (0, 0)))
    state_grad = (base.astype(f32) + edge.astype(f32)).astype(bf)

    factor = 1.0 / math.sqrt(n_rows * places.n_lat * n_cols * places.n_lon)
    qkv_grad, out_grad, gain_grad, bias_grad = pl.pallas_call(
        functools.partial(unpack_kernel, counts, n_proj, factor),
        out_shape=(
            jax.ShapeDtypeStruct((n_chan, n_proj), f32),
            jax.ShapeDtypeStruct((n_chan, n_chan), f32),
            jax.ShapeDtypeStruct((1, n_chan), f32),
            jax.ShapeDtypeStruct(bias_table.shape, f32),
        ),
        in_specs=[smem] + [whole()] * (2 * places.x),
        scratch_shapes=[pltpu.VMEM((n_chan, LANES), f32)],
        compiler_params=pltpu.CompilerParams(vmem_limit_bytes=16 * MIB),
        name="unpack",
    )(meta, *mine, *other)
    return state_grad, qkv_grad, out_grad, gain_grad.reshape(n_chan), bias_grad


def solution(mesh):
    return jax.shard_map(
        local,
        mesh=mesh,
        in_specs=(P("lat", "lon", None), P("lat", "lon", None), P("lat"), P(), P(), P(), P(), P()),
        out_specs=(P("lat", "lon", None), P(), P(), P(), P()),
        check_vma=False,
    )
```

```python
import functools
import itertools
import math

import jax
import jax.numpy as jnp
from jax import lax
from jax.experimental import pallas as pl
from jax.experimental.pallas import tpu as pltpu
from jax.sharding import PartitionSpec as P

EPSILON = 1e-05


NT = (((1,), (1,)), ((), ()))
NN = (((1,), (0,)), ((), ()))
LANES = 128
WINDOW = 8
CELLS = WINDOW * WINDOW
TOKENS = 256
MIB = 1024 * 1024


def dot(a, b, dims=NN):
    return lax.dot_general(a, b, dims, preferred_element_type=jnp.float32)


def whole(*_):
    return pl.BlockSpec(memory_space=pltpu.VMEM)


def norm_stats(x):
    cen = x - jnp.mean(x, -1, keepdims=True)
    inv = lax.rsqrt(jnp.mean(cen * cen, -1, keepdims=True) + EPSILON)
    return cen * inv, inv


def project_cells(scale, gain, wt_ref, w_ref, xf, x_out, nrm_t, proj_t, kv):
    n_tok, n_chan = xf.shape
    x_out[...] = xf[...].astype(jnp.bfloat16)
    for base in range(0, n_tok, TOKENS):
        rows = slice(base, base + TOKENS)
        x_hat, _ = norm_stats(xf[rows])
        normed_f = x_hat * gain
        normed = normed_f.astype(jnp.bfloat16)
        nrm_t[:, rows] = normed_f.T.astype(jnp.bfloat16)
        proj_t[:n_chan, rows] = (dot(wt_ref[:n_chan], normed, NT) * scale).astype(jnp.bfloat16)
        proj_t[n_chan:, rows] = dot(wt_ref[n_chan:], normed, NT).astype(jnp.bfloat16)
        kv[rows] = dot(normed, w_ref[:, n_chan:]).astype(jnp.bfloat16)


def block_diag(block, step):
    blank = jnp.zeros((step, block.shape[1]), block.dtype)
    count = block.shape[0] // step
    columns = []
    for h in range(count):
        parts = [blank] * count
        parts[h] = block[h * step : (h + 1) * step]
        columns.append(jnp.concatenate(parts, 0))
    return jnp.concatenate(columns, 1)


def attention_unit(n_chan, dim, scale, bias_ref, mask, proj_t, kv, gm_t, mix_t, gp_t, bsum_ref, pair, group):
    lanes = pl.ds(pl.multiple_of(pair * LANES, LANES), LANES)
    c0 = group * LANES
    q_t = proj_t[pl.ds(c0, LANES), lanes]
    k_t = proj_t[pl.ds(n_chan + c0, LANES), lanes]
    v_t = proj_t[pl.ds(2 * n_chan + c0, LANES), lanes]
    g_t = gm_t[pl.ds(c0, LANES), lanes]
    k_tok = kv[lanes, pl.ds(c0, LANES)]
    v_tok = kv[lanes, pl.ds(n_chan + c0, LANES)]
    q_bd = block_diag(q_t, dim)
    g_bd = block_diag(g_t, dim)
    scores = dot(k_tok, q_bd)
    grads = dot(v_tok, g_bd)
    first = lax.broadcasted_iota(jnp.int32, (CELLS, LANES), 1) < CELLS
    heads = LANES // dim
    mixed, dq, dk, dv = [], [], [], []
    for h in range(heads):
        cut = slice(h * LANES, (h + 1) * LANES)
        rows = slice(h * dim, (h + 1) * dim)
        head = group * heads + h
        s = jnp.where(first, scores[:CELLS, cut], scores[CELLS:, cut]) + bias_ref[head] + mask
        e = jnp.exp(s - jnp.max(s, 0, keepdims=True))
        a = e * (1.0 / jnp.sum(e, 0, keepdims=True))
        d = jnp.where(first, grads[:CELLS, cut], grads[CELLS:, cut])
        ad = a * d
        ds = ad - a * jnp.sum(ad, 0, keepdims=True)
        bsum_ref[head] += ds
        zero = jnp.zeros_like(a)
        a2 = jnp.concatenate([jnp.where(first, a, zero), jnp.where(first, zero, a)], 0).astype(jnp.bfloat16)
        ds2 = jnp.concatenate([jnp.where(first, ds, zero), jnp.where(first, zero, ds)], 0).astype(jnp.bfloat16)
        mixed.append(dot(v_t[rows], a2))
        dv.append(a2)
        dq.append(dot(k_t[rows], ds2) * scale)
        dk.append(ds2)
    mix_t[pl.ds(c0, LANES), lanes] = jnp.concatenate(mixed, 0).astype(jnp.bfloat16)
    gp_t[pl.ds(c0, LANES), lanes] = jnp.concatenate(dq, 0).astype(jnp.bfloat16)
    gp_t[pl.ds(n_chan + c0, LANES), lanes] = dot(q_bd, jnp.concatenate(dk, 1), NT).astype(jnp.bfloat16)
    gp_t[pl.ds(2 * n_chan + c0, LANES), lanes] = dot(g_bd, jnp.concatenate(dv, 1), NT).astype(jnp.bfloat16)


def place_row(line, shift, out, r, live=None):
    line = line.astype(jnp.float32).reshape(-1, WINDOW, line.shape[1])
    if live is not None:
        line = line * live
    line = pltpu.roll(line, WINDOW - shift, 1)
    head = lax.broadcasted_iota(jnp.int32, line.shape[1:], 0) < WINDOW - shift
    for w in range(line.shape[0] - 1):
        start = w * CELLS + r * WINDOW
        out[start : start + WINDOW] = jnp.where(head, line[w], line[w + 1])


def window_row(n_head, cf, live, wo_ref, bias_ref, go_ref, mix_t, gp_t, bsum_ref, proj_t, kv, gm_t):
    n_tok, n_chan = cf.shape
    dim = n_chan // n_head
    scale = dim ** (-0.5)
    go_ref[...] = cf[...].astype(jnp.bfloat16)
    for base in range(0, n_tok, TOKENS):
        rows = slice(base, base + TOKENS)
        gm_t[:, rows] = dot(wo_ref[...], go_ref[rows], NT).astype(jnp.bfloat16)
    mask = jnp.concatenate([(live[r][:, :LANES] - 1.0) * 1e30 for r in range(WINDOW)], 0)
    groups = n_chan // LANES

    @pl.loop(0, n_tok // LANES)
    def _(pair):
        for group in range(groups):
            attention_unit(n_chan, dim, scale, bias_ref, mask, proj_t, kv, gm_t, mix_t, gp_t, bsum_ref, pair, group)


def weight_sums(sums, nrm_t, gp_t, mix_t, go_ref, more):
    n_proj, n_chan = gp_t.shape[0], nrm_t.shape[0]
    for base in range(0, n_proj + n_chan, TOKENS):
        cols = slice(base, base + TOKENS)
        if base < n_proj:
            part = dot(nrm_t[...], gp_t[cols], NT)
        else:
            part = dot(mix_t[...], go_ref[:, base - n_proj : base - n_proj + TOKENS])
        sums[:, cols] = part if more is None else part + more[:, cols]


def inner_kernel(n_head, meta, x_ref, cot_ref, side_ref, bias_ref, gain_ref, wt_ref, w_ref, wo_ref,
                 x_out, gp_t, sums_ref, bsum_ref, go_ref, nrm_t, mix_t, xf, cf, proj_t, kv, gm_t):
    scale = (x_ref.shape[2] // n_head) ** (-0.5)
    lat, lon = meta[0], meta[1]
    live = []
    for r in range(WINDOW):
        live.append(jnp.full((WINDOW, x_ref.shape[2]), meta[6 + lat + r].astype(jnp.float32)))
        for k, (grid, out) in enumerate(((x_ref, xf), (cot_ref, cf))):
            line = jnp.concatenate([part.astype(jnp.float32) for part in (side_ref[k, lat + r], grid[lat + r])], 0)
            place_row(line, lon, out, r, live[r] if k else None)
    bsum_ref[...] = jnp.zeros_like(bsum_ref)
    project_cells(scale, gain_ref[...], wt_ref, w_ref, xf, x_out, nrm_t, proj_t, kv)
    window_row(n_head, cf, live, wo_ref, bias_ref, go_ref, mix_t, gp_t, bsum_ref, proj_t, kv, gm_t)
    weight_sums(sums_ref, nrm_t, gp_t, mix_t, go_ref, None)


def outer_line(k, e, grid, side_ref, top, corner_ref):
    n_top = top.shape[0]
    above = e < WINDOW
    up = jnp.clip(e - (WINDOW - n_top), 0, n_top - 1)
    own = jnp.maximum(e - WINDOW, 0)
    parts = jnp.where(above, corner_ref[k, up], side_ref[k, own]), jnp.where(above, top[up], grid[own])
    return jnp.concatenate([part.astype(jnp.float32) for part in parts], 0)


def front_kernel(n_head, meta, x_ref, side_ref, top, corner_ref, gain_ref, wt_ref, w_ref, _, x_out, nrm_t, proj_t, kv, xf):
    scale = (x_ref.shape[2] // n_head) ** (-0.5)
    for r in range(WINDOW):
        place_row(outer_line(0, meta[0] + r, x_ref, side_ref, top, corner_ref), meta[1], xf, r)
    project_cells(scale, gain_ref[...], wt_ref, w_ref, xf, x_out, nrm_t, proj_t, kv)


def outer_kernel(n_head, counts, meta, cot_ref, side_ref, top, corner_ref, bias_ref, gain_ref, w_ref, wo_ref,
                 nrm_t, proj_t, kv, sums_in, bsum_in,
                 gp_t, keep_ref, send_ref,
                 go_ref, mix_t, bsum_ref, cf, gm_t, sums, spread_a, spread_b):
    n_chan = gain_ref.shape[1]
    up_mask = corner_ref[0, WINDOW - 1].astype(jnp.float32) * meta[5].astype(jnp.float32)
    line_of = lax.broadcasted_iota(jnp.int32, up_mask.shape, 0)
    live = []
    for r in range(WINDOW):
        e = meta[0] + r
        row_live = jnp.full((WINDOW, n_chan), meta[6 + jnp.maximum(e - WINDOW, 0)].astype(jnp.float32))
        up_live = jnp.sum(jnp.where(line_of == e, up_mask, 0.0), 0, keepdims=True)
        live.append(jnp.where(e < WINDOW, jnp.broadcast_to(up_live, row_live.shape), row_live))
        place_row(outer_line(1, e, cot_ref, side_ref, top, corner_ref), meta[1], cf, r, live[r])
    bsum_ref[...] = bsum_in[...]
    window_row(n_head, cf, live, wo_ref, bias_ref, go_ref, mix_t, gp_t, bsum_ref, proj_t, kv, gm_t)

    n_proj = 3 * n_chan
    weight_sums(sums, nrm_t, gp_t, mix_t, go_ref, sums_in)
    gain_sum = jnp.sum(sums[:, :n_proj] * w_ref[...].astype(jnp.float32), 1, keepdims=True)

    width = 2 * LANES
    cell = lax.broadcasted_iota(jnp.int32, (LANES, width), 0) % CELLS
    lane = lax.broadcasted_iota(jnp.int32, (LANES, width), 1)
    place = (cell // WINDOW) * 16 + cell % WINDOW + 119
    onehot = (lane == place).astype(jnp.float32).astype(jnp.bfloat16)
    flat = bsum_ref[...].reshape(n_head * CELLS, LANES)
    high = flat.astype(jnp.bfloat16)
    low = (flat - high.astype(jnp.float32)).astype(jnp.bfloat16)
    spread = dot(high, onehot) + dot(low, onehot)
    spread_a[...] = spread[:, :LANES]
    spread_b[...] = spread[:, LANES:]
    bias_sum = jnp.zeros((n_head, width), jnp.float32)
    for j in range(CELLS):
        row = jnp.concatenate([ref[pl.ds(j, n_head, stride=CELLS), :] for ref in (spread_a, spread_b)], 1)
        by = (j // WINDOW) * 16 + j % WINDOW
        bias_sum += pltpu.roll(row, width - by, 1) if by else row
    tail = lax.broadcasted_iota(jnp.int32, (n_chan, LANES), 1) == LANES - 1
    bias_rows = jnp.concatenate(
        [bias_sum[:, :LANES], bias_sum[:, LANES:], jnp.zeros((n_chan - 2 * n_head, LANES), jnp.float32)], 0
    )
    sums[:, n_proj + n_chan :] = jnp.where(tail, gain_sum * (1.0 / gain_col(gain_ref)), bias_rows)

    n_c, n_x, n_y = counts
    rows = n_chan // (n_c * n_x * n_y)
    for c in range(n_c):
        for x in range(n_x):
            for y in range(n_y):
                chunk = sums[((c * n_x + x) * n_y + y) * rows : ((c * n_x + x) * n_y + y + 1) * rows]
                at = lax.rem(x - meta[3] + n_x, n_x) * n_y + lax.rem(y - meta[4] + n_y, n_y)

                @pl.when(meta[2] == c)
                def _():
                    keep_ref[at] = chunk

                @pl.when(meta[2] != c)
                def _():
                    send_ref[at] = chunk.astype(jnp.bfloat16)


def gain_col(gain_ref):
    n_chan = gain_ref.shape[1]
    return jnp.broadcast_to(gain_ref[...], (LANES, n_chan)).T[:, :1]


def cells_kernel(meta, xi_ref, xo_ref, gpi_ref, gpo_ref, cot_ref, gain_ref, w_ref, _, base_ref, top_ref, side_ref, ext):
    n_rows, n_cols, n_chan = cot_ref.shape
    lat, lon = meta[0], meta[1]
    ext[...] = jnp.zeros_like(ext)
    for part, (x_ref, gp_t) in enumerate(((xo_ref, gpo_ref), (xi_ref, gpi_ref))):
        n_tok = x_ref.shape[0]
        cells = []
        for base in range(0, n_tok, TOKENS):
            rows = slice(base, base + TOKENS)
            x_hat, inv = norm_stats(x_ref[rows].astype(jnp.float32))
            g = dot(w_ref[...], gp_t[:, rows]).T * gain_ref[...]
            cells.append(inv * (g - jnp.mean(g, -1, keepdims=True) - x_hat * jnp.mean(g * x_hat, -1, keepdims=True)))
        blank = jnp.zeros((1, WINDOW, n_chan), jnp.float32)
        head = lax.broadcasted_iota(jnp.int32, (WINDOW, n_chan), 0) < lon
        for r in range(WINDOW):
            row = jnp.stack(
                [
                    cells[w * CELLS // TOKENS][w * CELLS % TOKENS + r * WINDOW :][:WINDOW]
                    for w in range(n_tok // CELLS)
                ],
                0,
            )
            row = jnp.concatenate([blank, pltpu.roll(row, lon, 1), blank], 0)
            for t in range(row.shape[0] - 1):
                ext[lat + part * WINDOW + r, t * WINDOW : (t + 1) * WINDOW, :] = jnp.where(head, row[t], row[t + 1])
    for r in range(n_rows):
        base_ref[r] = (cot_ref[r].astype(jnp.float32) + ext[WINDOW + r, WINDOW:]).astype(jnp.bfloat16)
        side_ref[r] = ext[WINDOW + r, :WINDOW].astype(jnp.bfloat16)
    n_top = top_ref.shape[0]
    for r in range(n_top):
        top_ref[r] = ext[WINDOW - n_top + r].astype(jnp.bfloat16)


def edge_kernel(side_ref, top_ref, _, out_ref):
    n_rows, n_top = side_ref.shape[0], top_ref.shape[0]
    for r in range(n_rows):
        edge = side_ref[r].astype(jnp.float32)
        at = r - n_rows + n_top
        if at >= 0:
            edge = edge + top_ref[at].astype(jnp.float32)[:WINDOW]
        out_ref[r] = edge.astype(jnp.bfloat16)


def prepare_kernel(bias_ref, w_ref, full_ref, wt_ref):
    n_head, n_gap = bias_ref.shape
    span = 2 * WINDOW - 1
    width = 2 * LANES
    lane = lax.broadcasted_iota(jnp.int32, (width, LANES), 0)
    cell = lax.broadcasted_iota(jnp.int32, (width, LANES), 1) % CELLS
    place = cell // WINDOW * span + cell % WINDOW + n_gap // 2
    onehot = (lane == place).astype(jnp.float32).astype(jnp.bfloat16)
    table = jnp.concatenate([bias_ref[...], jnp.zeros((n_head, width - n_gap), jnp.float32)], 1)
    for h in range(n_head):
        line = jnp.broadcast_to(table[h : h + 1], (WINDOW, width))
        rows = [pltpu.roll(line, r * span, 1, stride=1, stride_axis=0) for r in range(WINDOW)]
        rest = jnp.concatenate(rows, 0)
        total = jnp.zeros((CELLS, LANES), jnp.float32)
        for _ in range(3):
            part = rest.astype(jnp.bfloat16)
            total += dot(part, onehot)
            rest = rest - part.astype(jnp.float32)
        full_ref[h] = total
    wt_ref[...] = w_ref[...].T


def pack_kernel(n_top, x_ref, cot_ref, mask, side_ref, top_x, top_c, corner_ref, edges, sems):
    n_rows, n_cols, n_chan = x_ref.shape
    copies = []
    for k, (ref, top) in enumerate(((x_ref, top_x), (cot_ref, top_c))):
        copies.append(pltpu.make_async_copy(ref.at[:, pl.ds(n_cols - 2 * WINDOW, 2 * WINDOW)], edges.at[k], sems.at[2 * k]))
        copies.append(pltpu.make_async_copy(ref.at[pl.ds(n_rows - n_top, n_top)], top, sems.at[2 * k + 1]))
    for copy in copies:
        copy.start()
    for k in range(2):
        copies[2 * k].wait()
        for r in range(n_rows):
            edge = edges[k, r][WINDOW:]
            side_ref[k, r] = edge
            at = r - n_rows + n_top
            if at >= 0:
                corner_ref[k, at] = edge
    line = lax.broadcasted_iota(jnp.int32, (WINDOW, n_chan), 0)
    live = jnp.zeros((WINDOW, n_chan), jnp.float32)
    for r in range(WINDOW):
        live = jnp.where(line == r, mask[n_rows - WINDOW + r].astype(jnp.float32), live)
    corner_ref[0, n_top] = live.astype(jnp.bfloat16)
    corner_ref[1, n_top] = live.astype(jnp.bfloat16)
    copies[1].wait()
    copies[3].wait()


def first_add_kernel(keep_ref, got_ref, own_ref, *send_refs):
    size = own_ref.shape[0]
    for k in range(len(send_refs) + 1):
        cut = slice(k * size, (k + 1) * size)
        total = keep_ref[cut] + got_ref[cut].astype(jnp.float32)
        if k:
            send_refs[k - 1][...] = total.astype(jnp.bfloat16)
        else:
            own_ref[...] = total


def next_add_kernel(n_got, n_more, own_ref, *refs):
    got, (out_ref, *send_refs) = refs[:n_got], refs[n_got + n_more :]
    size = out_ref.shape[0]
    for k in range(len(send_refs) + 1):
        cut = slice(k * size, (k + 1) * size)
        total = own_ref[cut]
        for ref in got:
            total = total + ref[cut].astype(jnp.float32)
        if k:
            send_refs[k - 1][...] = total.astype(jnp.bfloat16)
        else:
            out_ref[...] = total.astype(out_ref.dtype)


def join_kernel(n_got, *refs):
    for k in range(n_got):
        refs[-1][k : k + 1] = refs[k][...]


def tree_add_kernel(*refs):
    parts = [ref[...].astype(jnp.float32) for ref in refs[:-1]]
    while len(parts) > 1:
        parts = [parts[k] + parts[k + 1] for k in range(0, len(parts), 2)]
    refs[-1][...] = parts[0].astype(jnp.bfloat16)


def unpack_half(counts, n_proj, factor, meta, c, parts, qkv_ref, out_ref, small, qkv_half, out_half, sems):
    _, n_x, n_y = counts
    rows = parts[0].shape[1]
    n_half, n_chan = out_half.shape
    for k, ref in enumerate(parts):
        x = lax.rem(meta[3] + k, n_x)
        for j in range(n_y):
            y = lax.rem(meta[4] + j, n_y)
            chunk = ref[j].astype(jnp.float32) * factor
            to = pl.ds(pl.multiple_of((x * n_y + y) * rows, rows), rows)
            qkv_half[to] = chunk[:, :n_proj]
            out_half[to] = chunk[:, n_proj : n_proj + n_chan]
            small[to] = chunk[:, n_proj + n_chan :]
    place = pl.ds(pl.multiple_of(c * n_half, n_half), n_half)
    copies = [
        pltpu.make_async_copy(qkv_half, qkv_ref.at[place], sems.at[0]),
        pltpu.make_async_copy(out_half, out_ref.at[place], sems.at[1]),
    ]
    for copy in copies:
        copy.start()
    return copies


def first_unpack_kernel(counts, n_proj, factor, meta, *refs):
    parts, (qkv_ref, out_ref, small, *work) = refs[: counts[1]], refs[counts[1] :]
    for copy in unpack_half(counts, n_proj, factor, meta, meta[2], parts, qkv_ref, out_ref, small, *work):
        copy.wait()


def second_unpack_kernel(counts, n_proj, factor, meta, *refs):
    parts, (_, _, small_in, qkv_ref, out_ref, gain_ref, bias_ref, small, *work) = refs[: counts[1]], refs[counts[1] :]
    copies = unpack_half(counts, n_proj, factor, meta, 1 - meta[2], parts, qkv_ref, out_ref, small, *work)
    first = meta[2] == 0
    upper = jnp.where(first, small_in[...], small[...])
    lower = jnp.where(first, small[...], small_in[...])
    gain_ref[...] = jnp.concatenate([upper, lower], 0).T[LANES - 1 :]
    n_head, n_gap = bias_ref.shape
    span = 2 * WINDOW - 1
    wide = jnp.concatenate([upper[:n_head], upper[n_head : 2 * n_head]], 1)
    lane = lax.broadcasted_iota(jnp.int32, wide.shape, 1)
    bias = jnp.zeros_like(wide)
    for k in range(span):
        moved = pltpu.roll(wide, 2 * LANES - k, 1) if k else wide
        bias = jnp.where((lane >= k * span) & (lane < (k + 1) * span), moved, bias)
    bias_ref[...] = bias[:, :n_gap]
    for copy in copies:
        copy.wait()


class Places:
    def __init__(self):
        self.n_lat, self.n_lon = lax.axis_size("lat"), lax.axis_size("lon")
        self.c = 2
        self.x = min(4, self.n_lon // self.c)
        self.y_low = self.n_lon // (self.c * self.x)
        self.y_high = 2
        self.y = self.y_low * self.y_high
        self.z = self.n_lat // self.y_high

    def index(self, z, y, x, c):
        high, low = divmod(y, self.y_low)
        return (z * self.y_high + high) * self.n_lon + (low * self.x + x) * self.c + c

    def mine(self):
        lat, lon = lax.axis_index("lat"), lax.axis_index("lon")
        return (
            lon % self.c,
            lon // self.c % self.x,
            lat % self.y_high * self.y_low + lon // (self.c * self.x),
        )

    def move(self, array, to):
        every = itertools.product(range(self.z), range(self.y), range(self.x), range(self.c))
        pairs = [(self.index(*at), self.index(*to(*at))) for at in every]
        return lax.ppermute(array, ("lat", "lon"), pairs)

    def by_c(self, array):
        return self.move(array, lambda z, y, x, c: (z, y, x, 1 - c))

    def by_x(self, array, k):
        return self.move(array, lambda z, y, x, c: (z, y, (x + k) % self.x, c))

    def by_y(self, array, k):
        return self.move(array, lambda z, y, x, c: (z, (y + k) % self.y, x, c))

    def by_z(self, array, bits):
        return self.move(array, lambda z, y, x, c: (z ^ bits, y, x, c))


def small_call(kernel, outs, name, limit, *args):
    return pl.pallas_call(
        kernel,
        out_shape=outs,
        compiler_params=pltpu.CompilerParams(vmem_limit_bytes=limit * MIB),
        name=name,
    )(*args)


def total_over_devices(places, keep, send, beside):
    shape = keep.shape[1:]
    bf = functools.partial(jax.ShapeDtypeStruct, dtype=jnp.bfloat16)
    got = places.by_c(send)
    own = jax.ShapeDtypeStruct((places.y, *shape), jnp.float32)
    own, *sends = small_call(first_add_kernel, (own,) + (bf((places.y, *shape)),) * (places.x - 1), "add_c", 12, keep, got)
    got = [places.by_x(part, k + 1) for k, part in enumerate(sends)]
    nxt = jax.ShapeDtypeStruct((1, *shape), jnp.float32)
    ahead, finish = beside(own)
    own, *sends = pl.pallas_call(
        functools.partial(next_add_kernel, len(got), 1),
        out_shape=(nxt,) + (bf((1, *shape)),) * (places.y - 1),
        in_specs=[whole()] * (1 + len(got)) + [pl.BlockSpec(memory_space=pl.ANY)],
        compiler_params=pltpu.CompilerParams(vmem_limit_bytes=6 * MIB),
        name="add_x",
    )(own, *got, ahead)
    got = [places.by_y(part, k + 1) for k, part in enumerate(sends)]
    (mine,) = small_call(functools.partial(next_add_kernel, len(got), 0), (bf((1, *shape)),), "add_y", 4, own, *got)
    for group in {1: (), 2: ((1,),), 4: ((1, 2, 3),), 8: ((1, 2, 3), (6,))}[places.z]:
        others = [places.by_z(mine, bits) for bits in group]
        mine = small_call(tree_add_kernel, bf((1, *shape)), "add_z", 2, mine, *others)
    parts = [mine] + [places.by_y(mine, -k) for k in range(1, places.y)]
    mine = small_call(functools.partial(join_kernel, len(parts)), bf((places.y, *shape)), "join", 4, *parts)
    result = finish(mine)
    mine = [mine] + [places.by_x(mine, -k) for k in range(1, places.x)]
    return mine, [places.by_c(part) for part in mine], result


def ring(array, lat, lon):
    n_lat, n_lon = lax.axis_size("lat"), lax.axis_size("lon")
    pairs = [
        (i * n_lon + j, (i + lat) % n_lat * n_lon + (j + lon) % n_lon) for i in range(n_lat) for j in range(n_lon)
    ]
    return lax.ppermute(array, ("lat", "lon"), pairs)


def local(saved_state, cotangent, row_mask, shifts, norm_gain, w_qkv, w_out, bias_table):
    n_rows, n_cols, n_chan = saved_state.shape
    n_head = bias_table.shape[0]
    n_proj = w_qkv.shape[1]
    n_tok = n_rows // 2 * n_cols
    n_top = WINDOW - 1
    places = Places()
    counts = (places.c, places.x, places.y)
    bf, f32 = jnp.bfloat16, jnp.float32

    smem = pl.BlockSpec(memory_space=pltpu.SMEM)
    tile = functools.partial(jax.ShapeDtypeStruct, dtype=bf)
    side, top_x, top_c, corner = pl.pallas_call(
        functools.partial(pack_kernel, n_top),
        out_shape=(
            tile((2, n_rows, WINDOW, n_chan)),
            tile((n_top, n_cols, n_chan)),
            tile((n_top, n_cols, n_chan)),
            tile((2, WINDOW, WINDOW, n_chan)),
        ),
        in_specs=[pl.BlockSpec(memory_space=pltpu.HBM), pl.BlockSpec(memory_space=pltpu.HBM), smem],
        scratch_shapes=[pltpu.VMEM((2, n_rows, 2 * WINDOW, n_chan), bf), pltpu.SemaphoreType.DMA((4,))],
        compiler_params=pltpu.CompilerParams(vmem_limit_bytes=58 * MIB),
        name="pack",
    )(saved_state, cotangent, row_mask)
    side = ring(side, 0, 1)
    top_x = ring(top_x, 1, 0)
    top_c = ring(top_c, 1, 0)
    corner = ring(corner, 1, 1)
    at = jnp.stack(places.mine()).astype(jnp.int32)
    gain = norm_gain.reshape(1, n_chan)
    bias, w_t = pl.pallas_call(
        prepare_kernel,
        out_shape=(jax.ShapeDtypeStruct((n_head, CELLS, LANES), f32), tile((n_proj, n_chan))),
        compiler_params=pltpu.CompilerParams(vmem_limit_bytes=16 * MIB),
        cost_estimate=pl.CostEstimate(flops=10**9, bytes_accessed=4 * MIB, transcendentals=0),
        name="prepare",
    )(bias_table, w_qkv)

    below = jnp.minimum(lax.axis_index("lat"), 1).astype(jnp.int32).reshape(1)
    meta = jnp.concatenate([shifts, at, below, row_mask])
    cells_f, cells_t = pltpu.VMEM((n_tok, n_chan), f32), pltpu.VMEM((n_chan, n_tok), bf)
    x_in, gp_in, sums_in, bsum_in = pl.pallas_call(
        functools.partial(inner_kernel, n_head),
        out_shape=(
            tile((n_tok, n_chan)),
            tile((n_proj, n_tok)),
            jax.ShapeDtypeStruct((n_chan, n_proj + n_chan), f32),
            jax.ShapeDtypeStruct((n_head, CELLS, LANES), f32),
        ),
        in_specs=[smem] + [whole()] * 8,
        scratch_shapes=[
            pltpu.VMEM((n_tok, n_chan), bf),
            cells_t,
            cells_t,
            cells_f,
            cells_f,
            pltpu.VMEM((n_proj, n_tok), bf),
            pltpu.VMEM((n_tok, 2 * n_chan), bf),
            cells_t,
        ],
        compiler_params=pltpu.CompilerParams(vmem_limit_bytes=24 * MIB),
        cost_estimate=pl.CostEstimate(flops=8 * 10**9, bytes_accessed=16 * MIB, transcendentals=2**19),
        name="inner",
    )(meta, saved_state, cotangent, side, bias, gain, w_t, w_qkv, w_out)
    x_out, nrm_out, proj_out, kv_out = pl.pallas_call(
        functools.partial(front_kernel, n_head),
        out_shape=(tile((n_tok, n_chan)), tile((n_chan, n_tok)), tile((n_proj, n_tok)), tile((n_tok, 2 * n_chan))),
        in_specs=[smem] + [whole()] * 7 + [pl.BlockSpec(memory_space=pl.ANY)],
        scratch_shapes=[cells_f],
        compiler_params=pltpu.CompilerParams(vmem_limit_bytes=14 * MIB),
        cost_estimate=pl.CostEstimate(flops=3 * 10**9, bytes_accessed=8 * MIB, transcendentals=0),
        name="front",
    )(meta, saved_state, side, top_x, corner, gain, w_t, w_qkv, bsum_in)

    width = n_proj + n_chan + LANES
    rows = n_chan // math.prod(counts)
    half = math.prod(counts) // 2
    gp_out, keep, send = pl.pallas_call(
        functools.partial(outer_kernel, n_head, counts),
        out_shape=(
            tile((n_proj, n_tok)),
            jax.ShapeDtypeStruct((half, rows, width), f32),
            tile((half, rows, width)),
        ),
        in_specs=[smem] + [whole()] * 13,
        scratch_shapes=[
            pltpu.VMEM((n_tok, n_chan), bf),
            cells_t,
            pltpu.VMEM((n_head, CELLS, LANES), f32),
            cells_f,
            cells_t,
            pltpu.VMEM((n_chan, width), f32),
            pltpu.VMEM((n_head * CELLS, LANES), f32),
            pltpu.VMEM((n_head * CELLS, LANES), f32),
        ],
        compiler_params=pltpu.CompilerParams(vmem_limit_bytes=30 * MIB),
        cost_estimate=pl.CostEstimate(flops=10**10, bytes_accessed=24 * MIB, transcendentals=2**19),
        name="outer",
    )(meta, cotangent, side, top_c, corner, bias, gain, w_qkv, w_out, nrm_out, proj_out, kv_out, sums_in, bsum_in)

    def input_grad(start):
        base, *edges = pl.pallas_call(
            cells_kernel,
            out_shape=(
                tile((n_rows, n_cols, n_chan)),
                tile((n_top, n_cols + WINDOW, n_chan)),
                tile((n_rows, WINDOW, n_chan)),
            ),
            in_specs=[smem] + [whole()] * 7 + [pl.BlockSpec(memory_space=pl.ANY)],
            scratch_shapes=[pltpu.VMEM((n_rows + WINDOW, n_cols + WINDOW, n_chan), f32)],
            compiler_params=pltpu.CompilerParams(vmem_limit_bytes=24 * MIB),
            cost_estimate=pl.CostEstimate(flops=16 * 10**8, bytes_accessed=12 * MIB, transcendentals=0),
            name="cells",
        )(meta, x_in, x_out, gp_in, gp_out, cotangent, gain, w_qkv, start)
        top_back = ring(edges[0], -1, 0)

        def finish(later):
            side = pl.pallas_call(
                edge_kernel,
                out_shape=tile((n_rows, WINDOW, n_chan)),
                in_specs=[whole()] * 2 + [pl.BlockSpec(memory_space=pl.ANY)],
                compiler_params=pltpu.CompilerParams(vmem_limit_bytes=4 * MIB),
                name="edge",
            )(edges[1], top_back, later)
            return base, top_back, ring(side, 0, -1)

        return edges[1], finish

    mine, other, (base, top_back, side_back) = total_over_devices(places, keep, send, input_grad)
    edge = jnp.pad(top_back[:, WINDOW:], ((n_rows - n_top, 0), (0, 0), (0, 0)))
    edge = edge + jnp.pad(side_back, ((0, 0), (n_cols - WINDOW, 0), (0, 0)))
    state_grad = (base.astype(f32) + edge.astype(f32)).astype(bf)

    factor = 1.0 / math.sqrt(n_rows * places.n_lat * n_cols * places.n_lon)
    here = pl.BlockSpec(memory_space=pl.ANY)
    n_half = n_chan // places.c
    grads = (jax.ShapeDtypeStruct((n_chan, n_proj), f32), jax.ShapeDtypeStruct((n_chan, n_chan), f32))
    staged = [pltpu.VMEM((n_half, n_proj), f32), pltpu.VMEM((n_half, n_chan), f32), pltpu.SemaphoreType.DMA((2,))]
    qkv_grad, out_grad, small = pl.pallas_call(
        functools.partial(first_unpack_kernel, counts, n_proj, factor),
        out_shape=(*grads, jax.ShapeDtypeStruct((n_half, LANES), f32)),
        in_specs=[smem] + [whole()] * places.x,
        out_specs=(here, here, whole()),
        scratch_shapes=staged,
        compiler_params=pltpu.CompilerParams(vmem_limit_bytes=8 * MIB),
        name="unpack_mine",
    )(meta, *mine)
    qkv_grad, out_grad, gain_grad, bias_grad = pl.pallas_call(
        functools.partial(second_unpack_kernel, counts, n_proj, factor),
        out_shape=(*grads, jax.ShapeDtypeStruct((1, n_chan), f32), jax.ShapeDtypeStruct(bias_table.shape, f32)),
        in_specs=[smem] + [whole()] * places.x + [here, here, whole()],
        out_specs=(here, here, whole(), whole()),
        input_output_aliases={places.x + 1: 0, places.x + 2: 1},
        scratch_shapes=[pltpu.VMEM((n_half, LANES), f32), *staged],
        compiler_params=pltpu.CompilerParams(vmem_limit_bytes=8 * MIB),
        name="unpack_other",
    )(meta, *other, qkv_grad, out_grad, small)
    return state_grad, qkv_grad, out_grad, gain_grad.reshape(n_chan), bias_grad


def solution(mesh):
    return jax.shard_map(
        local,
        mesh=mesh,
        in_specs=(P("lat", "lon", None), P("lat", "lon", None), P("lat"), P(), P(), P(), P(), P()),
        out_specs=(P("lat", "lon", None), P(), P(), P(), P()),
        check_vma=False,
    )
```

```python
import functools
import itertools
import math

import jax
import jax.numpy as jnp
from jax import lax
from jax.experimental import pallas as pl
from jax.experimental.pallas import tpu as pltpu
from jax.sharding import PartitionSpec as P

EPSILON = 1e-05


NT = (((1,), (1,)), ((), ()))
NN = (((1,), (0,)), ((), ()))
LANES = 128
WINDOW = 8
CELLS = WINDOW * WINDOW
TOKENS = 256
MIB = 1024 * 1024


def dot(a, b, dims=NN):
    return lax.dot_general(a, b, dims, preferred_element_type=jnp.float32)


def whole(*_):
    return pl.BlockSpec(memory_space=pltpu.VMEM)


def norm_stats(x):
    cen = x - jnp.mean(x, -1, keepdims=True)
    inv = lax.rsqrt(jnp.mean(cen * cen, -1, keepdims=True) + EPSILON)
    return cen * inv, inv


def project_cells(scale, gain, wt_ref, w_ref, xf, x_out, nrm_t, proj_t, kv):
    n_tok, n_chan = xf.shape
    x_out[...] = xf[...].astype(jnp.bfloat16)
    for base in range(0, n_tok, TOKENS):
        rows = slice(base, base + TOKENS)
        x_hat, _ = norm_stats(xf[rows])
        normed_f = x_hat * gain
        normed = normed_f.astype(jnp.bfloat16)
        nrm_t[:, rows] = normed_f.T.astype(jnp.bfloat16)
        proj_t[:n_chan, rows] = (dot(wt_ref[:n_chan], normed, NT) * scale).astype(jnp.bfloat16)
        proj_t[n_chan:, rows] = dot(wt_ref[n_chan:], normed, NT).astype(jnp.bfloat16)
        kv[rows] = dot(normed, w_ref[:, n_chan:]).astype(jnp.bfloat16)


def block_diag(block, step):
    blank = jnp.zeros((step, block.shape[1]), block.dtype)
    count = block.shape[0] // step
    columns = []
    for h in range(count):
        parts = [blank] * count
        parts[h] = block[h * step : (h + 1) * step]
        columns.append(jnp.concatenate(parts, 0))
    return jnp.concatenate(columns, 1)


def attention_unit(n_chan, dim, scale, bias_ref, mask, proj_t, kv, gm_t, mix_t, gp_t, bsum_ref, pair, group):
    lanes = pl.ds(pl.multiple_of(pair * LANES, LANES), LANES)
    c0 = group * LANES
    q_t = proj_t[pl.ds(c0, LANES), lanes]
    k_t = proj_t[pl.ds(n_chan + c0, LANES), lanes]
    v_t = proj_t[pl.ds(2 * n_chan + c0, LANES), lanes]
    g_t = gm_t[pl.ds(c0, LANES), lanes]
    k_tok = kv[lanes, pl.ds(c0, LANES)]
    v_tok = kv[lanes, pl.ds(n_chan + c0, LANES)]
    q_bd = block_diag(q_t, dim)
    g_bd = block_diag(g_t, dim)
    scores = dot(k_tok, q_bd)
    grads = dot(v_tok, g_bd)
    first = lax.broadcasted_iota(jnp.int32, (CELLS, LANES), 1) < CELLS
    heads = LANES // dim
    mixed, dq, dk, dv = [], [], [], []
    for h in range(heads):
        cut = slice(h * LANES, (h + 1) * LANES)
        rows = slice(h * dim, (h + 1) * dim)
        head = group * heads + h
        s = jnp.where(first, scores[:CELLS, cut], scores[CELLS:, cut]) + bias_ref[head] + mask
        e = jnp.exp(s - jnp.max(s, 0, keepdims=True))
        a = e * (1.0 / jnp.sum(e, 0, keepdims=True))
        d = jnp.where(first, grads[:CELLS, cut], grads[CELLS:, cut])
        ad = a * d
        ds = ad - a * jnp.sum(ad, 0, keepdims=True)
        bsum_ref[head] += ds
        zero = jnp.zeros_like(a)
        a2 = jnp.concatenate([jnp.where(first, a, zero), jnp.where(first, zero, a)], 0).astype(jnp.bfloat16)
        ds2 = jnp.concatenate([jnp.where(first, ds, zero), jnp.where(first, zero, ds)], 0).astype(jnp.bfloat16)
        mixed.append(dot(v_t[rows], a2))
        dv.append(a2)
        dq.append(dot(k_t[rows], ds2) * scale)
        dk.append(ds2)
    mix_t[pl.ds(c0, LANES), lanes] = jnp.concatenate(mixed, 0).astype(jnp.bfloat16)
    gp_t[pl.ds(c0, LANES), lanes] = jnp.concatenate(dq, 0).astype(jnp.bfloat16)
    gp_t[pl.ds(n_chan + c0, LANES), lanes] = dot(q_bd, jnp.concatenate(dk, 1), NT).astype(jnp.bfloat16)
    gp_t[pl.ds(2 * n_chan + c0, LANES), lanes] = dot(g_bd, jnp.concatenate(dv, 1), NT).astype(jnp.bfloat16)


def place_row(line, shift, out, r, live=None):
    line = line.astype(jnp.float32).reshape(-1, WINDOW, line.shape[1])
    if live is not None:
        line = line * live
    line = pltpu.roll(line, WINDOW - shift, 1)
    head = lax.broadcasted_iota(jnp.int32, line.shape[1:], 0) < WINDOW - shift
    for w in range(line.shape[0] - 1):
        start = w * CELLS + r * WINDOW
        out[start : start + WINDOW] = jnp.where(head, line[w], line[w + 1])


def window_row(n_head, cf, live, wo_ref, bias_ref, go_ref, mix_t, gp_t, bsum_ref, proj_t, kv, gm_t):
    n_tok, n_chan = cf.shape
    dim = n_chan // n_head
    scale = dim ** (-0.5)
    go_ref[...] = cf[...].astype(jnp.bfloat16)
    for base in range(0, n_tok, TOKENS):
        rows = slice(base, base + TOKENS)
        gm_t[:, rows] = dot(wo_ref[...], go_ref[rows], NT).astype(jnp.bfloat16)
    mask = jnp.concatenate([(live[r][:, :LANES] - 1.0) * 1e30 for r in range(WINDOW)], 0)
    groups = n_chan // LANES

    @pl.loop(0, n_tok // LANES)
    def _(pair):
        for group in range(groups):
            attention_unit(n_chan, dim, scale, bias_ref, mask, proj_t, kv, gm_t, mix_t, gp_t, bsum_ref, pair, group)


def weight_sums(sums, nrm_t, gp_t, mix_t, go_ref, more):
    n_proj, n_chan = gp_t.shape[0], nrm_t.shape[0]
    for base in range(0, n_proj + n_chan, TOKENS):
        cols = slice(base, base + TOKENS)
        if base < n_proj:
            part = dot(nrm_t[...], gp_t[cols], NT)
        else:
            part = dot(mix_t[...], go_ref[:, base - n_proj : base - n_proj + TOKENS])
        sums[:, cols] = part if more is None else part + more[:, cols]


def inner_kernel(n_head, meta, x_ref, cot_ref, side_ref, bias_ref, gain_ref, wt_ref, w_ref, wo_ref,
                 x_out, gp_t, sums_ref, bsum_ref, go_ref, nrm_t, mix_t, xf, cf, proj_t, kv, gm_t):
    scale = (x_ref.shape[2] // n_head) ** (-0.5)
    lat, lon = meta[0], meta[1]
    live = []
    for r in range(WINDOW):
        live.append(jnp.full((WINDOW, x_ref.shape[2]), meta[6 + lat + r].astype(jnp.float32)))
        for k, (grid, out) in enumerate(((x_ref, xf), (cot_ref, cf))):
            line = jnp.concatenate([part.astype(jnp.float32) for part in (side_ref[k, lat + r], grid[lat + r])], 0)
            place_row(line, lon, out, r, live[r] if k else None)
    bsum_ref[...] = jnp.zeros_like(bsum_ref)
    project_cells(scale, gain_ref[...], wt_ref, w_ref, xf, x_out, nrm_t, proj_t, kv)
    window_row(n_head, cf, live, wo_ref, bias_ref, go_ref, mix_t, gp_t, bsum_ref, proj_t, kv, gm_t)
    weight_sums(sums_ref, nrm_t, gp_t, mix_t, go_ref, None)


def outer_line(k, e, grid, side_ref, top, corner_ref):
    n_top = top.shape[0]
    above = e < WINDOW
    up = jnp.clip(e - (WINDOW - n_top), 0, n_top - 1)
    own = jnp.maximum(e - WINDOW, 0)
    parts = jnp.where(above, corner_ref[k, up], side_ref[k, own]), jnp.where(above, top[up], grid[own])
    return jnp.concatenate([part.astype(jnp.float32) for part in parts], 0)


def front_kernel(n_head, meta, x_ref, side_ref, top, corner_ref, gain_ref, wt_ref, w_ref, _, x_out, nrm_t, proj_t, kv, xf):
    scale = (x_ref.shape[2] // n_head) ** (-0.5)
    for r in range(WINDOW):
        place_row(outer_line(0, meta[0] + r, x_ref, side_ref, top, corner_ref), meta[1], xf, r)
    project_cells(scale, gain_ref[...], wt_ref, w_ref, xf, x_out, nrm_t, proj_t, kv)


def outer_kernel(n_head, counts, meta, cot_ref, side_ref, top, corner_ref, bias_ref, gain_ref, w_ref, wo_ref,
                 nrm_t, proj_t, kv, sums_in, bsum_in,
                 gp_t, keep_ref, send_ref,
                 go_ref, mix_t, bsum_ref, cf, gm_t, sums, spread_a, spread_b):
    n_chan = gain_ref.shape[1]
    up_mask = corner_ref[0, WINDOW - 1].astype(jnp.float32) * meta[5].astype(jnp.float32)
    line_of = lax.broadcasted_iota(jnp.int32, up_mask.shape, 0)
    live = []
    for r in range(WINDOW):
        e = meta[0] + r
        row_live = jnp.full((WINDOW, n_chan), meta[6 + jnp.maximum(e - WINDOW, 0)].astype(jnp.float32))
        up_live = jnp.sum(jnp.where(line_of == e, up_mask, 0.0), 0, keepdims=True)
        live.append(jnp.where(e < WINDOW, jnp.broadcast_to(up_live, row_live.shape), row_live))
        place_row(outer_line(1, e, cot_ref, side_ref, top, corner_ref), meta[1], cf, r, live[r])
    bsum_ref[...] = bsum_in[...]
    window_row(n_head, cf, live, wo_ref, bias_ref, go_ref, mix_t, gp_t, bsum_ref, proj_t, kv, gm_t)

    n_proj = 3 * n_chan
    weight_sums(sums, nrm_t, gp_t, mix_t, go_ref, sums_in)
    gain_sum = jnp.sum(sums[:, :n_proj] * w_ref[...].astype(jnp.float32), 1, keepdims=True)

    width = 2 * LANES
    cell = lax.broadcasted_iota(jnp.int32, (LANES, width), 0) % CELLS
    lane = lax.broadcasted_iota(jnp.int32, (LANES, width), 1)
    place = (cell // WINDOW) * 16 + cell % WINDOW + 119
    onehot = (lane == place).astype(jnp.float32).astype(jnp.bfloat16)
    flat = bsum_ref[...].reshape(n_head * CELLS, LANES)
    high = flat.astype(jnp.bfloat16)
    low = (flat - high.astype(jnp.float32)).astype(jnp.bfloat16)
    spread = dot(high, onehot) + dot(low, onehot)
    spread_a[...] = spread[:, :LANES]
    spread_b[...] = spread[:, LANES:]
    bias_sum = jnp.zeros((n_head, width), jnp.float32)
    for j in range(CELLS):
        row = jnp.concatenate([ref[pl.ds(j, n_head, stride=CELLS), :] for ref in (spread_a, spread_b)], 1)
        by = (j // WINDOW) * 16 + j % WINDOW
        bias_sum += pltpu.roll(row, width - by, 1) if by else row
    tail = lax.broadcasted_iota(jnp.int32, (n_chan, LANES), 1) == LANES - 1
    bias_rows = jnp.concatenate(
        [bias_sum[:, :LANES], bias_sum[:, LANES:], jnp.zeros((n_chan - 2 * n_head, LANES), jnp.float32)], 0
    )
    sums[:, n_proj + n_chan :] = jnp.where(tail, gain_sum * (1.0 / gain_col(gain_ref)), bias_rows)

    n_c, n_x, n_y = counts
    rows = n_chan // (n_c * n_x * n_y)
    for c in range(n_c):
        for x in range(n_x):
            for y in range(n_y):
                chunk = sums[((c * n_x + x) * n_y + y) * rows : ((c * n_x + x) * n_y + y + 1) * rows]
                at = lax.rem(x - meta[3] + n_x, n_x) * n_y + lax.rem(y - meta[4] + n_y, n_y)

                @pl.when(meta[2] == c)
                def _():
                    keep_ref[at] = chunk

                @pl.when(meta[2] != c)
                def _():
                    send_ref[at] = chunk.astype(jnp.bfloat16)


def gain_col(gain_ref):
    n_chan = gain_ref.shape[1]
    return jnp.broadcast_to(gain_ref[...], (LANES, n_chan)).T[:, :1]


def cells_kernel(meta, xi_ref, xo_ref, gpi_ref, gpo_ref, cot_ref, gain_ref, w_ref, _, base_ref, top_ref, side_ref, ext):
    n_rows, n_cols, n_chan = cot_ref.shape
    lat, lon = meta[0], meta[1]
    ext[...] = jnp.zeros_like(ext)
    for part, (x_ref, gp_t) in enumerate(((xo_ref, gpo_ref), (xi_ref, gpi_ref))):
        n_tok = x_ref.shape[0]
        cells = []
        for base in range(0, n_tok, TOKENS):
            rows = slice(base, base + TOKENS)
            x_hat, inv = norm_stats(x_ref[rows].astype(jnp.float32))
            g = dot(w_ref[...], gp_t[:, rows]).T * gain_ref[...]
            cells.append(inv * (g - jnp.mean(g, -1, keepdims=True) - x_hat * jnp.mean(g * x_hat, -1, keepdims=True)))
        blank = jnp.zeros((1, WINDOW, n_chan), jnp.float32)
        head = lax.broadcasted_iota(jnp.int32, (WINDOW, n_chan), 0) < lon
        for r in range(WINDOW):
            row = jnp.stack(
                [
                    cells[w * CELLS // TOKENS][w * CELLS % TOKENS + r * WINDOW :][:WINDOW]
                    for w in range(n_tok // CELLS)
                ],
                0,
            )
            row = jnp.concatenate([blank, pltpu.roll(row, lon, 1), blank], 0)
            for t in range(row.shape[0] - 1):
                ext[lat + part * WINDOW + r, t * WINDOW : (t + 1) * WINDOW, :] = jnp.where(head, row[t], row[t + 1])
    for r in range(n_rows):
        base_ref[r] = (cot_ref[r].astype(jnp.float32) + ext[WINDOW + r, WINDOW:]).astype(jnp.bfloat16)
        side_ref[r] = ext[WINDOW + r, :WINDOW].astype(jnp.bfloat16)
    n_top = top_ref.shape[0]
    for r in range(n_top):
        top_ref[r] = ext[WINDOW - n_top + r].astype(jnp.bfloat16)


def edge_kernel(side_ref, top_ref, _, out_ref):
    n_rows, n_top = side_ref.shape[0], top_ref.shape[0]
    for r in range(n_rows):
        edge = side_ref[r].astype(jnp.float32)
        at = r - n_rows + n_top
        if at >= 0:
            edge = edge + top_ref[at].astype(jnp.float32)[:WINDOW]
        out_ref[r] = edge.astype(jnp.bfloat16)


def prepare_kernel(bias_ref, w_ref, full_ref, wt_ref):
    n_head, n_gap = bias_ref.shape
    span = 2 * WINDOW - 1
    width = 2 * LANES
    lane = lax.broadcasted_iota(jnp.int32, (width, LANES), 0)
    cell = lax.broadcasted_iota(jnp.int32, (width, LANES), 1) % CELLS
    place = cell // WINDOW * span + cell % WINDOW + n_gap // 2
    onehot = (lane == place).astype(jnp.float32).astype(jnp.bfloat16)
    table = jnp.concatenate([bias_ref[...], jnp.zeros((n_head, width - n_gap), jnp.float32)], 1)
    for h in range(n_head):
        line = jnp.broadcast_to(table[h : h + 1], (WINDOW, width))
        rows = [pltpu.roll(line, r * span, 1, stride=1, stride_axis=0) for r in range(WINDOW)]
        rest = jnp.concatenate(rows, 0)
        total = jnp.zeros((CELLS, LANES), jnp.float32)
        for _ in range(3):
            part = rest.astype(jnp.bfloat16)
            total += dot(part, onehot)
            rest = rest - part.astype(jnp.float32)
        full_ref[h] = total
    wt_ref[...] = w_ref[...].T


def pack_kernel(n_top, x_ref, cot_ref, mask, side_ref, top_x, top_c, corner_ref, edges, sems):
    n_rows, n_cols, n_chan = x_ref.shape
    copies = []
    for k, (ref, top) in enumerate(((x_ref, top_x), (cot_ref, top_c))):
        copies.append(pltpu.make_async_copy(ref.at[:, pl.ds(n_cols - 2 * WINDOW, 2 * WINDOW)], edges.at[k], sems.at[2 * k]))
        copies.append(pltpu.make_async_copy(ref.at[pl.ds(n_rows - n_top, n_top)], top, sems.at[2 * k + 1]))
    for copy in copies:
        copy.start()
    for k in range(2):
        copies[2 * k].wait()
        for r in range(n_rows):
            edge = edges[k, r][WINDOW:]
            side_ref[k, r] = edge
            at = r - n_rows + n_top
            if at >= 0:
                corner_ref[k, at] = edge
    line = lax.broadcasted_iota(jnp.int32, (WINDOW, n_chan), 0)
    live = jnp.zeros((WINDOW, n_chan), jnp.float32)
    for r in range(WINDOW):
        live = jnp.where(line == r, mask[n_rows - WINDOW + r].astype(jnp.float32), live)
    corner_ref[0, n_top] = live.astype(jnp.bfloat16)
    corner_ref[1, n_top] = live.astype(jnp.bfloat16)
    copies[1].wait()
    copies[3].wait()


def first_add_kernel(keep_ref, got_ref, own_ref, *send_refs):
    size = own_ref.shape[0]
    for k in range(len(send_refs) + 1):
        cut = slice(k * size, (k + 1) * size)
        total = keep_ref[cut] + got_ref[cut].astype(jnp.float32)
        if k:
            send_refs[k - 1][...] = total.astype(jnp.bfloat16)
        else:
            own_ref[...] = total


def next_add_kernel(n_got, n_more, own_ref, *refs):
    got, (out_ref, *send_refs) = refs[:n_got], refs[n_got + n_more :]
    size = out_ref.shape[0]
    for k in range(len(send_refs) + 1):
        cut = slice(k * size, (k + 1) * size)
        total = own_ref[cut]
        for ref in got:
            total = total + ref[cut].astype(jnp.float32)
        if k:
            send_refs[k - 1][...] = total.astype(jnp.bfloat16)
        else:
            out_ref[...] = total.astype(out_ref.dtype)


def join_kernel(n_got, *refs):
    for k in range(n_got):
        refs[-1][k : k + 1] = refs[k][...]


def tree_add_kernel(*refs):
    parts = [ref[...].astype(jnp.float32) for ref in refs[:-1]]
    while len(parts) > 1:
        parts = [parts[k] + parts[k + 1] for k in range(0, len(parts), 2)]
    refs[-1][...] = parts[0].astype(jnp.bfloat16)


def unpack_kernel(counts, n_proj, factor, meta, *refs):
    n_c, n_x, n_y = counts
    parts, (qkv_ref, out_ref, gain_ref, bias_ref, qkv_all, out_all, small, sems) = refs[: 2 * n_x], refs[2 * n_x :]
    rows = parts[0].shape[1]
    n_chan = out_all.shape[0]
    n_half = n_chan // n_c
    copies = []
    for half in range(2):
        c = meta[2] if half == 0 else 1 - meta[2]
        for k in range(n_x):
            x = lax.rem(meta[3] + k, n_x)
            for j in range(n_y):
                y = lax.rem(meta[4] + j, n_y)
                chunk = parts[half * n_x + k][j].astype(jnp.float32) * factor
                to = pl.ds(pl.multiple_of(((c * n_x + x) * n_y + y) * rows, rows), rows)
                qkv_all[to] = chunk[:, :n_proj]
                out_all[to] = chunk[:, n_proj : n_proj + n_chan]
                small[to] = chunk[:, n_proj + n_chan :]
        place = pl.ds(pl.multiple_of(c * n_half, n_half), n_half)
        for k, (ref, full) in enumerate(((qkv_ref, qkv_all), (out_ref, out_all))):
            copies.append(pltpu.make_async_copy(full.at[place], ref.at[place], sems.at[2 * half + k]))
            copies[-1].start()
    gain_ref[...] = small[...].T[LANES - 1 :]
    n_head, n_gap = bias_ref.shape
    span = 2 * WINDOW - 1
    wide = jnp.concatenate([small[:n_head], small[n_head : 2 * n_head]], 1)
    lane = lax.broadcasted_iota(jnp.int32, wide.shape, 1)
    bias = jnp.zeros_like(wide)
    for k in range(span):
        moved = pltpu.roll(wide, 2 * LANES - k, 1) if k else wide
        bias = jnp.where((lane >= k * span) & (lane < (k + 1) * span), moved, bias)
    bias_ref[...] = bias[:, :n_gap]
    for copy in copies:
        copy.wait()


class Places:
    def __init__(self):
        self.n_lat, self.n_lon = lax.axis_size("lat"), lax.axis_size("lon")
        self.c = 2
        self.x = min(4, self.n_lon // self.c)
        self.y_low = self.n_lon // (self.c * self.x)
        self.y_high = 2
        self.y = self.y_low * self.y_high
        self.z = self.n_lat // self.y_high

    def index(self, z, y, x, c):
        high, low = divmod(y, self.y_low)
        return (z * self.y_high + high) * self.n_lon + (low * self.x + x) * self.c + c

    def mine(self):
        lat, lon = lax.axis_index("lat"), lax.axis_index("lon")
        return (
            lon % self.c,
            lon // self.c % self.x,
            lat % self.y_high * self.y_low + lon // (self.c * self.x),
        )

    def move(self, array, to):
        every = itertools.product(range(self.z), range(self.y), range(self.x), range(self.c))
        pairs = [(self.index(*at), self.index(*to(*at))) for at in every]
        return lax.ppermute(array, ("lat", "lon"), pairs)

    def by_c(self, array):
        return self.move(array, lambda z, y, x, c: (z, y, x, 1 - c))

    def by_x(self, array, k):
        return self.move(array, lambda z, y, x, c: (z, y, (x + k) % self.x, c))

    def by_y(self, array, k):
        return self.move(array, lambda z, y, x, c: (z, (y + k) % self.y, x, c))

    def by_z(self, array, bits):
        return self.move(array, lambda z, y, x, c: (z ^ bits, y, x, c))


def small_call(kernel, outs, name, limit, *args):
    return pl.pallas_call(
        kernel,
        out_shape=outs,
        compiler_params=pltpu.CompilerParams(vmem_limit_bytes=limit * MIB),
        name=name,
    )(*args)


def total_over_devices(places, keep, send, beside):
    shape = keep.shape[1:]
    bf = functools.partial(jax.ShapeDtypeStruct, dtype=jnp.bfloat16)
    got = places.by_c(send)
    own = jax.ShapeDtypeStruct((places.y, *shape), jnp.float32)
    own, *sends = small_call(first_add_kernel, (own,) + (bf((places.y, *shape)),) * (places.x - 1), "add_c", 12, keep, got)
    got = [places.by_x(part, k + 1) for k, part in enumerate(sends)]
    nxt = jax.ShapeDtypeStruct((1, *shape), jnp.float32)
    ahead, finish = beside(own)
    own, *sends = pl.pallas_call(
        functools.partial(next_add_kernel, len(got), 1),
        out_shape=(nxt,) + (bf((1, *shape)),) * (places.y - 1),
        in_specs=[whole()] * (1 + len(got)) + [pl.BlockSpec(memory_space=pl.ANY)],
        compiler_params=pltpu.CompilerParams(vmem_limit_bytes=6 * MIB),
        name="add_x",
    )(own, *got, ahead)
    got = [places.by_y(part, k + 1) for k, part in enumerate(sends)]
    (mine,) = small_call(functools.partial(next_add_kernel, len(got), 0), (bf((1, *shape)),), "add_y", 4, own, *got)
    for group in {1: (), 2: ((1,),), 4: ((1, 2, 3),), 8: ((1, 2, 3), (6,))}[places.z]:
        others = [places.by_z(mine, bits) for bits in group]
        mine = small_call(tree_add_kernel, bf((1, *shape)), "add_z", 2, mine, *others)
    parts = [mine] + [places.by_y(mine, -k) for k in range(1, places.y)]
    mine = small_call(functools.partial(join_kernel, len(parts)), bf((places.y, *shape)), "join", 4, *parts)
    result = finish(mine)
    mine = [mine] + [places.by_x(mine, -k) for k in range(1, places.x)]
    return mine, [places.by_c(part) for part in mine], result


def ring(array, lat, lon):
    n_lat, n_lon = lax.axis_size("lat"), lax.axis_size("lon")
    pairs = [
        (i * n_lon + j, (i + lat) * n_lon + (j + lon) % n_lon)
        for i in range(n_lat)
        for j in range(n_lon)
        if 0 <= i + lat < n_lat
    ]
    return lax.ppermute(array, ("lat", "lon"), pairs)


def local(saved_state, cotangent, row_mask, shifts, norm_gain, w_qkv, w_out, bias_table):
    n_rows, n_cols, n_chan = saved_state.shape
    n_head = bias_table.shape[0]
    n_proj = w_qkv.shape[1]
    n_tok = n_rows // 2 * n_cols
    n_top = WINDOW - 1
    places = Places()
    counts = (places.c, places.x, places.y)
    bf, f32 = jnp.bfloat16, jnp.float32

    smem = pl.BlockSpec(memory_space=pltpu.SMEM)
    tile = functools.partial(jax.ShapeDtypeStruct, dtype=bf)
    side, top_x, top_c, corner = pl.pallas_call(
        functools.partial(pack_kernel, n_top),
        out_shape=(
            tile((2, n_rows, WINDOW, n_chan)),
            tile((n_top, n_cols, n_chan)),
            tile((n_top, n_cols, n_chan)),
            tile((2, WINDOW, WINDOW, n_chan)),
        ),
        in_specs=[pl.BlockSpec(memory_space=pltpu.HBM), pl.BlockSpec(memory_space=pltpu.HBM), smem],
        scratch_shapes=[pltpu.VMEM((2, n_rows, 2 * WINDOW, n_chan), bf), pltpu.SemaphoreType.DMA((4,))],
        compiler_params=pltpu.CompilerParams(vmem_limit_bytes=58 * MIB),
        name="pack",
    )(saved_state, cotangent, row_mask)
    side = ring(side, 0, 1)
    top_x = ring(top_x, 1, 0)
    top_c = ring(top_c, 1, 0)
    corner = ring(corner, 1, 1)
    at = jnp.stack(places.mine()).astype(jnp.int32)
    gain = norm_gain.reshape(1, n_chan)
    bias, w_t = pl.pallas_call(
        prepare_kernel,
        out_shape=(jax.ShapeDtypeStruct((n_head, CELLS, LANES), f32), tile((n_proj, n_chan))),
        compiler_params=pltpu.CompilerParams(vmem_limit_bytes=16 * MIB),
        cost_estimate=pl.CostEstimate(flops=10**9, bytes_accessed=4 * MIB, transcendentals=0),
        name="prepare",
    )(bias_table, w_qkv)

    below = jnp.minimum(lax.axis_index("lat"), 1).astype(jnp.int32).reshape(1)
    meta = jnp.concatenate([shifts, at, below, row_mask])
    cells_f, cells_t = pltpu.VMEM((n_tok, n_chan), f32), pltpu.VMEM((n_chan, n_tok), bf)
    x_in, gp_in, sums_in, bsum_in = pl.pallas_call(
        functools.partial(inner_kernel, n_head),
        out_shape=(
            tile((n_tok, n_chan)),
            tile((n_proj, n_tok)),
            jax.ShapeDtypeStruct((n_chan, n_proj + n_chan), f32),
            jax.ShapeDtypeStruct((n_head, CELLS, LANES), f32),
        ),
        in_specs=[smem] + [whole()] * 8,
        scratch_shapes=[
            pltpu.VMEM((n_tok, n_chan), bf),
            cells_t,
            cells_t,
            cells_f,
            cells_f,
            pltpu.VMEM((n_proj, n_tok), bf),
            pltpu.VMEM((n_tok, 2 * n_chan), bf),
            cells_t,
        ],
        compiler_params=pltpu.CompilerParams(vmem_limit_bytes=24 * MIB),
        cost_estimate=pl.CostEstimate(flops=8 * 10**9, bytes_accessed=16 * MIB, transcendentals=2**19),
        name="inner",
    )(meta, saved_state, cotangent, side, bias, gain, w_t, w_qkv, w_out)
    x_out, nrm_out, proj_out, kv_out = pl.pallas_call(
        functools.partial(front_kernel, n_head),
        out_shape=(tile((n_tok, n_chan)), tile((n_chan, n_tok)), tile((n_proj, n_tok)), tile((n_tok, 2 * n_chan))),
        in_specs=[smem] + [whole()] * 7 + [pl.BlockSpec(memory_space=pl.ANY)],
        scratch_shapes=[cells_f],
        compiler_params=pltpu.CompilerParams(vmem_limit_bytes=14 * MIB),
        cost_estimate=pl.CostEstimate(flops=3 * 10**9, bytes_accessed=8 * MIB, transcendentals=0),
        name="front",
    )(meta, saved_state, side, top_x, corner, gain, w_t, w_qkv, bsum_in)

    width = n_proj + n_chan + LANES
    rows = n_chan // math.prod(counts)
    half = math.prod(counts) // 2
    gp_out, keep, send = pl.pallas_call(
        functools.partial(outer_kernel, n_head, counts),
        out_shape=(
            tile((n_proj, n_tok)),
            jax.ShapeDtypeStruct((half, rows, width), f32),
            tile((half, rows, width)),
        ),
        in_specs=[smem] + [whole()] * 13,
        scratch_shapes=[
            pltpu.VMEM((n_tok, n_chan), bf),
            cells_t,
            pltpu.VMEM((n_head, CELLS, LANES), f32),
            cells_f,
            cells_t,
            pltpu.VMEM((n_chan, width), f32),
            pltpu.VMEM((n_head * CELLS, LANES), f32),
            pltpu.VMEM((n_head * CELLS, LANES), f32),
        ],
        compiler_params=pltpu.CompilerParams(vmem_limit_bytes=30 * MIB),
        cost_estimate=pl.CostEstimate(flops=10**10, bytes_accessed=24 * MIB, transcendentals=2**19),
        name="outer",
    )(meta, cotangent, side, top_c, corner, bias, gain, w_qkv, w_out, nrm_out, proj_out, kv_out, sums_in, bsum_in)

    def input_grad(start):
        base, *edges = pl.pallas_call(
            cells_kernel,
            out_shape=(
                tile((n_rows, n_cols, n_chan)),
                tile((n_top, n_cols + WINDOW, n_chan)),
                tile((n_rows, WINDOW, n_chan)),
            ),
            in_specs=[smem] + [whole()] * 7 + [pl.BlockSpec(memory_space=pl.ANY)],
            scratch_shapes=[pltpu.VMEM((n_rows + WINDOW, n_cols + WINDOW, n_chan), f32)],
            compiler_params=pltpu.CompilerParams(vmem_limit_bytes=24 * MIB),
            cost_estimate=pl.CostEstimate(flops=16 * 10**8, bytes_accessed=12 * MIB, transcendentals=0),
            name="cells",
        )(meta, x_in, x_out, gp_in, gp_out, cotangent, gain, w_qkv, start)
        top_back = ring(edges[0], -1, 0)

        def finish(later):
            side = pl.pallas_call(
                edge_kernel,
                out_shape=tile((n_rows, WINDOW, n_chan)),
                in_specs=[whole()] * 2 + [pl.BlockSpec(memory_space=pl.ANY)],
                compiler_params=pltpu.CompilerParams(vmem_limit_bytes=4 * MIB),
                name="edge",
            )(edges[1], top_back, later)
            return base, top_back, ring(side, 0, -1)

        return edges[1], finish

    mine, other, (base, top_back, side_back) = total_over_devices(places, keep, send, input_grad)
    edge = jnp.pad(top_back[:, WINDOW:], ((n_rows - n_top, 0), (0, 0), (0, 0)))
    edge = edge + jnp.pad(side_back, ((0, 0), (n_cols - WINDOW, 0), (0, 0)))
    state_grad = (base.astype(f32) + edge.astype(f32)).astype(bf)

    factor = 1.0 / math.sqrt(n_rows * places.n_lat * n_cols * places.n_lon)
    here = pl.BlockSpec(memory_space=pl.ANY)
    qkv_grad, out_grad, gain_grad, bias_grad = pl.pallas_call(
        functools.partial(unpack_kernel, counts, n_proj, factor),
        out_shape=(
            jax.ShapeDtypeStruct((n_chan, n_proj), f32),
            jax.ShapeDtypeStruct((n_chan, n_chan), f32),
            jax.ShapeDtypeStruct((1, n_chan), f32),
            jax.ShapeDtypeStruct(bias_table.shape, f32),
        ),
        in_specs=[smem] + [whole()] * (2 * places.x),
        out_specs=(here, here, whole(), whole()),
        scratch_shapes=[
            pltpu.VMEM((n_chan, n_proj), f32),
            pltpu.VMEM((n_chan, n_chan), f32),
            pltpu.VMEM((n_chan, LANES), f32),
            pltpu.SemaphoreType.DMA((4,)),
        ],
        compiler_params=pltpu.CompilerParams(vmem_limit_bytes=16 * MIB),
        name="unpack",
    )(meta, *mine, *other)
    return state_grad, qkv_grad, out_grad, gain_grad.reshape(n_chan), bias_grad


def solution(mesh):
    return jax.shard_map(
        local,
        mesh=mesh,
        in_specs=(P("lat", "lon", None), P("lat", "lon", None), P("lat"), P(), P(), P(), P(), P()),
        out_specs=(P("lat", "lon", None), P(), P(), P(), P()),
        check_vma=False,
    )
```

```python
import functools
import itertools
import math

import jax
import jax.numpy as jnp
from jax import lax
from jax.experimental import pallas as pl
from jax.experimental.pallas import tpu as pltpu
from jax.sharding import PartitionSpec as P

EPSILON = 1e-05


NT = (((1,), (1,)), ((), ()))
NN = (((1,), (0,)), ((), ()))
LANES = 128
WINDOW = 8
CELLS = WINDOW * WINDOW
TOKENS = 256
MIB = 1024 * 1024


def dot(a, b, dims=NN):
    return lax.dot_general(a, b, dims, preferred_element_type=jnp.float32)


def whole(*_):
    return pl.BlockSpec(memory_space=pltpu.VMEM)


def norm_stats(x):
    cen = x - jnp.mean(x, -1, keepdims=True)
    inv = lax.rsqrt(jnp.mean(cen * cen, -1, keepdims=True) + EPSILON)
    return cen * inv, inv


def project_cells(scale, gain, wt_ref, w_ref, xf, x_out, nrm_t, proj_t, kv):
    n_tok, n_chan = xf.shape
    x_out[...] = xf[...].astype(jnp.bfloat16)
    for base in range(0, n_tok, TOKENS):
        rows = slice(base, base + TOKENS)
        x_hat, _ = norm_stats(xf[rows])
        normed_f = x_hat * gain
        normed = normed_f.astype(jnp.bfloat16)
        nrm_t[:, rows] = normed_f.T.astype(jnp.bfloat16)
        proj_t[:n_chan, rows] = (dot(wt_ref[:n_chan], normed, NT) * scale).astype(jnp.bfloat16)
        proj_t[n_chan:, rows] = dot(wt_ref[n_chan:], normed, NT).astype(jnp.bfloat16)
        kv[rows] = dot(normed, w_ref[:, n_chan:]).astype(jnp.bfloat16)


def block_diag(block, step):
    blank = jnp.zeros((step, block.shape[1]), block.dtype)
    count = block.shape[0] // step
    columns = []
    for h in range(count):
        parts = [blank] * count
        parts[h] = block[h * step : (h + 1) * step]
        columns.append(jnp.concatenate(parts, 0))
    return jnp.concatenate(columns, 1)


def attention_unit(n_chan, dim, scale, bias_ref, mask, proj_t, kv, gm_t, mix_t, gp_t, bsum_ref, pair, group):
    lanes = pl.ds(pl.multiple_of(pair * LANES, LANES), LANES)
    c0 = group * LANES
    q_t = proj_t[pl.ds(c0, LANES), lanes]
    k_t = proj_t[pl.ds(n_chan + c0, LANES), lanes]
    v_t = proj_t[pl.ds(2 * n_chan + c0, LANES), lanes]
    g_t = gm_t[pl.ds(c0, LANES), lanes]
    k_tok = kv[lanes, pl.ds(c0, LANES)]
    v_tok = kv[lanes, pl.ds(n_chan + c0, LANES)]
    q_bd = block_diag(q_t, dim)
    g_bd = block_diag(g_t, dim)
    scores = dot(k_tok, q_bd)
    grads = dot(v_tok, g_bd)
    first = lax.broadcasted_iota(jnp.int32, (CELLS, LANES), 1) < CELLS
    heads = LANES // dim
    mixed, dq, dk, dv = [], [], [], []
    for h in range(heads):
        cut = slice(h * LANES, (h + 1) * LANES)
        rows = slice(h * dim, (h + 1) * dim)
        head = group * heads + h
        s = jnp.where(first, scores[:CELLS, cut], scores[CELLS:, cut]) + bias_ref[head] + mask
        e = jnp.exp(s - jnp.max(s, 0, keepdims=True))
        a = e * (1.0 / jnp.sum(e, 0, keepdims=True))
        d = jnp.where(first, grads[:CELLS, cut], grads[CELLS:, cut])
        ad = a * d
        ds = ad - a * jnp.sum(ad, 0, keepdims=True)
        bsum_ref[head] += ds
        zero = jnp.zeros_like(a)
        a2 = jnp.concatenate([jnp.where(first, a, zero), jnp.where(first, zero, a)], 0).astype(jnp.bfloat16)
        ds2 = jnp.concatenate([jnp.where(first, ds, zero), jnp.where(first, zero, ds)], 0).astype(jnp.bfloat16)
        mixed.append(dot(v_t[rows], a2))
        dv.append(a2)
        dq.append(dot(k_t[rows], ds2) * scale)
        dk.append(ds2)
    mix_t[pl.ds(c0, LANES), lanes] = jnp.concatenate(mixed, 0).astype(jnp.bfloat16)
    gp_t[pl.ds(c0, LANES), lanes] = jnp.concatenate(dq, 0).astype(jnp.bfloat16)
    gp_t[pl.ds(n_chan + c0, LANES), lanes] = dot(q_bd, jnp.concatenate(dk, 1), NT).astype(jnp.bfloat16)
    gp_t[pl.ds(2 * n_chan + c0, LANES), lanes] = dot(g_bd, jnp.concatenate(dv, 1), NT).astype(jnp.bfloat16)


def place_row(line, shift, out, r, live=None):
    line = line.astype(jnp.float32).reshape(-1, WINDOW, line.shape[1])
    if live is not None:
        line = line * live
    line = pltpu.roll(line, WINDOW - shift, 1)
    head = lax.broadcasted_iota(jnp.int32, line.shape[1:], 0) < WINDOW - shift
    for w in range(line.shape[0] - 1):
        start = w * CELLS + r * WINDOW
        out[start : start + WINDOW] = jnp.where(head, line[w], line[w + 1])


def window_row(n_head, cf, live, wo_ref, bias_ref, go_ref, mix_t, gp_t, bsum_ref, proj_t, kv, gm_t):
    n_tok, n_chan = cf.shape
    dim = n_chan // n_head
    scale = dim ** (-0.5)
    go_ref[...] = cf[...].astype(jnp.bfloat16)
    for base in range(0, n_tok, TOKENS):
        rows = slice(base, base + TOKENS)
        gm_t[:, rows] = dot(wo_ref[...], go_ref[rows], NT).astype(jnp.bfloat16)
    mask = jnp.concatenate([(live[r][:, :LANES] - 1.0) * 1e30 for r in range(WINDOW)], 0)
    groups = n_chan // LANES

    @pl.loop(0, n_tok // LANES, unroll=2)
    def _(pair):
        for group in range(groups):
            attention_unit(n_chan, dim, scale, bias_ref, mask, proj_t, kv, gm_t, mix_t, gp_t, bsum_ref, pair, group)


def weight_sums(sums, nrm_t, gp_t, mix_t, go_ref, more):
    n_proj, n_chan = gp_t.shape[0], nrm_t.shape[0]
    for base in range(0, n_proj + n_chan, TOKENS):
        cols = slice(base, base + TOKENS)
        if base < n_proj:
            part = dot(nrm_t[...], gp_t[cols], NT)
        else:
            part = dot(mix_t[...], go_ref[:, base - n_proj : base - n_proj + TOKENS])
        sums[:, cols] = part if more is None else part + more[:, cols]


def inner_kernel(n_head, meta, x_ref, cot_ref, side_ref, bias_ref, gain_ref, wt_ref, w_ref, wo_ref,
                 x_out, gp_t, sums_ref, bsum_ref, go_ref, nrm_t, mix_t, xf, cf, proj_t, kv, gm_t):
    scale = (x_ref.shape[2] // n_head) ** (-0.5)
    lat, lon = meta[0], meta[1]
    live = []
    for r in range(WINDOW):
        live.append(jnp.full((WINDOW, x_ref.shape[2]), meta[6 + lat + r].astype(jnp.float32)))
        for k, (grid, out) in enumerate(((x_ref, xf), (cot_ref, cf))):
            line = jnp.concatenate([part.astype(jnp.float32) for part in (side_ref[k, lat + r], grid[lat + r])], 0)
            place_row(line, lon, out, r, live[r] if k else None)
    bsum_ref[...] = jnp.zeros_like(bsum_ref)
    project_cells(scale, gain_ref[...], wt_ref, w_ref, xf, x_out, nrm_t, proj_t, kv)
    window_row(n_head, cf, live, wo_ref, bias_ref, go_ref, mix_t, gp_t, bsum_ref, proj_t, kv, gm_t)
    weight_sums(sums_ref, nrm_t, gp_t, mix_t, go_ref, None)


def outer_line(k, e, grid, side_ref, top, corner_ref):
    n_top = top.shape[0]
    above = e < WINDOW
    up = jnp.clip(e - (WINDOW - n_top), 0, n_top - 1)
    own = jnp.maximum(e - WINDOW, 0)
    parts = jnp.where(above, corner_ref[k, up], side_ref[k, own]), jnp.where(above, top[up], grid[own])
    return jnp.concatenate([part.astype(jnp.float32) for part in parts], 0)


def front_kernel(n_head, meta, x_ref, side_ref, top, corner_ref, gain_ref, wt_ref, w_ref, _, x_out, nrm_t, proj_t, kv, xf):
    scale = (x_ref.shape[2] // n_head) ** (-0.5)
    for r in range(WINDOW):
        place_row(outer_line(0, meta[0] + r, x_ref, side_ref, top, corner_ref), meta[1], xf, r)
    project_cells(scale, gain_ref[...], wt_ref, w_ref, xf, x_out, nrm_t, proj_t, kv)


def outer_kernel(n_head, counts, meta, cot_ref, side_ref, top, corner_ref, bias_ref, gain_ref, w_ref, wo_ref,
                 nrm_t, proj_t, kv, sums_in, bsum_in,
                 gp_t, keep_ref, send_ref,
                 go_ref, mix_t, bsum_ref, cf, gm_t, sums, spread_a, spread_b):
    n_chan = gain_ref.shape[1]
    up_mask = corner_ref[0, WINDOW - 1].astype(jnp.float32) * meta[5].astype(jnp.float32)
    line_of = lax.broadcasted_iota(jnp.int32, up_mask.shape, 0)
    live = []
    for r in range(WINDOW):
        e = meta[0] + r
        row_live = jnp.full((WINDOW, n_chan), meta[6 + jnp.maximum(e - WINDOW, 0)].astype(jnp.float32))
        up_live = jnp.sum(jnp.where(line_of == e, up_mask, 0.0), 0, keepdims=True)
        live.append(jnp.where(e < WINDOW, jnp.broadcast_to(up_live, row_live.shape), row_live))
        place_row(outer_line(1, e, cot_ref, side_ref, top, corner_ref), meta[1], cf, r, live[r])
    bsum_ref[...] = bsum_in[...]
    window_row(n_head, cf, live, wo_ref, bias_ref, go_ref, mix_t, gp_t, bsum_ref, proj_t, kv, gm_t)

    n_proj = 3 * n_chan
    weight_sums(sums, nrm_t, gp_t, mix_t, go_ref, sums_in)
    gain_sum = jnp.sum(sums[:, :n_proj] * w_ref[...].astype(jnp.float32), 1, keepdims=True)

    width = 2 * LANES
    cell = lax.broadcasted_iota(jnp.int32, (LANES, width), 0) % CELLS
    lane = lax.broadcasted_iota(jnp.int32, (LANES, width), 1)
    place = (cell // WINDOW) * 16 + cell % WINDOW + 119
    onehot = (lane == place).astype(jnp.float32).astype(jnp.bfloat16)
    flat = bsum_ref[...].reshape(n_head * CELLS, LANES)
    high = flat.astype(jnp.bfloat16)
    low = (flat - high.astype(jnp.float32)).astype(jnp.bfloat16)
    spread = dot(high, onehot) + dot(low, onehot)
    spread_a[...] = spread[:, :LANES]
    spread_b[...] = spread[:, LANES:]
    bias_sum = jnp.zeros((n_head, width), jnp.float32)
    for j in range(CELLS):
        row = jnp.concatenate([ref[pl.ds(j, n_head, stride=CELLS), :] for ref in (spread_a, spread_b)], 1)
        by = (j // WINDOW) * 16 + j % WINDOW
        bias_sum += pltpu.roll(row, width - by, 1) if by else row
    tail = lax.broadcasted_iota(jnp.int32, (n_chan, LANES), 1) == LANES - 1
    bias_rows = jnp.concatenate(
        [bias_sum[:, :LANES], bias_sum[:, LANES:], jnp.zeros((n_chan - 2 * n_head, LANES), jnp.float32)], 0
    )
    sums[:, n_proj + n_chan :] = jnp.where(tail, gain_sum * (1.0 / gain_col(gain_ref)), bias_rows)

    n_c, n_x, n_y = counts
    rows = n_chan // (n_c * n_x * n_y)
    for c in range(n_c):
        for x in range(n_x):
            for y in range(n_y):
                chunk = sums[((c * n_x + x) * n_y + y) * rows : ((c * n_x + x) * n_y + y + 1) * rows]
                at = lax.rem(x - meta[3] + n_x, n_x) * n_y + lax.rem(y - meta[4] + n_y, n_y)

                @pl.when(meta[2] == c)
                def _():
                    keep_ref[at] = chunk

                @pl.when(meta[2] != c)
                def _():
                    send_ref[at] = chunk.astype(jnp.bfloat16)


def gain_col(gain_ref):
    n_chan = gain_ref.shape[1]
    return jnp.broadcast_to(gain_ref[...], (LANES, n_chan)).T[:, :1]


def cells_kernel(meta, xi_ref, xo_ref, gpi_ref, gpo_ref, cot_ref, gain_ref, w_ref, _, base_ref, top_ref, side_ref, ext):
    n_rows, n_cols, n_chan = cot_ref.shape
    lat, lon = meta[0], meta[1]
    ext[...] = jnp.zeros_like(ext)
    for part, (x_ref, gp_t) in enumerate(((xo_ref, gpo_ref), (xi_ref, gpi_ref))):
        n_tok = x_ref.shape[0]
        cells = []
        for base in range(0, n_tok, TOKENS):
            rows = slice(base, base + TOKENS)
            x_hat, inv = norm_stats(x_ref[rows].astype(jnp.float32))
            g = dot(w_ref[...], gp_t[:, rows]).T * gain_ref[...]
            cells.append(inv * (g - jnp.mean(g, -1, keepdims=True) - x_hat * jnp.mean(g * x_hat, -1, keepdims=True)))
        blank = jnp.zeros((1, WINDOW, n_chan), jnp.float32)
        head = lax.broadcasted_iota(jnp.int32, (WINDOW, n_chan), 0) < lon
        for r in range(WINDOW):
            row = jnp.stack(
                [
                    cells[w * CELLS // TOKENS][w * CELLS % TOKENS + r * WINDOW :][:WINDOW]
                    for w in range(n_tok // CELLS)
                ],
                0,
            )
            row = jnp.concatenate([blank, pltpu.roll(row, lon, 1), blank], 0)
            for t in range(row.shape[0] - 1):
                ext[lat + part * WINDOW + r, t * WINDOW : (t + 1) * WINDOW, :] = jnp.where(head, row[t], row[t + 1])
    for r in range(n_rows):
        base_ref[r] = (cot_ref[r].astype(jnp.float32) + ext[WINDOW + r, WINDOW:]).astype(jnp.bfloat16)
        side_ref[r] = ext[WINDOW + r, :WINDOW].astype(jnp.bfloat16)
    n_top = top_ref.shape[0]
    for r in range(n_top):
        top_ref[r] = ext[WINDOW - n_top + r].astype(jnp.bfloat16)


def edge_kernel(side_ref, top_ref, _, out_ref):
    n_rows, n_top = side_ref.shape[0], top_ref.shape[0]
    for r in range(n_rows):
        edge = side_ref[r].astype(jnp.float32)
        at = r - n_rows + n_top
        if at >= 0:
            edge = edge + top_ref[at].astype(jnp.float32)[:WINDOW]
        out_ref[r] = edge.astype(jnp.bfloat16)


def prepare_kernel(bias_ref, w_ref, full_ref, wt_ref):
    n_head, n_gap = bias_ref.shape
    span = 2 * WINDOW - 1
    width = 2 * LANES
    lane = lax.broadcasted_iota(jnp.int32, (width, LANES), 0)
    cell = lax.broadcasted_iota(jnp.int32, (width, LANES), 1) % CELLS
    place = cell // WINDOW * span + cell % WINDOW + n_gap // 2
    onehot = (lane == place).astype(jnp.float32).astype(jnp.bfloat16)
    table = jnp.concatenate([bias_ref[...], jnp.zeros((n_head, width - n_gap), jnp.float32)], 1)
    for h in range(n_head):
        line = jnp.broadcast_to(table[h : h + 1], (WINDOW, width))
        rows = [pltpu.roll(line, r * span, 1, stride=1, stride_axis=0) for r in range(WINDOW)]
        rest = jnp.concatenate(rows, 0)
        total = jnp.zeros((CELLS, LANES), jnp.float32)
        for _ in range(3):
            part = rest.astype(jnp.bfloat16)
            total += dot(part, onehot)
            rest = rest - part.astype(jnp.float32)
        full_ref[h] = total
    wt_ref[...] = w_ref[...].T


def pack_kernel(n_top, x_ref, cot_ref, mask, side_ref, top_x, top_c, corner_ref, edges, sems):
    n_rows, n_cols, n_chan = x_ref.shape
    copies = []
    for k, (ref, top) in enumerate(((x_ref, top_x), (cot_ref, top_c))):
        copies.append(pltpu.make_async_copy(ref.at[:, pl.ds(n_cols - 2 * WINDOW, 2 * WINDOW)], edges.at[k], sems.at[2 * k]))
        copies.append(pltpu.make_async_copy(ref.at[pl.ds(n_rows - n_top, n_top)], top, sems.at[2 * k + 1]))
    for copy in copies:
        copy.start()
    for k in range(2):
        copies[2 * k].wait()
        for r in range(n_rows):
            edge = edges[k, r][WINDOW:]
            side_ref[k, r] = edge
            at = r - n_rows + n_top
            if at >= 0:
                corner_ref[k, at] = edge
    line = lax.broadcasted_iota(jnp.int32, (WINDOW, n_chan), 0)
    live = jnp.zeros((WINDOW, n_chan), jnp.float32)
    for r in range(WINDOW):
        live = jnp.where(line == r, mask[n_rows - WINDOW + r].astype(jnp.float32), live)
    corner_ref[0, n_top] = live.astype(jnp.bfloat16)
    corner_ref[1, n_top] = live.astype(jnp.bfloat16)
    copies[1].wait()
    copies[3].wait()


def first_add_kernel(keep_ref, got_ref, own_ref, *send_refs):
    size = own_ref.shape[0]
    for k in range(len(send_refs) + 1):
        cut = slice(k * size, (k + 1) * size)
        total = keep_ref[cut] + got_ref[cut].astype(jnp.float32)
        if k:
            send_refs[k - 1][...] = total.astype(jnp.bfloat16)
        else:
            own_ref[...] = total


def next_add_kernel(n_got, n_more, own_ref, *refs):
    got, (out_ref, *send_refs) = refs[:n_got], refs[n_got + n_more :]
    size = out_ref.shape[0]
    for k in range(len(send_refs) + 1):
        cut = slice(k * size, (k + 1) * size)
        total = own_ref[cut]
        for ref in got:
            total = total + ref[cut].astype(jnp.float32)
        if k:
            send_refs[k - 1][...] = total.astype(jnp.bfloat16)
        else:
            out_ref[...] = total.astype(out_ref.dtype)


def join_kernel(n_got, *refs):
    for k in range(n_got):
        refs[-1][k : k + 1] = refs[k][...]


def tree_add_kernel(*refs):
    parts = [ref[...].astype(jnp.float32) for ref in refs[:-1]]
    while len(parts) > 1:
        parts = [parts[k] + parts[k + 1] for k in range(0, len(parts), 2)]
    refs[-1][...] = parts[0].astype(jnp.bfloat16)


def unpack_kernel(counts, n_proj, factor, meta, *refs):
    n_c, n_x, n_y = counts
    mine, other = refs[:n_x], refs[n_x : 2 * n_x]
    qkv_ref, out_ref, gain_ref, bias_ref, small = refs[2 * n_x :]
    rows = mine[0].shape[1]
    n_chan = out_ref.shape[1]
    for half in range(2):
        c = meta[2] if half == 0 else 1 - meta[2]
        for k, ref in enumerate(other if half else mine):
            x = lax.rem(meta[3] + k, n_x)
            for j in range(n_y):
                y = lax.rem(meta[4] + j, n_y)
                chunk = ref[j].astype(jnp.float32) * factor
                to = pl.ds(pl.multiple_of(((c * n_x + x) * n_y + y) * rows, rows), rows)
                qkv_ref[to] = chunk[:, :n_proj]
                out_ref[to] = chunk[:, n_proj : n_proj + n_chan]
                small[to] = chunk[:, n_proj + n_chan :]
    gain_ref[...] = small[...].T[LANES - 1 :]
    n_head, n_gap = bias_ref.shape
    span = 2 * WINDOW - 1
    wide = jnp.concatenate([small[:n_head], small[n_head : 2 * n_head]], 1)
    lane = lax.broadcasted_iota(jnp.int32, wide.shape, 1)
    bias = jnp.zeros_like(wide)
    for k in range(span):
        moved = pltpu.roll(wide, 2 * LANES - k, 1) if k else wide
        bias = jnp.where((lane >= k * span) & (lane < (k + 1) * span), moved, bias)
    bias_ref[...] = bias[:, :n_gap]


class Places:
    def __init__(self):
        self.n_lat, self.n_lon = lax.axis_size("lat"), lax.axis_size("lon")
        self.c = 2
        self.x = min(4, self.n_lon // self.c)
        self.y_low = self.n_lon // (self.c * self.x)
        self.y_high = 2
        self.y = self.y_low * self.y_high
        self.z = self.n_lat // self.y_high

    def index(self, z, y, x, c):
        high, low = divmod(y, self.y_low)
        return (z * self.y_high + high) * self.n_lon + (low * self.x + x) * self.c + c

    def mine(self):
        lat, lon = lax.axis_index("lat"), lax.axis_index("lon")
        return (
            lon % self.c,
            lon // self.c % self.x,
            lat % self.y_high * self.y_low + lon // (self.c * self.x),
        )

    def move(self, array, to):
        every = itertools.product(range(self.z), range(self.y), range(self.x), range(self.c))
        pairs = [(self.index(*at), self.index(*to(*at))) for at in every]
        return lax.ppermute(array, ("lat", "lon"), pairs)

    def by_c(self, array):
        return self.move(array, lambda z, y, x, c: (z, y, x, 1 - c))

    def by_x(self, array, k):
        return self.move(array, lambda z, y, x, c: (z, y, (x + k) % self.x, c))

    def by_y(self, array, k):
        return self.move(array, lambda z, y, x, c: (z, (y + k) % self.y, x, c))

    def by_z(self, array, bits):
        return self.move(array, lambda z, y, x, c: (z ^ bits, y, x, c))


def small_call(kernel, outs, name, limit, *args):
    return pl.pallas_call(
        kernel,
        out_shape=outs,
        compiler_params=pltpu.CompilerParams(vmem_limit_bytes=limit * MIB),
        name=name,
    )(*args)


def total_over_devices(places, keep, send, beside):
    shape = keep.shape[1:]
    bf = functools.partial(jax.ShapeDtypeStruct, dtype=jnp.bfloat16)
    got = places.by_c(send)
    own = jax.ShapeDtypeStruct((places.y, *shape), jnp.float32)
    own, *sends = small_call(first_add_kernel, (own,) + (bf((places.y, *shape)),) * (places.x - 1), "add_c", 12, keep, got)
    got = [places.by_x(part, k + 1) for k, part in enumerate(sends)]
    nxt = jax.ShapeDtypeStruct((1, *shape), jnp.float32)
    ahead, finish = beside(own)
    own, *sends = pl.pallas_call(
        functools.partial(next_add_kernel, len(got), 1),
        out_shape=(nxt,) + (bf((1, *shape)),) * (places.y - 1),
        in_specs=[whole()] * (1 + len(got)) + [pl.BlockSpec(memory_space=pl.ANY)],
        compiler_params=pltpu.CompilerParams(vmem_limit_bytes=6 * MIB),
        name="add_x",
    )(own, *got, ahead)
    got = [places.by_y(part, k + 1) for k, part in enumerate(sends)]
    (mine,) = small_call(functools.partial(next_add_kernel, len(got), 0), (bf((1, *shape)),), "add_y", 4, own, *got)
    for group in {1: (), 2: ((1,),), 4: ((1, 2, 3),), 8: ((1, 2, 3), (6,))}[places.z]:
        others = [places.by_z(mine, bits) for bits in group]
        mine = small_call(tree_add_kernel, bf((1, *shape)), "add_z", 2, mine, *others)
    parts = [mine] + [places.by_y(mine, -k) for k in range(1, places.y)]
    mine = small_call(functools.partial(join_kernel, len(parts)), bf((places.y, *shape)), "join", 4, *parts)
    result = finish(mine)
    mine = [mine] + [places.by_x(mine, -k) for k in range(1, places.x)]
    return mine, [places.by_c(part) for part in mine], result


def ring(array, lat, lon):
    n_lat, n_lon = lax.axis_size("lat"), lax.axis_size("lon")
    pairs = [
        (i * n_lon + j, (i + lat) % n_lat * n_lon + (j + lon) % n_lon) for i in range(n_lat) for j in range(n_lon)
    ]
    return lax.ppermute(array, ("lat", "lon"), pairs)


def local(saved_state, cotangent, row_mask, shifts, norm_gain, w_qkv, w_out, bias_table):
    n_rows, n_cols, n_chan = saved_state.shape
    n_head = bias_table.shape[0]
    n_proj = w_qkv.shape[1]
    n_tok = n_rows // 2 * n_cols
    n_top = WINDOW - 1
    places = Places()
    counts = (places.c, places.x, places.y)
    bf, f32 = jnp.bfloat16, jnp.float32

    smem = pl.BlockSpec(memory_space=pltpu.SMEM)
    tile = functools.partial(jax.ShapeDtypeStruct, dtype=bf)
    side, top_x, top_c, corner = pl.pallas_call(
        functools.partial(pack_kernel, n_top),
        out_shape=(
            tile((2, n_rows, WINDOW, n_chan)),
            tile((n_top, n_cols, n_chan)),
            tile((n_top, n_cols, n_chan)),
            tile((2, WINDOW, WINDOW, n_chan)),
        ),
        in_specs=[pl.BlockSpec(memory_space=pltpu.HBM), pl.BlockSpec(memory_space=pltpu.HBM), smem],
        scratch_shapes=[pltpu.VMEM((2, n_rows, 2 * WINDOW, n_chan), bf), pltpu.SemaphoreType.DMA((4,))],
        compiler_params=pltpu.CompilerParams(vmem_limit_bytes=58 * MIB),
        name="pack",
    )(saved_state, cotangent, row_mask)
    side = ring(side, 0, 1)
    top_x = ring(top_x, 1, 0)
    top_c = ring(top_c, 1, 0)
    corner = ring(corner, 1, 1)
    at = jnp.stack(places.mine()).astype(jnp.int32)
    gain = norm_gain.reshape(1, n_chan)
    bias, w_t = pl.pallas_call(
        prepare_kernel,
        out_shape=(jax.ShapeDtypeStruct((n_head, CELLS, LANES), f32), tile((n_proj, n_chan))),
        compiler_params=pltpu.CompilerParams(vmem_limit_bytes=16 * MIB),
        cost_estimate=pl.CostEstimate(flops=10**9, bytes_accessed=4 * MIB, transcendentals=0),
        name="prepare",
    )(bias_table, w_qkv)

    below = jnp.minimum(lax.axis_index("lat"), 1).astype(jnp.int32).reshape(1)
    meta = jnp.concatenate([shifts, at, below, row_mask])
    cells_f, cells_t = pltpu.VMEM((n_tok, n_chan), f32), pltpu.VMEM((n_chan, n_tok), bf)
    x_in, gp_in, sums_in, bsum_in = pl.pallas_call(
        functools.partial(inner_kernel, n_head),
        out_shape=(
            tile((n_tok, n_chan)),
            tile((n_proj, n_tok)),
            jax.ShapeDtypeStruct((n_chan, n_proj + n_chan), f32),
            jax.ShapeDtypeStruct((n_head, CELLS, LANES), f32),
        ),
        in_specs=[smem] + [whole()] * 8,
        scratch_shapes=[
            pltpu.VMEM((n_tok, n_chan), bf),
            cells_t,
            cells_t,
            cells_f,
            cells_f,
            pltpu.VMEM((n_proj, n_tok), bf),
            pltpu.VMEM((n_tok, 2 * n_chan), bf),
            cells_t,
        ],
        compiler_params=pltpu.CompilerParams(vmem_limit_bytes=24 * MIB),
        cost_estimate=pl.CostEstimate(flops=8 * 10**9, bytes_accessed=16 * MIB, transcendentals=2**19),
        name="inner",
    )(meta, saved_state, cotangent, side, bias, gain, w_t, w_qkv, w_out)
    x_out, nrm_out, proj_out, kv_out = pl.pallas_call(
        functools.partial(front_kernel, n_head),
        out_shape=(tile((n_tok, n_chan)), tile((n_chan, n_tok)), tile((n_proj, n_tok)), tile((n_tok, 2 * n_chan))),
        in_specs=[smem] + [whole()] * 7 + [pl.BlockSpec(memory_space=pl.ANY)],
        scratch_shapes=[cells_f],
        compiler_params=pltpu.CompilerParams(vmem_limit_bytes=14 * MIB),
        cost_estimate=pl.CostEstimate(flops=3 * 10**9, bytes_accessed=8 * MIB, transcendentals=0),
        name="front",
    )(meta, saved_state, side, top_x, corner, gain, w_t, w_qkv, bsum_in)

    width = n_proj + n_chan + LANES
    rows = n_chan // math.prod(counts)
    half = math.prod(counts) // 2
    gp_out, keep, send = pl.pallas_call(
        functools.partial(outer_kernel, n_head, counts),
        out_shape=(
            tile((n_proj, n_tok)),
            jax.ShapeDtypeStruct((half, rows, width), f32),
            tile((half, rows, width)),
        ),
        in_specs=[smem] + [whole()] * 13,
        scratch_shapes=[
            pltpu.VMEM((n_tok, n_chan), bf),
            cells_t,
            pltpu.VMEM((n_head, CELLS, LANES), f32),
            cells_f,
            cells_t,
            pltpu.VMEM((n_chan, width), f32),
            pltpu.VMEM((n_head * CELLS, LANES), f32),
            pltpu.VMEM((n_head * CELLS, LANES), f32),
        ],
        compiler_params=pltpu.CompilerParams(vmem_limit_bytes=30 * MIB),
        cost_estimate=pl.CostEstimate(flops=10**10, bytes_accessed=24 * MIB, transcendentals=2**19),
        name="outer",
    )(meta, cotangent, side, top_c, corner, bias, gain, w_qkv, w_out, nrm_out, proj_out, kv_out, sums_in, bsum_in)

    def input_grad(start):
        base, *edges = pl.pallas_call(
            cells_kernel,
            out_shape=(
                tile((n_rows, n_cols, n_chan)),
                tile((n_top, n_cols + WINDOW, n_chan)),
                tile((n_rows, WINDOW, n_chan)),
            ),
            in_specs=[smem] + [whole()] * 7 + [pl.BlockSpec(memory_space=pl.ANY)],
            scratch_shapes=[pltpu.VMEM((n_rows + WINDOW, n_cols + WINDOW, n_chan), f32)],
            compiler_params=pltpu.CompilerParams(vmem_limit_bytes=24 * MIB),
            cost_estimate=pl.CostEstimate(flops=16 * 10**8, bytes_accessed=12 * MIB, transcendentals=0),
            name="cells",
        )(meta, x_in, x_out, gp_in, gp_out, cotangent, gain, w_qkv, start)
        top_back = ring(edges[0], -1, 0)

        def finish(later):
            side = pl.pallas_call(
                edge_kernel,
                out_shape=tile((n_rows, WINDOW, n_chan)),
                in_specs=[whole()] * 2 + [pl.BlockSpec(memory_space=pl.ANY)],
                compiler_params=pltpu.CompilerParams(vmem_limit_bytes=4 * MIB),
                name="edge",
            )(edges[1], top_back, later)
            return base, top_back, ring(side, 0, -1)

        return edges[1], finish

    mine, other, (base, top_back, side_back) = total_over_devices(places, keep, send, input_grad)
    edge = jnp.pad(top_back[:, WINDOW:], ((n_rows - n_top, 0), (0, 0), (0, 0)))
    edge = edge + jnp.pad(side_back, ((0, 0), (n_cols - WINDOW, 0), (0, 0)))
    state_grad = (base.astype(f32) + edge.astype(f32)).astype(bf)

    factor = 1.0 / math.sqrt(n_rows * places.n_lat * n_cols * places.n_lon)
    qkv_grad, out_grad, gain_grad, bias_grad = pl.pallas_call(
        functools.partial(unpack_kernel, counts, n_proj, factor),
        out_shape=(
            jax.ShapeDtypeStruct((n_chan, n_proj), f32),
            jax.ShapeDtypeStruct((n_chan, n_chan), f32),
            jax.ShapeDtypeStruct((1, n_chan), f32),
            jax.ShapeDtypeStruct(bias_table.shape, f32),
        ),
        in_specs=[smem] + [whole()] * (2 * places.x),
        scratch_shapes=[pltpu.VMEM((n_chan, LANES), f32)],
        compiler_params=pltpu.CompilerParams(vmem_limit_bytes=16 * MIB),
        name="unpack",
    )(meta, *mine, *other)
    return state_grad, qkv_grad, out_grad, gain_grad.reshape(n_chan), bias_grad


def solution(mesh):
    return jax.shard_map(
        local,
        mesh=mesh,
        in_specs=(P("lat", "lon", None), P("lat", "lon", None), P("lat"), P(), P(), P(), P(), P()),
        out_specs=(P("lat", "lon", None), P(), P(), P(), P()),
        check_vma=False,
    )
```
